256 devices in a mesh: cluster: 128 (over z, x_hi, y, core), narrow: 2 (over x_lo).
Axes of the slice: x: 4 (x_hi: 2, x_lo: 2; x = x_hi * 2 + x_lo), y: 4, z: 8, core: 2. Of those that a mesh axis runs over, the one named last changes fastest.
Arguments:
- panels: float32 [98, 131072], P(None, ('cluster', 'narrow')), may hold values from -103.4 to 103.4, as said below
- test_points: float32 [14, 131072], P(None, ('cluster', 'narrow')), may hold values from -103.4 to 103.4, as said below
- currents: float32 [512, 131072], P(None, ('cluster', 'narrow')), may hold values from -6 to 6
- near_mask: int32 [1024, 7], P(('cluster', 'narrow')), may hold values from 0 to 1, as said below
Outputs:
- product: float32 [512, 131072], P(None, ('cluster', 'narrow'))
The draws below stay inside these ranges and needn't reach their ends.
Inputs may be any that keep to these rules, and one draw needn't show every extreme that they name: Rows of panels are 7 channels of 14 points (channel * 14 + point): position x, y, z, weighted basis vector x, y, z, weighted divergence. Positions of block b lie near angle 2 pi b / 1024 on a circle. Rows of test_points are 7 channels of the two centroids (channel * 2 + centroid), channels as in panels. `near_mask`: column c marks source offset c - 3. Column 3 is 1 in every row. Every block of some clusters of the first half of the cluster axis has all columns 1; in the other blocks only the columns of offsets -1 and 1 may be 1 besides it.
All inputs are finite; a program needn't handle non-finite values.
Results may differ from the reference program's by a relative error of at most 0.0003.
Values sent between devices are 32-bit elements; how exact they have to be, the bound alone decides.
A program may use at most 128 MiB of HBM per device.

```python
import math
import jax
import jax.numpy as jnp
from jax import lax

BLK = 128
QP = 14
REACH = 3
NRHS = 128
TPB = 4
NBLK = 1024
NBF = 131072
N_CLUSTER = 128
N_NARROW = 2


def centre_points(key):
    block_ids = (jnp.arange(NBF, dtype=jnp.int32) // BLK).astype(jnp.float32)
    angle = block_ids * (2.0 * math.pi / NBLK)
    radius = NBLK * 0.6 / (2.0 * math.pi)
    jitter = jax.random.uniform(key, (3, NBF), jnp.float32, -0.5, 0.5)
    circle = jnp.stack([radius * jnp.cos(angle), radius * jnp.sin(angle), jnp.zeros_like(angle)])
    return circle + jitter


def draw_panels(key, part):
    centres = centre_points(key)
    key = jax.random.fold_in(key, 5)
    subkeys = jax.random.split(key, 3)
    places = centres[:, None, :] + jax.random.uniform(subkeys[0], (3, QP, NBF), jnp.float32, -0.1, 0.1)
    vectors = 0.02 * jnp.clip(jax.random.normal(subkeys[1], (3, QP, NBF), jnp.float32), -4.0, 4.0)
    charges = 0.06 * jnp.clip(jax.random.normal(subkeys[2], (1, QP, NBF), jnp.float32), -4.0, 4.0)
    return jnp.concatenate([places, vectors, charges], 0).reshape(7 * QP, NBF)


def draw_test_points(key, part):
    centres = centre_points(key)
    key = jax.random.fold_in(key, 7)
    subkeys = jax.random.split(key, 3)
    places = centres[:, None, :] + jax.random.uniform(subkeys[0], (3, 2, NBF), jnp.float32, -0.05, 0.05)
    vectors = 0.02 * jnp.clip(jax.random.normal(subkeys[1], (3, 2, NBF), jnp.float32), -4.0, 4.0)
    charges = 0.06 * jnp.clip(jax.random.normal(subkeys[2], (1, 2, NBF), jnp.float32), -4.0, 4.0)
    return jnp.concatenate([places, vectors, charges], 0).reshape(14, NBF)


def draw_near_mask(key, part):
    key = jax.random.fold_in(key, 11)
    first, second = jax.random.split(key)
    phase = jax.random.randint(first, (), 0, 8)
    block_ids = jnp.arange(NBLK, dtype=jnp.int32)
    cluster_ids = block_ids // (TPB * N_NARROW)
    crowded = (cluster_ids < N_CLUSTER // 2) & (cluster_ids % 8 == phase)
    coins = jax.random.randint(second, (NBLK, 2 * REACH + 1), 0, 2)
    offsets = jnp.arange(2 * REACH + 1, dtype=jnp.int32)[None, :]
    nearby = jnp.where(jnp.abs(offsets - REACH) == 1, coins, 0)
    nearby = jnp.where(offsets == REACH, 1, nearby)
    return jnp.where(crowded[:, None], 1, nearby).astype(jnp.int32)


def steps_of(rng, dims, pieces, low, high):
    def one(position, blocks):
        steps = jax.random.uniform(jax.random.fold_in(jax.random.fold_in(rng, 6), position), (blocks,), jnp.float32, low / len(pieces), high / len(pieces))
        return jnp.repeat(jnp.exp(steps), dims[position] // blocks).reshape((-1,) + (1,) * (len(dims) - position - 1))

    factor_of = one(*pieces[0])
    for cut in pieces[1:]:
        factor_of = factor_of * one(*cut)
    return factor_of


def centred(key, extent, deviation, bound, shards=(), kind=jnp.bfloat16):
    drawn = jax.random.normal(key, extent, jnp.float32) * deviation
    if len(shards) > 0:
        drawn = steps_of(key, extent, shards, -0.22, 0.18) * drawn
    return jnp.clip(drawn, min=-bound, max=bound).astype(kind)


def setup_inputs(seed: int = 0) -> dict:
    seeds = jax.random.split(jax.random.key(seed), 5)
    panels = draw_panels(jax.random.fold_in(seeds[4], 71), 0)
    test_points = draw_test_points(jax.random.fold_in(seeds[4], 71), 0)
    currents = centred(seeds[2], (4 * NRHS, NBF), 1.0, 6.0, ((1, 256),), jnp.float32)
    near_mask = draw_near_mask(jax.random.fold_in(seeds[4], 71), 0)
    return dict(panels=panels, test_points=test_points, currents=currents, near_mask=near_mask)


WAVES = ((2.0, 0.0), (1.0, 3.0))
CONTRAST = 0.5
SOFTEN = 0.04

def tile_ops(tester_geom, source_geom):
    npoints = source_geom.shape[0] // 7
    ncentres = tester_geom.shape[0] // 7
    source = source_geom.reshape(7, npoints, source_geom.shape[1])
    tester = tester_geom.reshape(7, ncentres, tester_geom.shape[1])
    summed = jnp.zeros((6, tester.shape[2], source.shape[2]), jnp.float32)
    for centre in range(ncentres):
        deltas = [tester[component, centre][None, :, None] - source[component][:, None, :] for component in range(3)]
        distance = jnp.sqrt(deltas[0] * deltas[0] + deltas[1] * deltas[1] + deltas[2] * deltas[2] + SOFTEN)
        tvector = [tester[3 + component, centre][None, :, None] for component in range(3)]
        svector = [source[3 + component][:, None, :] for component in range(3)]
        dotted = tvector[0] * svector[0] + tvector[1] * svector[1] + tvector[2] * svector[2]
        charge = tester[6, centre][None, :, None] * source[6][:, None, :]
        crossed = deltas[0] * (svector[1] * tvector[2] - svector[2] * tvector[1]) + deltas[1] * (svector[2] * tvector[0] - svector[0] * tvector[2]) + deltas[2] * (svector[0] * tvector[1] - svector[1] * tvector[0])
        media = []
        for wave_real, wave_imag in WAVES:
            decay = jnp.exp(-wave_imag * distance) / distance
            green_real = decay * jnp.cos(wave_real * distance)
            green_imag = decay * jnp.sin(wave_real * distance)
            coef_real = (wave_real * wave_real - wave_imag * wave_imag) * dotted - charge
            coef_imag = 2.0 * wave_real * wave_imag * dotted
            ell_real = coef_real * green_real - coef_imag * green_imag
            ell_imag = coef_real * green_imag + coef_imag * green_real
            factor_real = -wave_imag * distance - 1.0
            factor_imag = wave_real * distance
            scaled = crossed / (distance * distance)
            kay_real = scaled * (factor_real * green_real - factor_imag * green_imag)
            kay_imag = scaled * (factor_real * green_imag + factor_imag * green_real)
            media.append((lax.optimization_barrier(jnp.sum(ell_real, 0)), lax.optimization_barrier(jnp.sum(ell_imag, 0)), lax.optimization_barrier(jnp.sum(kay_real, 0)), lax.optimization_barrier(jnp.sum(kay_imag, 0))))
        first, second = media
        stacked = jnp.stack([first[0] + second[0], first[1] + second[1], first[2] + second[2], first[3] + second[3], first[0] + CONTRAST * second[0], first[1] + CONTRAST * second[1]])
        summed = summed + stacked
    return summed

def apply_tile(operators, flowing):
    rows = flowing.shape[0] // 4
    product = jnp.einsum('mij,cj->mci', operators, flowing, precision=lax.Precision.HIGHEST)

    def select(which, group):
        return product[which, group * rows:(group + 1) * rows]
    out_jreal = select(0, 0) - select(1, 1) - select(2, 2) + select(3, 3)
    out_jimag = select(1, 0) + select(0, 1) - select(3, 2) - select(2, 3)
    out_mreal = select(2, 0) - select(3, 1) + select(4, 2) - select(5, 3)
    out_mimag = select(3, 0) + select(2, 1) + select(5, 2) + select(4, 3)
    return jnp.concatenate([out_jreal, out_jimag, out_mreal, out_mimag], 0)

def reference(panels, test_points, currents, near_mask):
    columns = currents.shape[1]
    nblocks = columns // BLK
    span = 2 * REACH + 1

    def one_block(block_id):
        tester = lax.dynamic_slice_in_dim(test_points, block_id * BLK, BLK, 1)

        def add_tile(offset, running):
            anchor = ((block_id + offset - REACH + nblocks) % nblocks).astype(jnp.int32)

            def compute(carried):
                geometry = lax.dynamic_slice_in_dim(panels, anchor * BLK, BLK, 1)
                flowing = lax.dynamic_slice_in_dim(currents, anchor * BLK, BLK, 1)
                return carried + apply_tile(tile_ops(tester, geometry), flowing)

            def bypass(carried):
                return carried
            return lax.cond(near_mask[block_id, offset] > 0, compute, bypass, running)
        initial = jnp.zeros((currents.shape[0], BLK), jnp.float32)
        return lax.fori_loop(0, span, add_tile, initial)
    blocks = lax.map(one_block, jnp.arange(nblocks, dtype=jnp.int32))
    return jnp.transpose(blocks, (1, 0, 2)).reshape(currents.shape[0], columns)
```

```python
import functools
import itertools
import math

import jax
import jax.numpy as jnp
from jax import lax
from jax.experimental import pallas as pl
from jax.experimental.pallas import tpu as pltpu
from jax.sharding import PartitionSpec as P

F32 = jnp.float32
BF16 = jnp.bfloat16
BLK = 128
QP = 14
REACH = 3
SPAN = 7
TPB = 4
GROWS = 98
NRHS = 128
SOFTEN = 0.04

Z_MAX = 14.0
DEGREE = 4
COS_HALF = (2.828426289053651, -0.35355064760758376, 0.007364148070439611, -6.107114702262049e-05, 2.4846120790492805e-07)
SIN_HALF = (1.4142135239177973, -0.05892543897495882, 0.0007364984722676873, -4.370137027858996e-06, 1.4053654408325383e-08)

TERMS = []
for _total in range(DEGREE + 1):
    for _j in range(_total + 1):
        _l = _total - _j
        for _a in itertools.product(range(_l + 1), repeat=3):
            if sum(_a) == _l:
                TERMS.append((_j, _a))
NTERM = 72
assert len(TERMS) <= NTERM
ONE = TERMS.index((0, (0, 0, 0)))
LIN = [TERMS.index((0, tuple(int(c == k) for c in range(3)))) for k in range(3)]
SQR = TERMS.index((1, (0, 0, 0)))
KDIM = 256
NOUT = 7
JC = 16
NCH = BLK // JC
MROWS = JC * QP


def powers_of(vec):
    one = None
    table = {(0, 0, 0): one}
    for total in range(1, DEGREE + 1):
        for a in itertools.product(range(total + 1), repeat=3):
            if sum(a) != total:
                continue
            axis = next(c for c in range(3) if a[c] > 0)
            prev = tuple(a[c] - (c == axis) for c in range(3))
            table[a] = vec[axis] if table[prev] is None else table[prev] * vec[axis]
    return table


def split2(value):
    high = value.astype(BF16).astype(F32)
    return high, value - high


def source_features(stage, fts, sf, centre, y):
    mono = powers_of(y)
    square = y[0] * y[0] + y[1] * y[1] + y[2] * y[2]
    sq = [None, square, square * square]
    sq.append(sq[2] * square)
    sq.append(sq[2] * sq[2])
    ones = jnp.ones_like(square)

    def put(row, value):
        fts[row * 16 : row * 16 + QP, :] = value

    for k, (j, a) in enumerate(TERMS):
        const = (-2.0) ** sum(a) / (math.prod(math.factorial(v) for v in a) * math.factorial(j))
        value = mono[a]
        if sq[j] is not None:
            value = sq[j] if value is None else value * sq[j]
        if value is None:
            value = ones
        put(k, value * const if const != 1.0 else value)
    base = NTERM
    s = [stage[(3 + c) * QP : (4 + c) * QP, :] for c in range(3)]
    d = stage[6 * QP : 7 * QP, :]
    for c in range(3):
        put(base + c, s[c])
    put(base + 3, d)
    for c in range(3):
        c1, c2 = (c + 1) % 3, (c + 2) % 3
        put(base + 4 + c, y[c1] * s[c2] - y[c2] * s[c1])
    extra = base + 8
    for half in range(2):
        for c in range(3):
            put(extra + 4 * half + c, y[c] * -2.0)
        put(extra + 4 * half + 3, square)
    rows = lax.broadcasted_iota(jnp.int32, (8, BLK), 0)
    for q in range(QP):
        main = fts[pl.ds(q, NTERM, stride=16), :]
        bil = fts[pl.ds(base * 16 + q, 8, stride=16), :]
        ext = fts[pl.ds(extra * 16 + q, 8, stride=16), :]
        mh, ml = split2(main)
        bh, bl = split2(bil)
        eh, rest = split2(ext)
        em, el = split2(rest)
        zrow = jnp.where(rows < 4, em, eh)
        zrow2 = jnp.where(rows < 4, el, jnp.where(rows == 4, 1.0, 0.0))
        full = jnp.concatenate([mh, mh, ml, bh, bh, bl, zrow, zrow2], 0)
        turned = full.T.astype(BF16)
        for ch in range(NCH):
            sf[ch * MROWS + q * JC : ch * MROWS + (q + 1) * JC, :] = turned[ch * JC : (ch + 1) * JC, :]


def horner(coefs, m, w):
    der = [coefs[k] * math.factorial(k) / math.factorial(k - m) for k in range(m, len(coefs))]
    value = None
    for c in reversed(der):
        value = c if value is None else value * w + c
    return value


OFF_C, OFF_S, OFF_Z = 0, NTERM, 2 * NTERM
OFF_B = 3 * NTERM
OFF_E = OFF_B + 32
TROWS = OFF_E + 16


def test_features(xt, ftt, centre):
    x = [xt[c] - centre[c] for c in range(3)]
    t = [xt[3 + c] for c in range(3)]
    e = xt[6]
    w = x[0] * x[0] + x[1] * x[1] + x[2] * x[2] + SOFTEN
    mono = powers_of(x)

    def put(row, value):
        ftt[row * 8 : row * 8 + 8, :] = value

    for off, coefs in ((OFF_C, COS_HALF), (OFF_S, SIN_HALF)):
        der = [horner(coefs, m, w) for m in range(DEGREE + 1)]
        for k, (j, a) in enumerate(TERMS):
            level = der[j + sum(a)]
            value = level if mono[a] is None else mono[a] * level
            put(off + k, jnp.broadcast_to(value, w.shape))
    put(OFF_Z + ONE, w)
    put(OFF_Z + SQR, jnp.ones_like(w))
    for c in range(3):
        put(OFF_Z + LIN[c], x[c])
    charge = e * -0.25
    for c in range(3):
        put(OFF_B + c, t[c])
        put(OFF_B + 8 + c, t[c] * -2.0)
        put(OFF_B + 16 + c, t[c] * 1.5)
        c1, c2 = (c + 1) % 3, (c + 2) % 3
        put(OFF_B + 24 + c, (t[c1] * x[c2] - t[c2] * x[c1]) * -0.25)
        put(OFF_B + 28 + c, t[c] * 0.25)
    put(OFF_B + 3, charge)
    put(OFF_B + 11, charge)
    for half in range(2):
        for c in range(3):
            put(OFF_E + 4 * half + c, x[c])
        put(OFF_E + 4 * half + 3, jnp.ones_like(w))
    for c in range(4):
        put(OFF_E + 8 + c, x[c] if c < 3 else jnp.ones_like(w))
    put(OFF_E + 12, w)


def test_matrix(ftt, tf, b):
    rows = lax.broadcasted_iota(jnp.int32, (8, BLK), 0)
    zero8 = jnp.zeros((8, BLK), F32)
    for a in range(2):
        ba = 2 * b + a

        def take(off, n):
            return ftt[pl.ds(off * 8 + ba, n, stride=8), :]

        for out, off in ((0, OFF_Z), (1, OFF_C), (2, OFF_S)):
            high, low = split2(take(off, NTERM))
            lanes = slice(out * 256 + a * BLK, out * 256 + (a + 1) * BLK)
            tf[0:224, lanes] = jnp.concatenate([high, low, high, zero8], 0).astype(BF16)
        eh, rest = split2(take(OFF_E, 8))
        em, el = split2(rest)
        fh, rest2 = split2(take(OFF_E + 8, 8))
        fm, fl = split2(rest2)
        first = jnp.where(rows < 4, em, el)
        second = jnp.where(rows < 4, fh, jnp.where(rows == 4, fl, 0.0))
        tf[240:256, a * BLK : (a + 1) * BLK] = jnp.concatenate([first, second], 0).astype(BF16)
        for m in range(4):
            high, low = split2(take(OFF_B + 8 * m, 8))
            out = 3 + m
            lanes = slice(out * 256 + a * BLK, out * 256 + (a + 1) * BLK)
            tf[208:240, lanes] = jnp.concatenate([zero8, high, low, high], 0).astype(BF16)


EXP_RATE = -3.0 / math.log(2.0)


def pair_terms(z, cos_h, sin_h, k1, k2, k6, kk):
    inv = lax.rsqrt(z)
    dist = z * inv
    s0 = sin_h * dist
    c = 4.0 - s0 * s0
    s = s0 * cos_h
    c2 = c * c - 8.0
    s2 = c * s
    decay = jnp.exp2(dist * EXP_RATE)
    p = decay * c
    q = decay * s
    half = inv * 0.5
    c2r = c2 * half
    s2r = s2 * half
    pr = p * inv
    qr = q * inv
    weight = kk * (inv * inv)
    l1r = k1 * c2r
    l1i = k1 * s2r
    l2r = k2 * pr - k6 * qr
    l2i = k2 * qr + k6 * pr
    kr = weight * (((c2r + pr) + (s2 + 3.0 * p)) + q)
    ki = weight * (((s2r + qr) + (3.0 * q - c2)) - p)
    return l1r, l1i, l2r, l2i, kr, ki


def chunk_sums(buf, ops, chunk):
    for g in range(JC // 8):
        acc = None
        for q in range(QP):
            for a in range(2):
                row = q * JC + g * 8
                vals = [buf[row : row + 8, o * 256 + a * BLK : o * 256 + (a + 1) * BLK] for o in range(NOUT)]
                terms = pair_terms(*vals)
                acc = list(terms) if acc is None else [u + v for u, v in zip(acc, terms)]
        start = pl.multiple_of(chunk * JC + g * 8, 8)
        for m in range(6):
            ops[m, pl.ds(start, 8), :] = acc[m]


def fast_tile(ftt, tf, sf, bufs, ops, b):
    test_matrix(ftt, tf, b)

    def product(chunk, buf):
        rows = pl.ds(pl.multiple_of(chunk * MROWS, 16), MROWS)
        buf[...] = jnp.dot(sf[rows, :], tf[...], preferred_element_type=F32)

    product(0, bufs[0])

    def step(n, carry):
        product(2 * n + 1, bufs[1])
        chunk_sums(bufs[0], ops, 2 * n)
        product((2 * n + 2) % NCH, bufs[0])
        chunk_sums(bufs[1], ops, 2 * n + 1)
        return carry

    lax.fori_loop(0, NCH // 2, step, 0)


def direct_tile(stage, raw, xt, ops, b):
    for c in range(7):
        raw[c * 16 : c * 16 + QP, :] = stage[c * QP : (c + 1) * QP, :]
    raw[7 * 16 : 8 * 16, :] = jnp.zeros((16, BLK), F32)
    for m in range(6):
        ops[m] = jnp.zeros((BLK, BLK), F32)

    def point(q, carry):
        rows8 = raw[pl.ds(q, 8, stride=16), :]
        turned = jnp.concatenate([rows8, jnp.zeros((BLK - 8, BLK), F32)], 0).T
        src = [turned[:, c : c + 1] for c in range(7)]

        def centroid(a, carry2):
            tst = [xt[c, pl.ds(2 * b + a, 1), :] for c in range(7)]
            dl = [tst[c] - src[c] for c in range(3)]
            dist = jnp.sqrt(dl[0] * dl[0] + dl[1] * dl[1] + dl[2] * dl[2] + SOFTEN)
            dotted = tst[3] * src[3] + tst[4] * src[4] + tst[5] * src[5]
            charge = tst[6] * src[6]
            crossed = (
                dl[0] * (src[4] * tst[5] - src[5] * tst[4])
                + dl[1] * (src[5] * tst[3] - src[3] * tst[5])
                + dl[2] * (src[3] * tst[4] - src[4] * tst[3])
            )
            scaled = crossed / (dist * dist)
            kr = ki = None
            for m, (wr, wi) in enumerate(((2.0, 0.0), (1.0, 3.0))):
                decay = jnp.exp(-wi * dist) / dist
                gr = decay * jnp.cos(wr * dist)
                gi = decay * jnp.sin(wr * dist)
                cr = (wr * wr - wi * wi) * dotted - charge
                ci = 2.0 * wr * wi * dotted
                ops[2 * m] += cr * gr - ci * gi
                ops[2 * m + 1] += cr * gi + ci * gr
                fr = -wi * dist - 1.0
                fi = wr * dist
                ops[4] += scaled * (fr * gr - fi * gi)
                ops[5] += scaled * (fr * gi + fi * gr)
            return carry2

        return lax.fori_loop(0, 2, centroid, carry)

    lax.fori_loop(0, QP, point, 0)


def apply_operators(ops, xs, wh, wl, acc, b):
    def put(ref, value, places):
        neg = -value
        for row, col, sign in places:
            ref[row * BLK : (row + 1) * BLK, col * BLK : (col + 1) * BLK] = value if sign > 0 else neg

    def both(value, places):
        high = value.astype(BF16)
        low = (value - high.astype(F32)).astype(BF16)
        put(wh, high, places)
        put(wl, low, places)

    l1r, l1i, l2r, l2i = (ops[m] for m in range(4))
    both(l1r + l2r, ((0, 0, 1), (1, 1, 1)))
    both(l1i + l2i, ((0, 1, 1), (1, 0, -1)))
    both(l1r + 0.5 * l2r, ((2, 2, 1), (3, 3, 1)))
    both(l1i + 0.5 * l2i, ((2, 3, 1), (3, 2, -1)))
    both(ops[4], ((0, 2, 1), (1, 3, 1), (2, 0, -1), (3, 1, -1)))
    both(ops[5], ((0, 3, 1), (1, 2, -1), (2, 1, -1), (3, 0, 1)))
    first = jnp.dot(xs[...], wh[...], preferred_element_type=F32)
    second = jnp.dot(xs[0:BLK, :], wl[...], preferred_element_type=F32)
    acc[b] += first[0:BLK] + first[BLK:] + second


def near_kernel(groups, with_base, *refs):
    mask, test = refs[0], refs[1]
    pos = 2
    sources = []
    for _ in groups:
        sources.append((refs[pos], refs[pos + 1]))
        pos += 2
    base = None
    if with_base:
        base = refs[pos]
        pos += 1
    out = refs[pos]
    stage, xt, fts, ftt, tf, sf, buf0, buf1, ops, xs, wh, wl, acc, raw, flags = refs[pos + 1 :]

    tf[...] = jnp.zeros_like(tf)
    ftt[...] = jnp.zeros_like(ftt)
    fts[...] = jnp.zeros_like(fts)
    for c in range(7):
        for b in range(TPB):
            xt[c, 2 * b : 2 * b + 2, :] = test[2 * c : 2 * c + 2, b * BLK : (b + 1) * BLK]
    for b in range(TPB):
        for g in range(4):
            if base is None:
                acc[b, :, g * BLK : (g + 1) * BLK] = jnp.zeros((BLK, BLK), F32)
            else:
                acc[b, :, g * BLK : (g + 1) * BLK] = base[g * NRHS : (g + 1) * NRHS, b * BLK : (b + 1) * BLK]

    total = sum(count for count, _ in groups)

    def source(n, carry):
        rel = jnp.int32(0)
        seen = 0
        for count, begin in groups:
            rel = jnp.where(n >= seen, n - seen + begin, rel)
            seen += count

        def wanted(b):
            column = rel - b + REACH
            inside = (column >= 0) & (column < SPAN)
            return inside & (mask[b, jnp.clip(column, 0, SPAN - 1)] > 0)

        any_wanted = wanted(0)
        for b in range(1, TPB):
            any_wanted = any_wanted | wanted(b)

        @pl.when(any_wanted)
        def _():
            seen = 0
            for (count, begin), (pan, cur) in zip(groups, sources):

                def load(seen=seen, pan=pan, cur=cur):
                    lanes = pl.ds(pl.multiple_of((n - seen) * BLK, BLK), BLK)
                    stage[...] = pan[:, lanes]
                    for g in range(4):
                        value = cur[g * NRHS : (g + 1) * NRHS, lanes]
                        high = value.astype(BF16)
                        xs[0:BLK, g * BLK : (g + 1) * BLK] = high
                        xs[BLK : 2 * BLK, g * BLK : (g + 1) * BLK] = (value - high.astype(F32)).astype(BF16)

                if len(groups) == 1:
                    load()
                else:
                    pl.when((n >= seen) & (n < seen + count))(load)
                seen += count

            place = [stage[c * QP : (c + 1) * QP, :] for c in range(3)]
            low = [jnp.min(jnp.min(v, 0, keepdims=True), 1, keepdims=True) for v in place]
            high = [jnp.max(jnp.max(v, 0, keepdims=True), 1, keepdims=True) for v in place]
            centre = [(u + v) * 0.5 for u, v in zip(low, high)]
            bound = jnp.full((8, BLK), SOFTEN, F32)
            for c in range(3):
                far = jnp.maximum(jnp.abs(xt[c] - low[c]), jnp.abs(xt[c] - high[c]))
                bound = bound + far * far
            for b in range(TPB):
                flags[b] = (jnp.max(bound[2 * b : 2 * b + 2]) <= Z_MAX).astype(jnp.int32)
            source_features(stage, fts, sf, centre, [place[c] - centre[c] for c in range(3)])
            test_features(xt, ftt, centre)

            def tile(b, carry2):
                @pl.when(wanted(b))
                def _():
                    @pl.when(flags[b] > 0)
                    def _():
                        fast_tile(ftt, tf, sf, (buf0, buf1), ops, b)

                    @pl.when(flags[b] == 0)
                    def _():
                        direct_tile(stage, raw, xt, ops, b)

                    apply_operators(ops, xs, wh, wl, acc, b)

                return carry2

            lax.fori_loop(0, TPB, tile, 0)

        return carry

    lax.fori_loop(0, total, source, 0)
    for b in range(TPB):
        for g in range(4):
            out[g * NRHS : (g + 1) * NRHS, b * BLK : (b + 1) * BLK] = acc[b, :, g * BLK : (g + 1) * BLK]


def near_call(mask, test, sources, begins, base=None):
    groups = tuple((cur.shape[1] // BLK, begin) for (_, cur), begin in zip(sources, begins))
    operands = [mask, test]
    for pan, cur in sources:
        operands += [pan, cur]
    if base is not None:
        operands.append(base)
    vmem = pl.BlockSpec(memory_space=pltpu.VMEM)
    return pl.pallas_call(
        functools.partial(near_kernel, groups, base is not None),
        out_shape=jax.ShapeDtypeStruct((4 * NRHS, TPB * BLK), F32),
        in_specs=[pl.BlockSpec(memory_space=pltpu.SMEM)] + [vmem] * (len(operands) - 1),
        out_specs=vmem,
        scratch_shapes=[
            pltpu.VMEM((GROWS, BLK), F32),
            pltpu.VMEM((7, 8, BLK), F32),
            pltpu.VMEM(((NTERM + 16) * 16, BLK), F32),
            pltpu.VMEM((TROWS * 8, BLK), F32),
            pltpu.VMEM((KDIM, NOUT * 256), BF16),
            pltpu.VMEM((NCH * MROWS, KDIM), BF16),
            pltpu.VMEM((MROWS, NOUT * 256), F32),
            pltpu.VMEM((MROWS, NOUT * 256), F32),
            pltpu.VMEM((6, BLK, BLK), F32),
            pltpu.VMEM((2 * BLK, 4 * BLK), BF16),
            pltpu.VMEM((4 * BLK, 4 * BLK), BF16),
            pltpu.VMEM((4 * BLK, 4 * BLK), BF16),
            pltpu.VMEM((TPB, BLK, 4 * BLK), F32),
            pltpu.VMEM((8 * 16, BLK), F32),
            pltpu.SMEM((TPB,), jnp.int32),
        ],
        compiler_params=pltpu.CompilerParams(vmem_limit_bytes=48 * 1024 * 1024),
        cost_estimate=pl.CostEstimate(flops=2 * 10**10, bytes_accessed=4 * 10**6, transcendentals=0),
    )(*operands)


def body(panels, test_points, currents, near_mask):
    count = lax.axis_size("cluster") * lax.axis_size("narrow")
    axes = ("cluster", "narrow")
    forward = [(i, (i + 1) % count) for i in range(count)]
    backward = [(target, source) for source, target in forward]
    width = REACH * BLK
    size = panels.shape[1]
    lows = [lax.ppermute(v[:, size - width :], axes, forward) for v in (panels, currents)]
    highs = [lax.ppermute(v[:, :width], axes, backward) for v in (panels, currents)]
    own = near_call(near_mask, test_points, [(panels, currents)], (0,))
    return near_call(near_mask, test_points, [tuple(lows), tuple(highs)], (-REACH, TPB), own)


def solution(mesh):
    return jax.shard_map(
        body,
        mesh=mesh,
        in_specs=(
            P(None, ("cluster", "narrow")),
            P(None, ("cluster", "narrow")),
            P(None, ("cluster", "narrow")),
            P(("cluster", "narrow"), None),
        ),
        out_specs=P(None, ("cluster", "narrow")),
        check_vma=False,
    )
```

```python
import functools
import itertools
import math

import jax
import jax.numpy as jnp
from jax import lax
from jax.experimental import pallas as pl
from jax.experimental.pallas import tpu as pltpu
from jax.sharding import PartitionSpec as P

F32 = jnp.float32
BF16 = jnp.bfloat16
BLK = 128
QP = 14
REACH = 3
SPAN = 7
TPB = 4
GROWS = 98
NRHS = 128
SOFTEN = 0.04

Z_MAX = 14.0
DEGREE = 4
COS_HALF = (2.828426289053651, -0.35355064760758376, 0.007364148070439611, -6.107114702262049e-05, 2.4846120790492805e-07)
SIN_HALF = (1.4142135239177973, -0.05892543897495882, 0.0007364984722676873, -4.370137027858996e-06, 1.4053654408325383e-08)

TERMS = []
for _total in range(DEGREE + 1):
    for _j in range(_total + 1):
        _l = _total - _j
        for _a in itertools.product(range(_l + 1), repeat=3):
            if sum(_a) == _l:
                TERMS.append((_j, _a))
NTERM = 72
assert len(TERMS) <= NTERM
ONE = TERMS.index((0, (0, 0, 0)))
LIN = [TERMS.index((0, tuple(int(c == k) for c in range(3)))) for k in range(3)]
SQR = TERMS.index((1, (0, 0, 0)))
KDIM = 256
NOUT = 7
JC = 16
NCH = BLK // JC
MROWS = JC * QP


def powers_of(vec):
    one = None
    table = {(0, 0, 0): one}
    for total in range(1, DEGREE + 1):
        for a in itertools.product(range(total + 1), repeat=3):
            if sum(a) != total:
                continue
            axis = next(c for c in range(3) if a[c] > 0)
            prev = tuple(a[c] - (c == axis) for c in range(3))
            table[a] = vec[axis] if table[prev] is None else table[prev] * vec[axis]
    return table


def split2(value):
    high = value.astype(BF16).astype(F32)
    return high, value - high


def source_features(stage, fts, sf, centre, y):
    mono = powers_of(y)
    square = y[0] * y[0] + y[1] * y[1] + y[2] * y[2]
    sq = [None, square, square * square]
    sq.append(sq[2] * square)
    sq.append(sq[2] * sq[2])
    ones = jnp.ones_like(square)

    def put(row, value):
        fts[row * 16 : row * 16 + QP, :] = value

    for k, (j, a) in enumerate(TERMS):
        const = (-2.0) ** sum(a) / (math.prod(math.factorial(v) for v in a) * math.factorial(j))
        value = mono[a]
        if sq[j] is not None:
            value = sq[j] if value is None else value * sq[j]
        if value is None:
            value = ones
        put(k, value * const if const != 1.0 else value)
    base = NTERM
    s = [stage[(3 + c) * QP : (4 + c) * QP, :] for c in range(3)]
    d = stage[6 * QP : 7 * QP, :]
    for c in range(3):
        put(base + c, s[c])
    put(base + 3, d)
    for c in range(3):
        c1, c2 = (c + 1) % 3, (c + 2) % 3
        put(base + 4 + c, y[c1] * s[c2] - y[c2] * s[c1])
    extra = base + 8
    for half in range(2):
        for c in range(3):
            put(extra + 4 * half + c, y[c] * -2.0)
        put(extra + 4 * half + 3, square)
    rows = lax.broadcasted_iota(jnp.int32, (8, BLK), 0)
    for q in range(QP):
        main = fts[pl.ds(q, NTERM, stride=16), :]
        bil = fts[pl.ds(base * 16 + q, 8, stride=16), :]
        ext = fts[pl.ds(extra * 16 + q, 8, stride=16), :]
        mh, ml = split2(main)
        bh, bl = split2(bil)
        eh, rest = split2(ext)
        em, el = split2(rest)
        zrow = jnp.where(rows < 4, em, eh)
        zrow2 = jnp.where(rows < 4, el, jnp.where(rows == 4, 1.0, 0.0))
        full = jnp.concatenate([mh, mh, ml, bh, bh, bl, zrow, zrow2], 0)
        turned = full.T.astype(BF16)
        for ch in range(NCH):
            sf[ch * MROWS + q * JC : ch * MROWS + (q + 1) * JC, :] = turned[ch * JC : (ch + 1) * JC, :]


def horner(coefs, m, w):
    der = [coefs[k] * math.factorial(k) / math.factorial(k - m) for k in range(m, len(coefs))]
    value = None
    for c in reversed(der):
        value = c if value is None else value * w + c
    return value


OFF_C, OFF_S, OFF_Z = 0, NTERM, 2 * NTERM
OFF_B = 3 * NTERM
OFF_E = OFF_B + 32
TROWS = OFF_E + 16


def test_features(xt, ftt, centre):
    x = [xt[c] - centre[c] for c in range(3)]
    t = [xt[3 + c] for c in range(3)]
    e = xt[6]
    w = x[0] * x[0] + x[1] * x[1] + x[2] * x[2] + SOFTEN
    mono = powers_of(x)

    def put(row, value):
        ftt[row * 8 : row * 8 + 8, :] = value

    for off, coefs in ((OFF_C, COS_HALF), (OFF_S, SIN_HALF)):
        der = [horner(coefs, m, w) for m in range(DEGREE + 1)]
        for k, (j, a) in enumerate(TERMS):
            level = der[j + sum(a)]
            value = level if mono[a] is None else mono[a] * level
            put(off + k, jnp.broadcast_to(value, w.shape))
    put(OFF_Z + ONE, w)
    put(OFF_Z + SQR, jnp.ones_like(w))
    for c in range(3):
        put(OFF_Z + LIN[c], x[c])
    charge = e * -0.25
    for c in range(3):
        put(OFF_B + c, t[c])
        put(OFF_B + 8 + c, t[c] * -2.0)
        put(OFF_B + 16 + c, t[c] * 1.5)
        c1, c2 = (c + 1) % 3, (c + 2) % 3
        put(OFF_B + 24 + c, (t[c1] * x[c2] - t[c2] * x[c1]) * -0.25)
        put(OFF_B + 28 + c, t[c] * 0.25)
    put(OFF_B + 3, charge)
    put(OFF_B + 11, charge)
    for half in range(2):
        for c in range(3):
            put(OFF_E + 4 * half + c, x[c])
        put(OFF_E + 4 * half + 3, jnp.ones_like(w))
    for c in range(4):
        put(OFF_E + 8 + c, x[c] if c < 3 else jnp.ones_like(w))
    put(OFF_E + 12, w)


def test_matrix(ftt, tf, b):
    rows = lax.broadcasted_iota(jnp.int32, (8, BLK), 0)
    zero8 = jnp.zeros((8, BLK), F32)
    for a in range(2):
        ba = 2 * b + a

        def take(off, n):
            return ftt[pl.ds(off * 8 + ba, n, stride=8), :]

        for out, off in ((0, OFF_Z), (1, OFF_C), (2, OFF_S)):
            high, low = split2(take(off, NTERM))
            lanes = slice(out * 256 + a * BLK, out * 256 + (a + 1) * BLK)
            tf[0:224, lanes] = jnp.concatenate([high, low, high, zero8], 0).astype(BF16)
        eh, rest = split2(take(OFF_E, 8))
        em, el = split2(rest)
        fh, rest2 = split2(take(OFF_E + 8, 8))
        fm, fl = split2(rest2)
        first = jnp.where(rows < 4, em, el)
        second = jnp.where(rows < 4, fh, jnp.where(rows == 4, fl, 0.0))
        tf[240:256, a * BLK : (a + 1) * BLK] = jnp.concatenate([first, second], 0).astype(BF16)
        for m in range(4):
            high, low = split2(take(OFF_B + 8 * m, 8))
            out = 3 + m
            lanes = slice(out * 256 + a * BLK, out * 256 + (a + 1) * BLK)
            tf[208:240, lanes] = jnp.concatenate([zero8, high, low, high], 0).astype(BF16)


EXP_RATE = -3.0 / math.log(2.0)


def pair_terms(z, cos_h, sin_h, k1, k2, k6, kk):
    inv = lax.rsqrt(z)
    dist = z * inv
    s0 = sin_h * dist
    c = 4.0 - s0 * s0
    s = s0 * cos_h
    c2 = c * c - 8.0
    s2 = c * s
    decay = jnp.exp2(dist * EXP_RATE)
    p = decay * c
    q = decay * s
    half = inv * 0.5
    c2r = c2 * half
    s2r = s2 * half
    pr = p * inv
    qr = q * inv
    weight = kk * (inv * inv)
    l1r = k1 * c2r
    l1i = k1 * s2r
    l2r = k2 * pr - k6 * qr
    l2i = k2 * qr + k6 * pr
    kr = weight * (((c2r + pr) + (s2 + 3.0 * p)) + q)
    ki = weight * (((s2r + qr) + (3.0 * q - c2)) - p)
    return l1r, l1i, l2r, l2i, kr, ki


def chunk_sums(buf, ops, chunk):
    for g in range(JC // 8):
        acc = None
        for q in range(QP):
            for a in range(2):
                row = q * JC + g * 8
                vals = [buf[row : row + 8, o * 256 + a * BLK : o * 256 + (a + 1) * BLK] for o in range(NOUT)]
                terms = pair_terms(*vals)
                acc = list(terms) if acc is None else [u + v for u, v in zip(acc, terms)]
        start = pl.multiple_of(chunk * JC + g * 8, 8)
        for m in range(6):
            ops[m, pl.ds(start, 8), :] = acc[m]


def fast_tile(ftt, tf, sf, bufs, ops, b):
    test_matrix(ftt, tf, b)

    def product(chunk, buf):
        rows = pl.ds(pl.multiple_of(chunk * MROWS, 16), MROWS)
        buf[...] = jnp.dot(sf[rows, :], tf[...], preferred_element_type=F32)

    product(0, bufs[0])

    def step(n, carry):
        product(2 * n + 1, bufs[1])
        chunk_sums(bufs[0], ops, 2 * n)
        product((2 * n + 2) % NCH, bufs[0])
        chunk_sums(bufs[1], ops, 2 * n + 1)
        return carry

    lax.fori_loop(0, NCH // 2, step, 0)


def direct_tile(stage, raw, xt, ops, b):
    for c in range(7):
        raw[c * 16 : c * 16 + QP, :] = stage[c * QP : (c + 1) * QP, :]
    raw[7 * 16 : 8 * 16, :] = jnp.zeros((16, BLK), F32)
    for m in range(6):
        ops[m] = jnp.zeros((BLK, BLK), F32)

    def point(q, carry):
        rows8 = raw[pl.ds(q, 8, stride=16), :]
        turned = jnp.concatenate([rows8, jnp.zeros((BLK - 8, BLK), F32)], 0).T
        src = [turned[:, c : c + 1] for c in range(7)]

        def centroid(a, carry2):
            tst = [xt[c, pl.ds(2 * b + a, 1), :] for c in range(7)]
            dl = [tst[c] - src[c] for c in range(3)]
            dist = jnp.sqrt(dl[0] * dl[0] + dl[1] * dl[1] + dl[2] * dl[2] + SOFTEN)
            dotted = tst[3] * src[3] + tst[4] * src[4] + tst[5] * src[5]
            charge = tst[6] * src[6]
            crossed = (
                dl[0] * (src[4] * tst[5] - src[5] * tst[4])
                + dl[1] * (src[5] * tst[3] - src[3] * tst[5])
                + dl[2] * (src[3] * tst[4] - src[4] * tst[3])
            )
            scaled = crossed / (dist * dist)
            kr = ki = None
            for m, (wr, wi) in enumerate(((2.0, 0.0), (1.0, 3.0))):
                decay = jnp.exp(-wi * dist) / dist
                gr = decay * jnp.cos(wr * dist)
                gi = decay * jnp.sin(wr * dist)
                cr = (wr * wr - wi * wi) * dotted - charge
                ci = 2.0 * wr * wi * dotted
                ops[2 * m] += cr * gr - ci * gi
                ops[2 * m + 1] += cr * gi + ci * gr
                fr = -wi * dist - 1.0
                fi = wr * dist
                ops[4] += scaled * (fr * gr - fi * gi)
                ops[5] += scaled * (fr * gi + fi * gr)
            return carry2

        return lax.fori_loop(0, 2, centroid, carry)

    lax.fori_loop(0, QP, point, 0)


def apply_operators(ops, xs, wh, wl, acc, b):
    def put(ref, value, places):
        neg = -value
        for row, col, sign in places:
            ref[row * BLK : (row + 1) * BLK, col * BLK : (col + 1) * BLK] = value if sign > 0 else neg

    def both(value, places):
        high = value.astype(BF16)
        low = (value - high.astype(F32)).astype(BF16)
        put(wh, high, places)
        put(wl, low, places)

    l1r, l1i, l2r, l2i = (ops[m] for m in range(4))
    both(l1r + l2r, ((0, 0, 1), (1, 1, 1)))
    both(l1i + l2i, ((0, 1, 1), (1, 0, -1)))
    both(l1r + 0.5 * l2r, ((2, 2, 1), (3, 3, 1)))
    both(l1i + 0.5 * l2i, ((2, 3, 1), (3, 2, -1)))
    both(ops[4], ((0, 2, 1), (1, 3, 1), (2, 0, -1), (3, 1, -1)))
    both(ops[5], ((0, 3, 1), (1, 2, -1), (2, 1, -1), (3, 0, 1)))
    first = jnp.dot(xs[...], wh[...], preferred_element_type=F32)
    second = jnp.dot(xs[0:BLK, :], wl[...], preferred_element_type=F32)
    acc[b] += first[0:BLK] + first[BLK:] + second


CROW = 104
XROW = CROW + 4 * NRHS
OUTER_ROWS = XROW + 64 + 8
FAR_ROWS = XROW + 32 + 8
MATE_ROWS = XROW
FULL = TPB * SPAN


def is_even():
    return lax.axis_index("narrow") == 0


def mirrored(even, block):
    return jnp.where(even, block, TPB - 1 - block)


def load_of(mask):
    total = mask[0, 0]
    for b in range(TPB):
        for c in range(SPAN):
            if b or c:
                total = total + mask[b, c]
    return total


def number(ref, row):
    return jnp.max(ref[row : row + 8, 0:BLK]).astype(jnp.int32)


def shares(load_near, load_far):
    goal = lax.div(FULL + load_near + load_far + 1, 3)
    return jnp.clip(goal - load_near, 6, 9), jnp.clip(goal - load_far, 0, 8)


def pack_kernel(mask, panels, test, currents, mate, outer, far, load):
    even = is_even()
    for ref, count, begin in (
        (mate, 3, jnp.where(even, BLK, 0)),
        (outer, 1, jnp.where(even, 0, 3 * BLK)),
        (far, 2, jnp.where(even, 2 * BLK, 0)),
    ):
        lanes = pl.ds(pl.multiple_of(begin, BLK), count * BLK)
        ref[0:GROWS, :] = panels[:, lanes]
        ref[CROW:XROW, :] = currents[:, lanes]
    value = load_of(mask).astype(F32)
    for b in range(TPB):
        points = test[:, b * BLK : (b + 1) * BLK]
        outer[XROW + 16 * b : XROW + 16 * b + 14, :] = points
        row = XROW + 16 * (b // 2)
        far[row : row + 14, (b % 2) * BLK : (b % 2 + 1) * BLK] = points
    outer[XROW + 64 : XROW + 72, :] = jnp.full((8, BLK), value, F32)
    far[XROW + 32 : XROW + 40, :] = jnp.full((8, 2 * BLK), value, F32)
    load[...] = jnp.full((8, BLK), value, F32)


def engine(scratch, steps, wanted, load_source, accset):
    stage, xt, fts, ftt, tf, sf, buf0, buf1, ops, xs, wh, wl, acc, raw, flags = scratch

    def source(n, carry):
        any_wanted = wanted(n, 0)
        for b in range(1, TPB):
            any_wanted = any_wanted | wanted(n, b)

        @pl.when(any_wanted)
        def _():
            load_source(n)
            points = xt.at[accset(n)]
            place = [stage[c * QP : (c + 1) * QP, :] for c in range(3)]
            low = [jnp.min(jnp.min(v, 0, keepdims=True), 1, keepdims=True) for v in place]
            high = [jnp.max(jnp.max(v, 0, keepdims=True), 1, keepdims=True) for v in place]
            centre = [(u + v) * 0.5 for u, v in zip(low, high)]
            bound = jnp.full((8, BLK), SOFTEN, F32)
            for c in range(3):
                far = jnp.maximum(jnp.abs(points[c] - low[c]), jnp.abs(points[c] - high[c]))
                bound = bound + far * far
            for b in range(TPB):
                flags[b] = (jnp.max(bound[2 * b : 2 * b + 2]) <= Z_MAX).astype(jnp.int32)
            source_features(stage, fts, sf, centre, [place[c] - centre[c] for c in range(3)])
            test_features(points, ftt, centre)

            def tile(b, carry2):
                @pl.when(wanted(n, b))
                def _():
                    @pl.when(flags[b] > 0)
                    def _():
                        fast_tile(ftt, tf, sf, (buf0, buf1), ops, b)

                    @pl.when(flags[b] == 0)
                    def _():
                        direct_tile(stage, raw, points, ops, b)

                    apply_operators(ops, xs, wh, wl, acc, TPB * accset(n) + b)

                return carry2

            lax.fori_loop(0, TPB, tile, 0)

        return carry

    tf[...] = jnp.zeros_like(tf)
    ftt[...] = jnp.zeros_like(ftt)
    fts[...] = jnp.zeros_like(fts)
    lax.fori_loop(0, steps, source, 0)


def fill(scratch, pan, cur, row, slot):
    stage, xs = scratch[0], scratch[9]
    lanes = pl.ds(pl.multiple_of(slot * BLK, BLK), BLK)
    stage[...] = pan[0:GROWS, lanes]
    for g in range(4):
        value = cur[row + g * NRHS : row + (g + 1) * NRHS, lanes]
        high = value.astype(BF16)
        xs[0:BLK, g * BLK : (g + 1) * BLK] = high
        xs[BLK : 2 * BLK, g * BLK : (g + 1) * BLK] = (value - high.astype(F32)).astype(BF16)


def fill_tests(xt, which, blocks):
    for c in range(7):
        for b in range(TPB):
            xt[which, c, 2 * b : 2 * b + 2, :] = blocks(b, 2 * c)


def own_tests(test):
    return lambda b, row: test[row : row + 2, b * BLK : (b + 1) * BLK]


def clear(acc, count):
    for b in range(count):
        acc[b] = jnp.zeros((BLK, 4 * BLK), F32)


def write_out(out, acc, blocks):
    for col, b in enumerate(blocks):
        for g in range(4):
            out[g * NRHS : (g + 1) * NRHS, col * BLK : (col + 1) * BLK] = acc[b, :, g * BLK : (g + 1) * BLK]


def first_kernel(mask, test, panels, currents, out, *scratch):
    even = is_even()
    full = load_of(mask) == FULL
    fill_tests(scratch[1], 0, own_tests(test))
    clear(scratch[12], TPB)

    def wanted(n, b):
        return (full & (mirrored(even, n) == 1)) | (jnp.logical_not(full) & (n == b))

    engine(scratch, TPB, wanted, lambda n: fill(scratch, panels, currents, 0, n), lambda n: 0)
    write_out(out, scratch[12], range(TPB))


def help_kernel(mask, panels, currents, outer, far, load_mate, after, out_near, out_far, *scratch):
    even = is_even()
    odd = jnp.logical_not(even)
    own, mate = load_of(mask), number(load_mate, 0)
    near_full = number(outer, XROW + 64) == FULL
    far_full = number(far, XROW + 32) == FULL
    share_near, _ = shares(own, mate)
    _, share_far = shares(mate, own)
    xt, acc = scratch[1], scratch[12]
    fill_tests(xt, 0, lambda b, row: outer[XROW + 16 * b + row : XROW + 16 * b + row + 2, :])
    fill_tests(
        xt,
        1,
        lambda b, row: far[
            XROW + 16 * (b // 2) + row : XROW + 16 * (b // 2) + row + 2, (b % 2) * BLK : (b % 2 + 1) * BLK
        ],
    )
    clear(acc, 2 * TPB)

    def wanted(n, b):
        v_near, v_far = mirrored(odd, b), mirrored(even, b)
        of_own = (n < 3) & (v_near <= 2 - n)
        of_outer = (n == 3) & (v_near < share_near - 6)
        of_far = (n > 3) & ((n - 4) * TPB + v_far < share_far)
        return (near_full & (of_own | of_outer)) | (far_full & of_far)

    def load_source(n):
        @pl.when(n < 3)
        def _():
            fill(scratch, panels, currents, 0, mirrored(even, n))

        @pl.when(n == 3)
        def _():
            fill(scratch, outer, outer, CROW, 0)

        @pl.when(n > 3)
        def _():
            fill(scratch, far, far, CROW, jnp.where(even, 5 - n, n - 4))

    engine(scratch, 6, wanted, load_source, lambda n: jnp.where(n > 3, 1, 0))
    shift = jnp.where(even, 1, 0)
    write_out(out_near, acc, [b + shift for b in range(TPB - 1)])
    write_out(out_far, acc, range(TPB, 2 * TPB))


def rest_kernel(mask, test, panels, currents, outer, mate, load_far, part, after, out, *scratch):
    even = is_even()
    full = load_of(mask) == FULL
    share_near, share_far = shares(number(outer, XROW + 64), number(load_far, 0))
    acc = scratch[12]
    fill_tests(scratch[1], 0, own_tests(test))
    for b in range(TPB):
        for g in range(4):
            acc[b, :, g * BLK : (g + 1) * BLK] = part[g * NRHS : (g + 1) * NRHS, b * BLK : (b + 1) * BLK]

    def wanted(n, b):
        rel = jnp.where(n < 4, n, jnp.where(n == 4, jnp.where(even, -1, 4), jnp.where(even, n - 1, n - 8)))
        column = rel - b + REACH
        inside = (column >= 0) & (column < SPAN)
        sparse = inside & (mask[b, jnp.clip(column, 0, SPAN - 1)] > 0) & (rel != b)
        u, v = mirrored(even, rel), mirrored(even, b)
        given = (u == 1) | ((u == 0) & (v < share_near - 6))
        given = given | ((u == 3) & (v < share_far)) | ((u == 2) & (TPB + v < share_far))
        dense = inside & (u >= 0) & jnp.logical_not(given)
        return (full & dense) | (jnp.logical_not(full) & sparse)

    def load_source(n):
        @pl.when(n < 4)
        def _():
            fill(scratch, panels, currents, 0, n)

        @pl.when(n == 4)
        def _():
            fill(scratch, outer, outer, CROW, 0)

        @pl.when(n > 4)
        def _():
            fill(scratch, mate, mate, CROW, n - 5)

    engine(scratch, 8, wanted, load_source, lambda n: 0)
    write_out(out, acc, range(TPB))


def scratch_for(sets):
    return [
        pltpu.VMEM((GROWS, BLK), F32),
        pltpu.VMEM((sets, 7, 8, BLK), F32),
        pltpu.VMEM(((NTERM + 16) * 16, BLK), F32),
        pltpu.VMEM((TROWS * 8, BLK), F32),
        pltpu.VMEM((KDIM, NOUT * 256), BF16),
        pltpu.VMEM((NCH * MROWS, KDIM), BF16),
        pltpu.VMEM((MROWS, NOUT * 256), F32),
        pltpu.VMEM((MROWS, NOUT * 256), F32),
        pltpu.VMEM((6, BLK, BLK), F32),
        pltpu.VMEM((2 * BLK, 4 * BLK), BF16),
        pltpu.VMEM((4 * BLK, 4 * BLK), BF16),
        pltpu.VMEM((4 * BLK, 4 * BLK), BF16),
        pltpu.VMEM((sets * TPB, BLK, 4 * BLK), F32),
        pltpu.VMEM((8 * 16, BLK), F32),
        pltpu.SMEM((TPB,), jnp.int32),
    ]


def call(kernel, outs, operands, sets=0, unread=0, tiles=1):
    vmem = pl.BlockSpec(memory_space=pltpu.VMEM)
    anywhere = pl.BlockSpec(memory_space=pl.ANY)
    several = len(outs) > 1
    plain = len(operands) - 1 - unread
    return pl.pallas_call(
        kernel,
        out_shape=[jax.ShapeDtypeStruct(s, F32) for s in outs] if several else jax.ShapeDtypeStruct(outs[0], F32),
        in_specs=[pl.BlockSpec(memory_space=pltpu.SMEM)] + [vmem] * plain + [anywhere] * unread,
        out_specs=[vmem] * len(outs) if several else vmem,
        scratch_shapes=scratch_for(sets) if sets else [],
        compiler_params=pltpu.CompilerParams(vmem_limit_bytes=48 * 1024 * 1024),
        cost_estimate=pl.CostEstimate(flops=tiles * 5 * 10**9, bytes_accessed=4 * 10**6, transcendentals=0),
    )(*operands)


def body(panels, test_points, currents, near_mask):
    count = lax.axis_size("cluster") * lax.axis_size("narrow")
    axes = ("cluster", "narrow")
    swap = [(i, i ^ 1) for i in range(count)]
    across = [(i, (i - 1) % count if i % 2 == 0 else (i + 1) % count) for i in range(count)]
    away = [(i, (i - 2) % count if i % 2 == 0 else (i + 2) % count) for i in range(count)]
    back = [(target, source) for source, target in away]
    width = TPB * BLK
    wide = 4 * NRHS
    mate, outer, far, load = call(
        pack_kernel,
        [(MATE_ROWS, 3 * BLK), (OUTER_ROWS, BLK), (FAR_ROWS, 2 * BLK), (8, BLK)],
        [near_mask, panels, test_points, currents],
    )
    load_mate = lax.ppermute(load, axes, swap)
    load_far = lax.ppermute(load, axes, back)
    outer = lax.ppermute(outer, axes, across)
    far = lax.ppermute(far, axes, away)
    mate = lax.ppermute(mate, axes, swap)
    part = call(first_kernel, [(wide, width)], [near_mask, test_points, panels, currents], 1, tiles=4)
    to_near, to_far = call(
        help_kernel,
        [(wide, width - BLK), (wide, width)],
        [near_mask, panels, currents, outer, far, load_mate, part],
        2,
        unread=1,
        tiles=7,
    )
    from_near = lax.ppermute(to_near, axes, across)
    from_far = lax.ppermute(to_far, axes, back)
    rest = call(
        rest_kernel,
        [(wide, width)],
        [near_mask, test_points, panels, currents, outer, mate, load_far, part, to_near],
        1,
        unread=1,
        tiles=8,
    )
    padded = jnp.where(
        lax.axis_index("narrow") == 0,
        jnp.pad(from_near, ((0, 0), (0, BLK))),
        jnp.pad(from_near, ((0, 0), (BLK, 0))),
    )
    return rest + from_far + padded


def solution(mesh):
    return jax.shard_map(
        body,
        mesh=mesh,
        in_specs=(
            P(None, ("cluster", "narrow")),
            P(None, ("cluster", "narrow")),
            P(None, ("cluster", "narrow")),
            P(("cluster", "narrow"), None),
        ),
        out_specs=P(None, ("cluster", "narrow")),
        check_vma=False,
    )
```

```python
import functools
import itertools
import math

import jax
import jax.numpy as jnp
from jax import lax
from jax.experimental import pallas as pl
from jax.experimental.pallas import tpu as pltpu
from jax.sharding import PartitionSpec as P

F32 = jnp.float32
BF16 = jnp.bfloat16
BLK = 128
QP = 14
REACH = 3
SPAN = 7
TPB = 4
GROWS = 98
NRHS = 128
SOFTEN = 0.04

Z_MAX = 14.0
DEGREE = 4
COS_HALF = (2.828426289053651, -0.35355064760758376, 0.007364148070439611, -6.107114702262049e-05, 2.4846120790492805e-07)
SIN_HALF = (1.4142135239177973, -0.05892543897495882, 0.0007364984722676873, -4.370137027858996e-06, 1.4053654408325383e-08)

TERMS = []
for _total in range(DEGREE + 1):
    for _j in range(_total + 1):
        _l = _total - _j
        for _a in itertools.product(range(_l + 1), repeat=3):
            if sum(_a) == _l:
                TERMS.append((_j, _a))
NTERM = 72
assert len(TERMS) <= NTERM
ONE = TERMS.index((0, (0, 0, 0)))
LIN = [TERMS.index((0, tuple(int(c == k) for c in range(3)))) for k in range(3)]
SQR = TERMS.index((1, (0, 0, 0)))
KDIM = 256
NOUT = 7
JC = 16
NCH = BLK // JC
MROWS = JC * QP


def powers_of(vec):
    one = None
    table = {(0, 0, 0): one}
    for total in range(1, DEGREE + 1):
        for a in itertools.product(range(total + 1), repeat=3):
            if sum(a) != total:
                continue
            axis = next(c for c in range(3) if a[c] > 0)
            prev = tuple(a[c] - (c == axis) for c in range(3))
            table[a] = vec[axis] if table[prev] is None else table[prev] * vec[axis]
    return table


def split2(value):
    high = value.astype(BF16).astype(F32)
    return high, value - high


def source_features(stage, fts, sf, centre, y):
    mono = powers_of(y)
    square = y[0] * y[0] + y[1] * y[1] + y[2] * y[2]
    sq = [None, square, square * square]
    sq.append(sq[2] * square)
    sq.append(sq[2] * sq[2])
    ones = jnp.ones_like(square)

    def put(row, value):
        fts[row * 16 : row * 16 + QP, :] = value

    for k, (j, a) in enumerate(TERMS):
        const = (-2.0) ** sum(a) / (math.prod(math.factorial(v) for v in a) * math.factorial(j))
        value = mono[a]
        if sq[j] is not None:
            value = sq[j] if value is None else value * sq[j]
        if value is None:
            value = ones
        put(k, value * const if const != 1.0 else value)
    base = NTERM
    s = [stage[(3 + c) * QP : (4 + c) * QP, :] for c in range(3)]
    d = stage[6 * QP : 7 * QP, :]
    for c in range(3):
        put(base + c, s[c])
    put(base + 3, d)
    for c in range(3):
        c1, c2 = (c + 1) % 3, (c + 2) % 3
        put(base + 4 + c, y[c1] * s[c2] - y[c2] * s[c1])
    extra = base + 8
    for half in range(2):
        for c in range(3):
            put(extra + 4 * half + c, y[c] * -2.0)
        put(extra + 4 * half + 3, square)
    rows = lax.broadcasted_iota(jnp.int32, (8, BLK), 0)
    for q in range(QP):
        main = fts[pl.ds(q, NTERM, stride=16), :]
        bil = fts[pl.ds(base * 16 + q, 8, stride=16), :]
        ext = fts[pl.ds(extra * 16 + q, 8, stride=16), :]
        mh, ml = split2(main)
        bh, bl = split2(bil)
        eh, rest = split2(ext)
        em, el = split2(rest)
        zrow = jnp.where(rows < 4, em, eh)
        zrow2 = jnp.where(rows < 4, el, jnp.where(rows == 4, 1.0, 0.0))
        full = jnp.concatenate([mh, mh, ml, bh, bh, bl, zrow, zrow2], 0)
        turned = full.T.astype(BF16)
        for ch in range(NCH):
            sf[ch * MROWS + q * JC : ch * MROWS + (q + 1) * JC, :] = turned[ch * JC : (ch + 1) * JC, :]


def horner(coefs, m, w):
    der = [coefs[k] * math.factorial(k) / math.factorial(k - m) for k in range(m, len(coefs))]
    value = None
    for c in reversed(der):
        value = c if value is None else value * w + c
    return value


OFF_C, OFF_S, OFF_Z = 0, NTERM, 2 * NTERM
OFF_B = 3 * NTERM
OFF_E = OFF_B + 32
TROWS = OFF_E + 16


def test_features(xt, ftt, centre):
    x = [xt[c] - centre[c] for c in range(3)]
    t = [xt[3 + c] for c in range(3)]
    e = xt[6]
    w = x[0] * x[0] + x[1] * x[1] + x[2] * x[2] + SOFTEN
    mono = powers_of(x)

    def put(row, value):
        ftt[row * 8 : row * 8 + 8, :] = value

    for off, coefs in ((OFF_C, COS_HALF), (OFF_S, SIN_HALF)):
        der = [horner(coefs, m, w) for m in range(DEGREE + 1)]
        for k, (j, a) in enumerate(TERMS):
            level = der[j + sum(a)]
            value = level if mono[a] is None else mono[a] * level
            put(off + k, jnp.broadcast_to(value, w.shape))
    put(OFF_Z + ONE, w)
    put(OFF_Z + SQR, jnp.ones_like(w))
    for c in range(3):
        put(OFF_Z + LIN[c], x[c])
    charge = e * -0.25
    for c in range(3):
        put(OFF_B + c, t[c])
        put(OFF_B + 8 + c, t[c] * -2.0)
        put(OFF_B + 16 + c, t[c] * 1.5)
        c1, c2 = (c + 1) % 3, (c + 2) % 3
        put(OFF_B + 24 + c, (t[c1] * x[c2] - t[c2] * x[c1]) * -0.25)
        put(OFF_B + 28 + c, t[c] * 0.25)
    put(OFF_B + 3, charge)
    put(OFF_B + 11, charge)
    for half in range(2):
        for c in range(3):
            put(OFF_E + 4 * half + c, x[c])
        put(OFF_E + 4 * half + 3, jnp.ones_like(w))
    for c in range(4):
        put(OFF_E + 8 + c, x[c] if c < 3 else jnp.ones_like(w))
    put(OFF_E + 12, w)


def test_matrix(ftt, tf, b):
    rows = lax.broadcasted_iota(jnp.int32, (8, BLK), 0)
    zero8 = jnp.zeros((8, BLK), F32)
    for a in range(2):
        ba = 2 * b + a

        def take(off, n):
            return ftt[pl.ds(off * 8 + ba, n, stride=8), :]

        for out, off in ((0, OFF_Z), (1, OFF_C), (2, OFF_S)):
            high, low = split2(take(off, NTERM))
            lanes = slice(out * 256 + a * BLK, out * 256 + (a + 1) * BLK)
            tf[0:224, lanes] = jnp.concatenate([high, low, high, zero8], 0).astype(BF16)
        eh, rest = split2(take(OFF_E, 8))
        em, el = split2(rest)
        fh, rest2 = split2(take(OFF_E + 8, 8))
        fm, fl = split2(rest2)
        first = jnp.where(rows < 4, em, el)
        second = jnp.where(rows < 4, fh, jnp.where(rows == 4, fl, 0.0))
        tf[240:256, a * BLK : (a + 1) * BLK] = jnp.concatenate([first, second], 0).astype(BF16)
        for m in range(4):
            high, low = split2(take(OFF_B + 8 * m, 8))
            out = 3 + m
            lanes = slice(out * 256 + a * BLK, out * 256 + (a + 1) * BLK)
            tf[208:240, lanes] = jnp.concatenate([zero8, high, low, high], 0).astype(BF16)


EXP_RATE = -3.0 / math.log(2.0)


def pair_terms(z, cos_h, sin_h, k1, k2, k6, kk):
    inv = lax.rsqrt(z)
    dist = z * inv
    s0 = sin_h * dist
    c = 4.0 - s0 * s0
    s = s0 * cos_h
    c2 = c * c - 8.0
    s2 = c * s
    decay = jnp.exp2(dist * EXP_RATE)
    p = decay * c
    q = decay * s
    half = inv * 0.5
    c2r = c2 * half
    s2r = s2 * half
    pr = p * inv
    qr = q * inv
    weight = kk * (inv * inv)
    l1r = k1 * c2r
    l1i = k1 * s2r
    l2r = k2 * pr - k6 * qr
    l2i = k2 * qr + k6 * pr
    kr = weight * (((c2r + pr) + (s2 + 3.0 * p)) + q)
    ki = weight * (((s2r + qr) + (3.0 * q - c2)) - p)
    return l1r, l1i, l2r, l2i, kr, ki


AHEAD = 6


def fast_tile(ftt, tf, sf, bufs, ops, b, flag):
    test_matrix(ftt, tf, b)
    spare = pl.multiple_of(MROWS - 8 + 8 * flag, 8)

    def piece(chunk, buf, o):
        rows = pl.ds(pl.multiple_of(chunk * MROWS, 16), MROWS)
        lanes = slice(o * 256, (o + 1) * 256)
        buf[0:MROWS, lanes] = jnp.dot(sf[rows, :], tf[:, lanes], preferred_element_type=F32)

    def phase(chunk, buf, next_chunk, next_buf):
        work = [(g, q, a) for g in range(JC // 8) for q in range(QP) for a in range(2)]
        per = -(-len(work) // NOUT)
        acc, history = None, []
        for o in range(NOUT):
            piece(next_chunk, next_buf, o)
            for g, q, a in work[o * per : (o + 1) * per]:
                if q == 0 and a == 0:
                    acc = None
                row = q * JC + g * 8
                if len(history) >= AHEAD:
                    buf[pl.ds(spare, 8), 0:BLK] = history[-AHEAD]
                vals = [buf[row : row + 8, k * 256 + a * BLK : k * 256 + (a + 1) * BLK] for k in range(NOUT)]
                terms = pair_terms(*vals)
                acc = list(terms) if acc is None else [u + v for u, v in zip(acc, terms)]
                history.append(acc[5])
                if q == QP - 1 and a == 1:
                    start = pl.multiple_of(chunk * JC + g * 8, 8)
                    for m in range(6):
                        ops[m, pl.ds(start, 8), :] = acc[m]

    for o in range(NOUT):
        piece(0, bufs[0], o)

    def step(n, carry):
        phase(2 * n, bufs[0], 2 * n + 1, bufs[1])
        phase(2 * n + 1, bufs[1], lax.rem(2 * n + 2, NCH), bufs[0])
        return carry

    lax.fori_loop(0, NCH // 2, step, 0)


def direct_tile(stage, raw, xt, ops, b):
    for c in range(7):
        raw[c * 16 : c * 16 + QP, :] = stage[c * QP : (c + 1) * QP, :]
    raw[7 * 16 : 8 * 16, :] = jnp.zeros((16, BLK), F32)
    for m in range(6):
        ops[m] = jnp.zeros((BLK, BLK), F32)

    def point(q, carry):
        rows8 = raw[pl.ds(q, 8, stride=16), :]
        turned = jnp.concatenate([rows8, jnp.zeros((BLK - 8, BLK), F32)], 0).T
        src = [turned[:, c : c + 1] for c in range(7)]

        def centroid(a, carry2):
            tst = [xt[c, pl.ds(2 * b + a, 1), :] for c in range(7)]
            dl = [tst[c] - src[c] for c in range(3)]
            dist = jnp.sqrt(dl[0] * dl[0] + dl[1] * dl[1] + dl[2] * dl[2] + SOFTEN)
            dotted = tst[3] * src[3] + tst[4] * src[4] + tst[5] * src[5]
            charge = tst[6] * src[6]
            crossed = (
                dl[0] * (src[4] * tst[5] - src[5] * tst[4])
                + dl[1] * (src[5] * tst[3] - src[3] * tst[5])
                + dl[2] * (src[3] * tst[4] - src[4] * tst[3])
            )
            scaled = crossed / (dist * dist)
            kr = ki = None
            for m, (wr, wi) in enumerate(((2.0, 0.0), (1.0, 3.0))):
                decay = jnp.exp(-wi * dist) / dist
                gr = decay * jnp.cos(wr * dist)
                gi = decay * jnp.sin(wr * dist)
                cr = (wr * wr - wi * wi) * dotted - charge
                ci = 2.0 * wr * wi * dotted
                ops[2 * m] += cr * gr - ci * gi
                ops[2 * m + 1] += cr * gi + ci * gr
                fr = -wi * dist - 1.0
                fi = wr * dist
                ops[4] += scaled * (fr * gr - fi * gi)
                ops[5] += scaled * (fr * gi + fi * gr)
            return carry2

        return lax.fori_loop(0, 2, centroid, carry)

    lax.fori_loop(0, QP, point, 0)


def apply_operators(ops, xs, wh, wl, acc, b):
    def put(ref, value, places):
        neg = -value
        for row, col, sign in places:
            ref[row * BLK : (row + 1) * BLK, col * BLK : (col + 1) * BLK] = value if sign > 0 else neg

    def both(value, places):
        high = value.astype(BF16)
        low = (value - high.astype(F32)).astype(BF16)
        put(wh, high, places)
        put(wl, low, places)

    l1r, l1i, l2r, l2i = (ops[m] for m in range(4))
    both(l1r + l2r, ((0, 0, 1), (1, 1, 1)))
    both(l1i + l2i, ((0, 1, 1), (1, 0, -1)))
    both(l1r + 0.5 * l2r, ((2, 2, 1), (3, 3, 1)))
    both(l1i + 0.5 * l2i, ((2, 3, 1), (3, 2, -1)))
    both(ops[4], ((0, 2, 1), (1, 3, 1), (2, 0, -1), (3, 1, -1)))
    both(ops[5], ((0, 3, 1), (1, 2, -1), (2, 1, -1), (3, 0, 1)))
    first = jnp.dot(xs[...], wh[...], preferred_element_type=F32)
    second = jnp.dot(xs[0:BLK, :], wl[...], preferred_element_type=F32)
    acc[b] += first[0:BLK] + first[BLK:] + second


CROW = 104
XROW = CROW + 4 * NRHS
OUTER_ROWS = XROW + 64 + 8
FAR_ROWS = XROW + 32 + 8
MATE_ROWS = XROW + 8
FULL = TPB * SPAN


def is_even():
    return lax.axis_index("narrow") == 0


def mirrored(even, block):
    return jnp.where(even, block, TPB - 1 - block)


def load_of(mask):
    total = mask[0, 0]
    for b in range(TPB):
        for c in range(SPAN):
            if b or c:
                total = total + mask[b, c]
    return total


def number(ref, row):
    return jnp.max(ref[row : row + 8, 0:BLK]).astype(jnp.int32)


def shares(load_near, load_far):
    goal = lax.div(FULL + load_near + load_far + 1, 3)
    return jnp.clip(goal - load_near, 6, 9), jnp.clip(goal - load_far, 0, 8)


def pack_kernel(mask, panels, test, currents, mate, outer, far, load):
    even = is_even()
    for ref, count, begin in (
        (mate, 3, jnp.where(even, BLK, 0)),
        (outer, 1, jnp.where(even, 0, 3 * BLK)),
        (far, 2, jnp.where(even, 2 * BLK, 0)),
    ):
        lanes = pl.ds(pl.multiple_of(begin, BLK), count * BLK)
        ref[0:GROWS, :] = panels[:, lanes]
        ref[CROW:XROW, :] = currents[:, lanes]
    value = load_of(mask).astype(F32)
    for b in range(TPB):
        points = test[:, b * BLK : (b + 1) * BLK]
        outer[XROW + 16 * b : XROW + 16 * b + 14, :] = points
        row = XROW + 16 * (b // 2)
        far[row : row + 14, (b % 2) * BLK : (b % 2 + 1) * BLK] = points
    outer[XROW + 64 : XROW + 72, :] = jnp.full((8, BLK), value, F32)
    far[XROW + 32 : XROW + 40, :] = jnp.full((8, 2 * BLK), value, F32)
    mate[XROW : XROW + 8, :] = jnp.full((8, 3 * BLK), value, F32)
    load[...] = jnp.full((8, BLK), value, F32)


def engine(scratch, steps, wanted, load_source, accset):
    stage, xt, fts, ftt, tf, sf, buf0, buf1, ops, xs, wh, wl, acc, raw, flags = scratch

    def source(n, carry):
        any_wanted = wanted(n, 0)
        for b in range(1, TPB):
            any_wanted = any_wanted | wanted(n, b)

        @pl.when(any_wanted)
        def _():
            load_source(n)
            points = xt.at[accset(n)]
            place = [stage[c * QP : (c + 1) * QP, :] for c in range(3)]
            low = [jnp.min(jnp.min(v, 0, keepdims=True), 1, keepdims=True) for v in place]
            high = [jnp.max(jnp.max(v, 0, keepdims=True), 1, keepdims=True) for v in place]
            centre = [(u + v) * 0.5 for u, v in zip(low, high)]
            bound = jnp.full((8, BLK), SOFTEN, F32)
            for c in range(3):
                far = jnp.maximum(jnp.abs(points[c] - low[c]), jnp.abs(points[c] - high[c]))
                bound = bound + far * far
            for b in range(TPB):
                flags[b] = (jnp.max(bound[2 * b : 2 * b + 2]) <= Z_MAX).astype(jnp.int32)
            source_features(stage, fts, sf, centre, [place[c] - centre[c] for c in range(3)])
            test_features(points, ftt, centre)

            def tile(b, carry2):
                @pl.when(wanted(n, b))
                def _():
                    @pl.when(flags[b] > 0)
                    def _():
                        fast_tile(ftt, tf, sf, (buf0, buf1), ops, b, flags[b])

                    @pl.when(flags[b] == 0)
                    def _():
                        direct_tile(stage, raw, points, ops, b)

                    apply_operators(ops, xs, wh, wl, acc, TPB * accset(n) + b)

                return carry2

            lax.fori_loop(0, TPB, tile, 0)

        return carry

    tf[...] = jnp.zeros_like(tf)
    ftt[...] = jnp.zeros_like(ftt)
    fts[...] = jnp.zeros_like(fts)
    lax.fori_loop(0, steps, source, 0)


def fill(scratch, pan, cur, row, slot):
    stage, xs = scratch[0], scratch[9]
    lanes = pl.ds(pl.multiple_of(slot * BLK, BLK), BLK)
    stage[...] = pan[0:GROWS, lanes]
    for g in range(4):
        value = cur[row + g * NRHS : row + (g + 1) * NRHS, lanes]
        high = value.astype(BF16)
        xs[0:BLK, g * BLK : (g + 1) * BLK] = high
        xs[BLK : 2 * BLK, g * BLK : (g + 1) * BLK] = (value - high.astype(F32)).astype(BF16)


def fill_tests(xt, which, blocks):
    for c in range(7):
        for b in range(TPB):
            xt[which, c, 2 * b : 2 * b + 2, :] = blocks(b, 2 * c)


def own_tests(test):
    return lambda b, row: test[row : row + 2, b * BLK : (b + 1) * BLK]


def clear(acc, count):
    for b in range(count):
        acc[b] = jnp.zeros((BLK, 4 * BLK), F32)


def write_out(out, acc, blocks):
    for col, b in enumerate(blocks):
        for g in range(4):
            out[g * NRHS : (g + 1) * NRHS, col * BLK : (col + 1) * BLK] = acc[b, :, g * BLK : (g + 1) * BLK]


def first_kernel(mask, test, panels, currents, out, *scratch):
    even = is_even()
    full = load_of(mask) == FULL
    fill_tests(scratch[1], 0, own_tests(test))
    clear(scratch[12], TPB)

    def wanted(n, b):
        return (full & (mirrored(even, n) == 1)) | (jnp.logical_not(full) & (n == b))

    engine(scratch, TPB, wanted, lambda n: fill(scratch, panels, currents, 0, n), lambda n: 0)
    write_out(out, scratch[12], range(TPB))


QUOTA = 7
HELP_STEPS = 6
OWN_STEPS = 8


def own_place(even, n):
    return jnp.where(n < 4, n, jnp.where(n == 4, jnp.where(even, -1, 4), jnp.where(even, n - 1, n - 8)))


def load_own(scratch, panels, currents, outer, mate, n):
    @pl.when(n < 4)
    def _():
        fill(scratch, panels, currents, 0, n)

    @pl.when(n == 4)
    def _():
        fill(scratch, outer, outer, CROW, 0)

    @pl.when(n > 4)
    def _():
        fill(scratch, mate, mate, CROW, n - 5)


def second_kernel(
    mask, test, panels, currents, outer, far, mate, load_far, part, out_near, out_far, out_own, todo, *scratch
):
    plan, scratch = scratch[-1], scratch[:-1]
    even = is_even()
    odd = jnp.logical_not(even)
    own_load, mate_load = load_of(mask), number(mate, XROW)
    near_load, far_load = number(outer, XROW + 64), number(far, XROW + 32)
    share_near, _ = shares(own_load, mate_load)
    _, share_far = shares(mate_load, own_load)
    give_near, give_far = shares(near_load, number(load_far, 0))
    full = own_load == FULL
    xt, acc = scratch[1], scratch[12]
    fill_tests(xt, 0, lambda b, row: outer[XROW + 16 * b + row : XROW + 16 * b + row + 2, :])
    fill_tests(
        xt,
        1,
        lambda b, row: far[
            XROW + 16 * (b // 2) + row : XROW + 16 * (b // 2) + row + 2, (b % 2) * BLK : (b % 2 + 1) * BLK
        ],
    )
    fill_tests(xt, 2, own_tests(test))
    clear(acc, 2 * TPB)
    for b in range(TPB):
        for g in range(4):
            acc[2 * TPB + b, :, g * BLK : (g + 1) * BLK] = part[g * NRHS : (g + 1) * NRHS, b * BLK : (b + 1) * BLK]

    def plan_help(i, used):
        n, b = lax.div(i, TPB), lax.rem(i, TPB)
        v_near, v_far = mirrored(odd, b), mirrored(even, b)
        of_own = (n < 3) & (v_near <= 2 - n)
        of_outer = (n == 3) & (v_near < share_near - 6)
        of_far = (n > 3) & ((n - 4) * TPB + v_far < share_far)
        wanted = ((near_load == FULL) & (of_own | of_outer)) | ((far_load == FULL) & of_far)
        plan[i] = wanted.astype(jnp.int32)
        return used + wanted.astype(jnp.int32)

    def plan_own(i, used):
        n, b = lax.div(i, TPB), lax.rem(i, TPB)
        rel = own_place(even, n)
        column = rel - b + REACH
        inside = (column >= 0) & (column < SPAN)
        sparse = inside & (mask[b, jnp.clip(column, 0, SPAN - 1)] > 0) & (rel != b)
        u, v = mirrored(even, rel), mirrored(even, b)
        given = (u == 1) | ((u == 0) & (v < give_near - 6))
        given = given | ((u == 3) & (v < give_far)) | ((u == 2) & (TPB + v < give_far))
        dense = inside & (u >= 0) & jnp.logical_not(given)
        wanted = (full & dense) | (jnp.logical_not(full) & sparse)
        now = wanted & (used < QUOTA)
        plan[HELP_STEPS * TPB + i] = now.astype(jnp.int32)
        todo[n, b] = (wanted & jnp.logical_not(now)).astype(jnp.int32)
        return used + now.astype(jnp.int32)

    used = lax.fori_loop(0, HELP_STEPS * TPB, plan_help, jnp.int32(0))
    lax.fori_loop(0, OWN_STEPS * TPB, plan_own, used)

    def load_source(n):
        @pl.when(n < 3)
        def _():
            fill(scratch, panels, currents, 0, mirrored(even, n))

        @pl.when(n == 3)
        def _():
            fill(scratch, outer, outer, CROW, 0)

        @pl.when((n > 3) & (n < HELP_STEPS))
        def _():
            fill(scratch, far, far, CROW, jnp.where(even, 5 - n, n - 4))

        @pl.when(n >= HELP_STEPS)
        def _():
            load_own(scratch, panels, currents, outer, mate, n - HELP_STEPS)

    engine(
        scratch,
        HELP_STEPS + OWN_STEPS,
        lambda n, b: plan[n * TPB + b] > 0,
        load_source,
        lambda n: jnp.where(n < 4, 0, jnp.where(n < HELP_STEPS, 1, 2)),
    )
    shift = jnp.where(even, 1, 0)
    write_out(out_near, acc, [b + shift for b in range(TPB - 1)])
    write_out(out_far, acc, range(TPB, 2 * TPB))
    write_out(out_own, acc, range(2 * TPB, 3 * TPB))


def rest_kernel(todo, test, panels, currents, outer, mate, part, after, out, *scratch):
    acc = scratch[12]
    fill_tests(scratch[1], 0, own_tests(test))
    for b in range(TPB):
        for g in range(4):
            acc[b, :, g * BLK : (g + 1) * BLK] = part[g * NRHS : (g + 1) * NRHS, b * BLK : (b + 1) * BLK]
    engine(
        scratch,
        OWN_STEPS,
        lambda n, b: todo[n, b] > 0,
        lambda n: load_own(scratch, panels, currents, outer, mate, n),
        lambda n: 0,
    )
    write_out(out, acc, range(TPB))


def scratch_for(sets):
    return [
        pltpu.VMEM((GROWS, BLK), F32),
        pltpu.VMEM((sets, 7, 8, BLK), F32),
        pltpu.VMEM(((NTERM + 16) * 16, BLK), F32),
        pltpu.VMEM((TROWS * 8, BLK), F32),
        pltpu.VMEM((KDIM, NOUT * 256), BF16),
        pltpu.VMEM((NCH * MROWS, KDIM), BF16),
        pltpu.VMEM((MROWS + 8, NOUT * 256), F32),
        pltpu.VMEM((MROWS + 8, NOUT * 256), F32),
        pltpu.VMEM((6, BLK, BLK), F32),
        pltpu.VMEM((2 * BLK, 4 * BLK), BF16),
        pltpu.VMEM((4 * BLK, 4 * BLK), BF16),
        pltpu.VMEM((4 * BLK, 4 * BLK), BF16),
        pltpu.VMEM((sets * TPB, BLK, 4 * BLK), F32),
        pltpu.VMEM((8 * 16, BLK), F32),
        pltpu.SMEM((TPB,), jnp.int32),
    ]


def call(kernel, outs, operands, sets=0, unread=0, tiles=1, table=False):
    vmem = pl.BlockSpec(memory_space=pltpu.VMEM)
    smem = pl.BlockSpec(memory_space=pltpu.SMEM)
    anywhere = pl.BlockSpec(memory_space=pl.ANY)
    plain = len(operands) - 1 - unread
    shapes = [jax.ShapeDtypeStruct(s, F32) for s in outs]
    specs = [vmem] * len(outs)
    scratch = scratch_for(sets) if sets else []
    if table:
        shapes.append(jax.ShapeDtypeStruct((OWN_STEPS, TPB), jnp.int32))
        specs.append(smem)
        scratch.append(pltpu.SMEM(((HELP_STEPS + OWN_STEPS) * TPB,), jnp.int32))
    return pl.pallas_call(
        kernel,
        out_shape=shapes,
        in_specs=[smem] + [vmem] * plain + [anywhere] * unread,
        out_specs=specs,
        scratch_shapes=scratch,
        compiler_params=pltpu.CompilerParams(vmem_limit_bytes=52 * 1024 * 1024),
        cost_estimate=pl.CostEstimate(flops=tiles * 5 * 10**9, bytes_accessed=4 * 10**6, transcendentals=0),
    )(*operands)


def body(panels, test_points, currents, near_mask):
    count = lax.axis_size("cluster") * lax.axis_size("narrow")
    axes = ("cluster", "narrow")
    swap = [(i, i ^ 1) for i in range(count)]
    across = [(i, (i - 1) % count if i % 2 == 0 else (i + 1) % count) for i in range(count)]
    away = [(i, (i - 2) % count if i % 2 == 0 else (i + 2) % count) for i in range(count)]
    back = [(target, source) for source, target in away]
    width = TPB * BLK
    wide = 4 * NRHS
    mate, outer, far, load = call(
        pack_kernel,
        [(MATE_ROWS, 3 * BLK), (OUTER_ROWS, BLK), (FAR_ROWS, 2 * BLK), (8, BLK)],
        [near_mask, panels, test_points, currents],
    )
    load_far = lax.ppermute(load, axes, back)
    outer = lax.ppermute(outer, axes, across)
    far = lax.ppermute(far, axes, away)
    mate = lax.ppermute(mate, axes, swap)
    (part,) = call(first_kernel, [(wide, width)], [near_mask, test_points, panels, currents], 1, tiles=4)
    to_near, to_far, part, todo = call(
        second_kernel,
        [(wide, width - BLK), (wide, width), (wide, width)],
        [near_mask, test_points, panels, currents, outer, far, mate, load_far, part],
        3,
        tiles=7,
        table=True,
    )
    from_near = lax.ppermute(to_near, axes, across)
    from_far = lax.ppermute(to_far, axes, back)
    (rest,) = call(
        rest_kernel,
        [(wide, width)],
        [todo, test_points, panels, currents, outer, mate, part, to_near],
        1,
        unread=1,
        tiles=8,
    )
    padded = jnp.where(
        lax.axis_index("narrow") == 0,
        jnp.pad(from_near, ((0, 0), (0, BLK))),
        jnp.pad(from_near, ((0, 0), (BLK, 0))),
    )
    return rest + from_far + padded


def solution(mesh):
    return jax.shard_map(
        body,
        mesh=mesh,
        in_specs=(
            P(None, ("cluster", "narrow")),
            P(None, ("cluster", "narrow")),
            P(None, ("cluster", "narrow")),
            P(("cluster", "narrow"), None),
        ),
        out_specs=P(None, ("cluster", "narrow")),
        check_vma=False,
    )
```

```python
import functools
import itertools
import math

import jax
import jax.numpy as jnp
from jax import lax
from jax.experimental import pallas as pl
from jax.experimental.pallas import tpu as pltpu
from jax.sharding import PartitionSpec as P

F32 = jnp.float32
BF16 = jnp.bfloat16
BLK = 128
QP = 14
REACH = 3
SPAN = 7
TPB = 4
GROWS = 98
NRHS = 128
SOFTEN = 0.04

Z_MAX = 14.0
DEGREE = 4
COS_HALF = (2.828426289053651, -0.35355064760758376, 0.007364148070439611, -6.107114702262049e-05, 2.4846120790492805e-07)
SIN_HALF = (1.4142135239177973, -0.05892543897495882, 0.0007364984722676873, -4.370137027858996e-06, 1.4053654408325383e-08)

TERMS = []
for _total in range(DEGREE + 1):
    for _j in range(_total + 1):
        _l = _total - _j
        for _a in itertools.product(range(_l + 1), repeat=3):
            if sum(_a) == _l:
                TERMS.append((_j, _a))
NTERM = 72
assert len(TERMS) <= NTERM
ONE = TERMS.index((0, (0, 0, 0)))
LIN = [TERMS.index((0, tuple(int(c == k) for c in range(3)))) for k in range(3)]
SQR = TERMS.index((1, (0, 0, 0)))
KDIM = 256
NOUT = 7
JC = 16
NCH = BLK // JC
MROWS = JC * QP


def powers_of(vec):
    one = None
    table = {(0, 0, 0): one}
    for total in range(1, DEGREE + 1):
        for a in itertools.product(range(total + 1), repeat=3):
            if sum(a) != total:
                continue
            axis = next(c for c in range(3) if a[c] > 0)
            prev = tuple(a[c] - (c == axis) for c in range(3))
            table[a] = vec[axis] if table[prev] is None else table[prev] * vec[axis]
    return table


def split2(value):
    high = value.astype(BF16).astype(F32)
    return high, value - high


def source_features(stage, fts, sf, centre, y):
    mono = powers_of(y)
    square = y[0] * y[0] + y[1] * y[1] + y[2] * y[2]
    sq = [None, square, square * square]
    sq.append(sq[2] * square)
    sq.append(sq[2] * sq[2])
    ones = jnp.ones_like(square)

    def put(row, value):
        fts[row * 16 : row * 16 + QP, :] = value

    for k, (j, a) in enumerate(TERMS):
        const = (-2.0) ** sum(a) / (math.prod(math.factorial(v) for v in a) * math.factorial(j))
        value = mono[a]
        if sq[j] is not None:
            value = sq[j] if value is None else value * sq[j]
        if value is None:
            value = ones
        put(k, value * const if const != 1.0 else value)
    base = NTERM
    s = [stage[(3 + c) * QP : (4 + c) * QP, :] for c in range(3)]
    d = stage[6 * QP : 7 * QP, :]
    for c in range(3):
        put(base + c, s[c])
    put(base + 3, d)
    for c in range(3):
        c1, c2 = (c + 1) % 3, (c + 2) % 3
        put(base + 4 + c, y[c1] * s[c2] - y[c2] * s[c1])
    extra = base + 8
    for half in range(2):
        for c in range(3):
            put(extra + 4 * half + c, y[c] * -2.0)
        put(extra + 4 * half + 3, square)
    rows = lax.broadcasted_iota(jnp.int32, (8, BLK), 0)
    for q in range(QP):
        main = fts[pl.ds(q, NTERM, stride=16), :]
        bil = fts[pl.ds(base * 16 + q, 8, stride=16), :]
        ext = fts[pl.ds(extra * 16 + q, 8, stride=16), :]
        mh, ml = split2(main)
        bh, bl = split2(bil)
        eh, rest = split2(ext)
        em, el = split2(rest)
        zrow = jnp.where(rows < 4, em, eh)
        zrow2 = jnp.where(rows < 4, el, jnp.where(rows == 4, 1.0, 0.0))
        full = jnp.concatenate([mh, mh, ml, bh, bh, bl, zrow, zrow2], 0)
        turned = full.astype(BF16).T
        for ch in range(NCH):
            sf[ch * MROWS + q * JC : ch * MROWS + (q + 1) * JC, :] = turned[ch * JC : (ch + 1) * JC, :]


def horner(coefs, m, w):
    der = [coefs[k] * math.factorial(k) / math.factorial(k - m) for k in range(m, len(coefs))]
    value = None
    for c in reversed(der):
        value = c if value is None else value * w + c
    return value


OFF_C, OFF_S, OFF_Z = 0, NTERM, 2 * NTERM
OFF_B = 3 * NTERM
OFF_E = OFF_B + 32
TROWS = OFF_E + 16


def test_features(xt, ftt, centre):
    x = [xt[c] - centre[c] for c in range(3)]
    t = [xt[3 + c] for c in range(3)]
    e = xt[6]
    w = x[0] * x[0] + x[1] * x[1] + x[2] * x[2] + SOFTEN
    mono = powers_of(x)

    def put(row, value):
        ftt[row * 8 : row * 8 + 8, :] = value

    for off, coefs in ((OFF_C, COS_HALF), (OFF_S, SIN_HALF)):
        der = [horner(coefs, m, w) for m in range(DEGREE + 1)]
        for k, (j, a) in enumerate(TERMS):
            level = der[j + sum(a)]
            value = level if mono[a] is None else mono[a] * level
            put(off + k, jnp.broadcast_to(value, w.shape))
    put(OFF_Z + ONE, w)
    put(OFF_Z + SQR, jnp.ones_like(w))
    for c in range(3):
        put(OFF_Z + LIN[c], x[c])
    charge = e * -0.25
    for c in range(3):
        put(OFF_B + c, t[c])
        put(OFF_B + 8 + c, t[c] * -2.0)
        put(OFF_B + 16 + c, t[c] * 1.5)
        c1, c2 = (c + 1) % 3, (c + 2) % 3
        put(OFF_B + 24 + c, (t[c1] * x[c2] - t[c2] * x[c1]) * -0.25)
        put(OFF_B + 28 + c, t[c] * 0.25)
    put(OFF_B + 3, charge)
    put(OFF_B + 11, charge)
    for half in range(2):
        for c in range(3):
            put(OFF_E + 4 * half + c, x[c])
        put(OFF_E + 4 * half + 3, jnp.ones_like(w))
    for c in range(4):
        put(OFF_E + 8 + c, x[c] if c < 3 else jnp.ones_like(w))
    put(OFF_E + 12, w)


def test_matrix(ftt, tf, b):
    rows = lax.broadcasted_iota(jnp.int32, (8, BLK), 0)
    zero8 = jnp.zeros((8, BLK), F32)
    for a in range(2):
        ba = 2 * b + a

        def take(off, n):
            return ftt[pl.ds(off * 8 + ba, n, stride=8), :]

        for out, off in ((0, OFF_Z), (1, OFF_C), (2, OFF_S)):
            high, low = split2(take(off, NTERM))
            lanes = slice(out * 256 + a * BLK, out * 256 + (a + 1) * BLK)
            tf[0:224, lanes] = jnp.concatenate([high, low, high, zero8], 0).astype(BF16)
        eh, rest = split2(take(OFF_E, 8))
        em, el = split2(rest)
        fh, rest2 = split2(take(OFF_E + 8, 8))
        fm, fl = split2(rest2)
        first = jnp.where(rows < 4, em, el)
        second = jnp.where(rows < 4, fh, jnp.where(rows == 4, fl, 0.0))
        tf[240:256, a * BLK : (a + 1) * BLK] = jnp.concatenate([first, second], 0).astype(BF16)
        for m in range(4):
            high, low = split2(take(OFF_B + 8 * m, 8))
            out = 3 + m
            lanes = slice(out * 256 + a * BLK, out * 256 + (a + 1) * BLK)
            tf[208:240, lanes] = jnp.concatenate([zero8, high, low, high], 0).astype(BF16)


EXP_RATE = -3.0 / math.log(2.0)


def pair_terms(z, cos_h, sin_h, k1, k2, k6, kk):
    inv = lax.rsqrt(z)
    dist = z * inv
    s0 = sin_h * dist
    c = 4.0 - s0 * s0
    s = s0 * cos_h
    c2 = c * c - 8.0
    s2 = c * s
    decay = jnp.exp2(dist * EXP_RATE)
    p = decay * c
    q = decay * s
    half = inv * 0.5
    c2r = c2 * half
    s2r = s2 * half
    pr = p * inv
    qr = q * inv
    weight = kk * (inv * inv)
    l1r = k1 * c2r
    l1i = k1 * s2r
    l2r = k2 * pr - k6 * qr
    l2i = k2 * qr + k6 * pr
    kr = weight * (((c2r + pr) + (s2 + 3.0 * p)) + q)
    ki = weight * (((s2r + qr) + (3.0 * q - c2)) - p)
    return l1r, l1i, l2r, l2i, kr, ki


AHEAD = 6


def fast_tile(ftt, tf, sf, bufs, ops, b, flag):
    test_matrix(ftt, tf, b)
    spare = pl.multiple_of(MROWS - 8 + 8 * flag, 8)

    def piece(chunk, buf, o):
        rows = pl.ds(pl.multiple_of(chunk * MROWS, 16), MROWS)
        lanes = slice(o * 256, (o + 1) * 256)
        buf[0:MROWS, lanes] = jnp.dot(sf[rows, :], tf[:, lanes], preferred_element_type=F32)

    def phase(chunk, buf, next_chunk, next_buf):
        work = [(g, q, a) for g in range(JC // 8) for q in range(QP) for a in range(2)]
        per = -(-len(work) // NOUT)
        acc, history = None, []
        for o in range(NOUT):
            piece(next_chunk, next_buf, o)
            for g, q, a in work[o * per : (o + 1) * per]:
                if q == 0 and a == 0:
                    acc = None
                row = q * JC + g * 8
                if len(history) >= AHEAD:
                    buf[pl.ds(spare, 8), 0:BLK] = history[-AHEAD]
                vals = [buf[row : row + 8, k * 256 + a * BLK : k * 256 + (a + 1) * BLK] for k in range(NOUT)]
                terms = pair_terms(*vals)
                acc = list(terms) if acc is None else [u + v for u, v in zip(acc, terms)]
                history.append(acc[5])
                if q == QP - 1 and a == 1:
                    start = pl.multiple_of(chunk * JC + g * 8, 8)
                    for m in range(6):
                        ops[m, pl.ds(start, 8), :] = acc[m]

    for o in range(NOUT):
        piece(0, bufs[0], o)

    def step(n, carry):
        phase(2 * n, bufs[0], 2 * n + 1, bufs[1])
        phase(2 * n + 1, bufs[1], lax.rem(2 * n + 2, NCH), bufs[0])
        return carry

    lax.fori_loop(0, NCH // 2, step, 0)


def direct_tile(stage, raw, xt, ops, b):
    for c in range(7):
        raw[c * 16 : c * 16 + QP, :] = stage[c * QP : (c + 1) * QP, :]
    raw[7 * 16 : 8 * 16, :] = jnp.zeros((16, BLK), F32)
    for m in range(6):
        ops[m] = jnp.zeros((BLK, BLK), F32)

    def point(q, carry):
        rows8 = raw[pl.ds(q, 8, stride=16), :]
        turned = jnp.concatenate([rows8, jnp.zeros((BLK - 8, BLK), F32)], 0).T
        src = [turned[:, c : c + 1] for c in range(7)]

        def centroid(a, carry2):
            tst = [xt[c, pl.ds(2 * b + a, 1), :] for c in range(7)]
            dl = [tst[c] - src[c] for c in range(3)]
            dist = jnp.sqrt(dl[0] * dl[0] + dl[1] * dl[1] + dl[2] * dl[2] + SOFTEN)
            dotted = tst[3] * src[3] + tst[4] * src[4] + tst[5] * src[5]
            charge = tst[6] * src[6]
            crossed = (
                dl[0] * (src[4] * tst[5] - src[5] * tst[4])
                + dl[1] * (src[5] * tst[3] - src[3] * tst[5])
                + dl[2] * (src[3] * tst[4] - src[4] * tst[3])
            )
            scaled = crossed / (dist * dist)
            kr = ki = None
            for m, (wr, wi) in enumerate(((2.0, 0.0), (1.0, 3.0))):
                decay = jnp.exp(-wi * dist) / dist
                gr = decay * jnp.cos(wr * dist)
                gi = decay * jnp.sin(wr * dist)
                cr = (wr * wr - wi * wi) * dotted - charge
                ci = 2.0 * wr * wi * dotted
                ops[2 * m] += cr * gr - ci * gi
                ops[2 * m + 1] += cr * gi + ci * gr
                fr = -wi * dist - 1.0
                fi = wr * dist
                ops[4] += scaled * (fr * gr - fi * gi)
                ops[5] += scaled * (fr * gi + fi * gr)
            return carry2

        return lax.fori_loop(0, 2, centroid, carry)

    lax.fori_loop(0, QP, point, 0)


def apply_operators(ops, xs, wh, wl, acc, b):
    def put(ref, value, places):
        neg = -value
        for row, col, sign in places:
            ref[row * BLK : (row + 1) * BLK, col * BLK : (col + 1) * BLK] = value if sign > 0 else neg

    def both(value, places):
        high = value.astype(BF16)
        low = (value - high.astype(F32)).astype(BF16)
        put(wh, high, places)
        put(wl, low, places)

    l1r, l1i, l2r, l2i = (ops[m] for m in range(4))
    both(l1r + l2r, ((0, 0, 1), (1, 1, 1)))
    both(l1i + l2i, ((0, 1, 1), (1, 0, -1)))
    both(l1r + 0.5 * l2r, ((2, 2, 1), (3, 3, 1)))
    both(l1i + 0.5 * l2i, ((2, 3, 1), (3, 2, -1)))
    both(ops[4], ((0, 2, 1), (1, 3, 1), (2, 0, -1), (3, 1, -1)))
    both(ops[5], ((0, 3, 1), (1, 2, -1), (2, 1, -1), (3, 0, 1)))
    first = jnp.dot(xs[...], wh[...], preferred_element_type=F32)
    second = jnp.dot(xs[0:BLK, :], wl[...], preferred_element_type=F32)
    acc[b] += first[0:BLK] + first[BLK:] + second


CROW = 104
XROW = CROW + 4 * NRHS
OUTER_ROWS = XROW + 64 + 8
FAR_ROWS = XROW + 32 + 8
MATE_ROWS = XROW + 8
FULL = TPB * SPAN


def is_even():
    return lax.axis_index("narrow") == 0


def mirrored(even, block):
    return jnp.where(even, block, TPB - 1 - block)


def load_of(mask):
    total = mask[0, 0]
    for b in range(TPB):
        for c in range(SPAN):
            if b or c:
                total = total + mask[b, c]
    return total


def number(ref, row):
    return jnp.max(ref[row : row + 8, 0:BLK]).astype(jnp.int32)


def shares(load_near, load_far):
    goal = lax.div(FULL + load_near + load_far + 1, 3)
    return jnp.clip(goal - load_near, 6, 9), jnp.clip(goal - load_far, 0, 8)


PACK_COPIES = 5


def pack_kernel(mask, panels_at, test_at, currents, mate, outer, far, load, panels, test, sems):
    even = is_even()
    places = (
        (outer, 1, jnp.where(even, 0, 3 * BLK)),
        (far, 2, jnp.where(even, 2 * BLK, 0)),
        (mate, 3, jnp.where(even, BLK, 0)),
    )
    lanes = [pl.ds(pl.multiple_of(begin, BLK), count * BLK) for _, count, begin in places]
    copies = [pltpu.make_async_copy(panels_at, panels, sems.at[0]), pltpu.make_async_copy(test_at, test, sems.at[1])]
    for k in range(3):
        copies.append(pltpu.make_async_copy(currents.at[:, lanes[k]], places[k][0].at[CROW:XROW, :], sems.at[2 + k]))
    for each in copies:
        each.start()
    value = load_of(mask).astype(F32)
    outer[XROW + 64 : XROW + 72, :] = jnp.full((8, BLK), value, F32)
    far[XROW + 32 : XROW + 40, :] = jnp.full((8, 2 * BLK), value, F32)
    mate[XROW : XROW + 8, :] = jnp.full((8, 3 * BLK), value, F32)
    load[...] = jnp.full((8, BLK), value, F32)
    copies[0].wait()
    copies[1].wait()
    for k in range(3):
        places[k][0][0:GROWS, :] = panels[:, lanes[k]]
    for b in range(TPB):
        points = test[:, b * BLK : (b + 1) * BLK]
        outer[XROW + 16 * b : XROW + 16 * b + 14, :] = points
        row = XROW + 16 * (b // 2)
        far[row : row + 14, (b % 2) * BLK : (b % 2 + 1) * BLK] = points
    for each in copies[2:]:
        each.wait()


def engine(scratch, steps, wanted, load_source, accset):
    stage, xt, fts, ftt, tf, sf, buf0, buf1, ops, xs, wh, wl, acc, raw, flags = scratch

    def source(n, carry):
        any_wanted = wanted(n, 0)
        for b in range(1, TPB):
            any_wanted = any_wanted | wanted(n, b)

        @pl.when(any_wanted)
        def _():
            load_source(n)
            points = xt.at[accset(n)]
            place = [stage[c * QP : (c + 1) * QP, :] for c in range(3)]
            low = [jnp.min(jnp.min(v, 0, keepdims=True), 1, keepdims=True) for v in place]
            high = [jnp.max(jnp.max(v, 0, keepdims=True), 1, keepdims=True) for v in place]
            centre = [(u + v) * 0.5 for u, v in zip(low, high)]
            bound = jnp.full((8, BLK), SOFTEN, F32)
            for c in range(3):
                far = jnp.maximum(jnp.abs(points[c] - low[c]), jnp.abs(points[c] - high[c]))
                bound = bound + far * far
            for b in range(TPB):
                flags[b] = (jnp.max(bound[2 * b : 2 * b + 2]) <= Z_MAX).astype(jnp.int32)
            source_features(stage, fts, sf, centre, [place[c] - centre[c] for c in range(3)])
            test_features(points, ftt, centre)

            def tile(b, carry2):
                @pl.when(wanted(n, b))
                def _():
                    @pl.when(flags[b] > 0)
                    def _():
                        fast_tile(ftt, tf, sf, (buf0, buf1), ops, b, flags[b])

                    @pl.when(flags[b] == 0)
                    def _():
                        direct_tile(stage, raw, points, ops, b)

                    apply_operators(ops, xs, wh, wl, acc, TPB * accset(n) + b)

                return carry2

            lax.fori_loop(0, TPB, tile, 0)

        return carry

    tf[...] = jnp.zeros_like(tf)
    ftt[...] = jnp.zeros_like(ftt)
    fts[...] = jnp.zeros_like(fts)
    lax.fori_loop(0, steps, source, 0)


def fill(scratch, pan, cur, row, slot):
    stage, xs = scratch[0], scratch[9]
    lanes = pl.ds(pl.multiple_of(slot * BLK, BLK), BLK)
    stage[...] = pan[0:GROWS, lanes]
    for g in range(4):
        value = cur[row + g * NRHS : row + (g + 1) * NRHS, lanes]
        high = value.astype(BF16)
        xs[0:BLK, g * BLK : (g + 1) * BLK] = high
        xs[BLK : 2 * BLK, g * BLK : (g + 1) * BLK] = (value - high.astype(F32)).astype(BF16)


def fill_tests(xt, which, blocks):
    for c in range(7):
        for b in range(TPB):
            xt[which, c, 2 * b : 2 * b + 2, :] = blocks(b, 2 * c)


def own_tests(test):
    return lambda b, row: test[row : row + 2, b * BLK : (b + 1) * BLK]


def clear(acc, count):
    for b in range(count):
        acc[b] = jnp.zeros((BLK, 4 * BLK), F32)


def write_out(out, acc, blocks):
    for col, b in enumerate(blocks):
        for g in range(4):
            out[g * NRHS : (g + 1) * NRHS, col * BLK : (col + 1) * BLK] = acc[b, :, g * BLK : (g + 1) * BLK]


def first_kernel(mask, test, panels, currents, out, *scratch):
    even = is_even()
    full = load_of(mask) == FULL
    fill_tests(scratch[1], 0, own_tests(test))
    clear(scratch[12], TPB)

    def wanted(n, b):
        return (full & (mirrored(even, n) == 1)) | (jnp.logical_not(full) & (n == b))

    engine(scratch, TPB, wanted, lambda n: fill(scratch, panels, currents, 0, n), lambda n: 0)
    write_out(out, scratch[12], range(TPB))


QUOTA = 7
HELP_STEPS = 6
OWN_STEPS = 8


def own_place(even, n):
    return jnp.where(n < 4, n, jnp.where(n == 4, jnp.where(even, -1, 4), jnp.where(even, n - 1, n - 8)))


def load_own(scratch, panels, currents, outer, mate, n):
    @pl.when(n < 4)
    def _():
        fill(scratch, panels, currents, 0, n)

    @pl.when(n == 4)
    def _():
        fill(scratch, outer, outer, CROW, 0)

    @pl.when(n > 4)
    def _():
        fill(scratch, mate, mate, CROW, n - 5)


def second_kernel(
    mask, test, panels, currents, outer, far, mate, load_far, part, out_near, out_far, out_own, todo, *scratch
):
    plan, scratch = scratch[-1], scratch[:-1]
    even = is_even()
    odd = jnp.logical_not(even)
    own_load, mate_load = load_of(mask), number(mate, XROW)
    near_load, far_load = number(outer, XROW + 64), number(far, XROW + 32)
    share_near, _ = shares(own_load, mate_load)
    _, share_far = shares(mate_load, own_load)
    give_near, give_far = shares(near_load, number(load_far, 0))
    full = own_load == FULL
    xt, acc = scratch[1], scratch[12]
    fill_tests(xt, 0, lambda b, row: outer[XROW + 16 * b + row : XROW + 16 * b + row + 2, :])
    fill_tests(
        xt,
        1,
        lambda b, row: far[
            XROW + 16 * (b // 2) + row : XROW + 16 * (b // 2) + row + 2, (b % 2) * BLK : (b % 2 + 1) * BLK
        ],
    )
    fill_tests(xt, 2, own_tests(test))
    clear(acc, 2 * TPB)
    for b in range(TPB):
        for g in range(4):
            acc[2 * TPB + b, :, g * BLK : (g + 1) * BLK] = part[g * NRHS : (g + 1) * NRHS, b * BLK : (b + 1) * BLK]

    def plan_help(i, used):
        n, b = lax.div(i, TPB), lax.rem(i, TPB)
        v_near, v_far = mirrored(odd, b), mirrored(even, b)
        of_own = (n < 3) & (v_near <= 2 - n)
        of_outer = (n == 3) & (v_near < share_near - 6)
        of_far = (n > 3) & ((n - 4) * TPB + v_far < share_far)
        wanted = ((near_load == FULL) & (of_own | of_outer)) | ((far_load == FULL) & of_far)
        plan[i] = wanted.astype(jnp.int32)
        return used + wanted.astype(jnp.int32)

    def plan_own(i, used):
        n, b = lax.div(i, TPB), lax.rem(i, TPB)
        rel = own_place(even, n)
        column = rel - b + REACH
        inside = (column >= 0) & (column < SPAN)
        sparse = inside & (mask[b, jnp.clip(column, 0, SPAN - 1)] > 0) & (rel != b)
        u, v = mirrored(even, rel), mirrored(even, b)
        given = (u == 1) | ((u == 0) & (v < give_near - 6))
        given = given | ((u == 3) & (v < give_far)) | ((u == 2) & (TPB + v < give_far))
        dense = inside & (u >= 0) & jnp.logical_not(given)
        wanted = (full & dense) | (jnp.logical_not(full) & sparse)
        now = wanted & (used < QUOTA)
        plan[HELP_STEPS * TPB + i] = now.astype(jnp.int32)
        todo[n, b] = (wanted & jnp.logical_not(now)).astype(jnp.int32)
        return used + now.astype(jnp.int32)

    used = lax.fori_loop(0, HELP_STEPS * TPB, plan_help, jnp.int32(0))
    lax.fori_loop(0, OWN_STEPS * TPB, plan_own, used)

    def load_source(n):
        @pl.when(n < 3)
        def _():
            fill(scratch, panels, currents, 0, mirrored(even, n))

        @pl.when(n == 3)
        def _():
            fill(scratch, outer, outer, CROW, 0)

        @pl.when((n > 3) & (n < HELP_STEPS))
        def _():
            fill(scratch, far, far, CROW, jnp.where(even, 5 - n, n - 4))

        @pl.when(n >= HELP_STEPS)
        def _():
            load_own(scratch, panels, currents, outer, mate, n - HELP_STEPS)

    engine(
        scratch,
        HELP_STEPS + OWN_STEPS,
        lambda n, b: plan[n * TPB + b] > 0,
        load_source,
        lambda n: jnp.where(n < 4, 0, jnp.where(n < HELP_STEPS, 1, 2)),
    )
    shift = jnp.where(even, 1, 0)
    write_out(out_near, acc, [b + shift for b in range(TPB - 1)])
    write_out(out_far, acc, range(TPB, 2 * TPB))
    write_out(out_own, acc, range(2 * TPB, 3 * TPB))


def rest_kernel(todo, test, panels, currents, outer, mate, part, after, out, *scratch):
    acc = scratch[12]
    fill_tests(scratch[1], 0, own_tests(test))
    for b in range(TPB):
        for g in range(4):
            acc[b, :, g * BLK : (g + 1) * BLK] = part[g * NRHS : (g + 1) * NRHS, b * BLK : (b + 1) * BLK]
    engine(
        scratch,
        OWN_STEPS,
        lambda n, b: todo[n, b] > 0,
        lambda n: load_own(scratch, panels, currents, outer, mate, n),
        lambda n: 0,
    )
    write_out(out, acc, range(TPB))


def scratch_for(sets):
    return [
        pltpu.VMEM((GROWS, BLK), F32),
        pltpu.VMEM((sets, 7, 8, BLK), F32),
        pltpu.VMEM(((NTERM + 16) * 16, BLK), F32),
        pltpu.VMEM((TROWS * 8, BLK), F32),
        pltpu.VMEM((KDIM, NOUT * 256), BF16),
        pltpu.VMEM((NCH * MROWS, KDIM), BF16),
        pltpu.VMEM((MROWS + 8, NOUT * 256), F32),
        pltpu.VMEM((MROWS + 8, NOUT * 256), F32),
        pltpu.VMEM((6, BLK, BLK), F32),
        pltpu.VMEM((2 * BLK, 4 * BLK), BF16),
        pltpu.VMEM((4 * BLK, 4 * BLK), BF16),
        pltpu.VMEM((4 * BLK, 4 * BLK), BF16),
        pltpu.VMEM((sets * TPB, BLK, 4 * BLK), F32),
        pltpu.VMEM((8 * 16, BLK), F32),
        pltpu.SMEM((TPB,), jnp.int32),
    ]


def call(kernel, outs, operands, sets=0, unread=0, tiles=1, table=False, copies=0):
    vmem = pl.BlockSpec(memory_space=pltpu.VMEM)
    smem = pl.BlockSpec(memory_space=pltpu.SMEM)
    anywhere = pl.BlockSpec(memory_space=pl.ANY)
    plain = len(operands) - 1 - unread
    shapes = [jax.ShapeDtypeStruct(s, F32) for s in outs]
    specs = [vmem] * len(outs)
    scratch = scratch_for(sets) if sets else []
    if copies:
        scratch += [
            pltpu.VMEM((GROWS, TPB * BLK), F32),
            pltpu.VMEM((14, TPB * BLK), F32),
            pltpu.SemaphoreType.DMA((copies,)),
        ]
    if table:
        shapes.append(jax.ShapeDtypeStruct((OWN_STEPS, TPB), jnp.int32))
        specs.append(smem)
        scratch.append(pltpu.SMEM(((HELP_STEPS + OWN_STEPS) * TPB,), jnp.int32))
    return pl.pallas_call(
        kernel,
        out_shape=shapes,
        in_specs=[smem] + [vmem] * plain + [anywhere] * unread,
        out_specs=specs,
        scratch_shapes=scratch,
        compiler_params=pltpu.CompilerParams(vmem_limit_bytes=(60 if copies else 26) * 1024 * 1024),
        cost_estimate=pl.CostEstimate(flops=tiles * 5 * 10**9, bytes_accessed=4 * 10**6, transcendentals=0),
    )(*operands)


def body(panels, test_points, currents, near_mask):
    count = lax.axis_size("cluster") * lax.axis_size("narrow")
    axes = ("cluster", "narrow")
    swap = [(i, i ^ 1) for i in range(count)]
    across = [(i, (i - 1) % count if i % 2 == 0 else (i + 1) % count) for i in range(count)]
    away = [(i, (i - 2) % count if i % 2 == 0 else (i + 2) % count) for i in range(count)]
    back = [(target, source) for source, target in away]
    width = TPB * BLK
    wide = 4 * NRHS
    mate, outer, far, load = call(
        pack_kernel,
        [(MATE_ROWS, 3 * BLK), (OUTER_ROWS, BLK), (FAR_ROWS, 2 * BLK), (8, BLK)],
        [near_mask, panels, test_points, currents],
        unread=3,
        copies=PACK_COPIES,
    )
    load_far = lax.ppermute(load, axes, back)
    outer = lax.ppermute(outer, axes, across)
    far = lax.ppermute(far, axes, away)
    mate = lax.ppermute(mate, axes, swap)
    (part,) = call(first_kernel, [(wide, width)], [near_mask, test_points, panels, currents], 1, tiles=4)
    to_near, to_far, part, todo = call(
        second_kernel,
        [(wide, width - BLK), (wide, width), (wide, width)],
        [near_mask, test_points, panels, currents, outer, far, mate, load_far, part],
        3,
        tiles=7,
        table=True,
    )
    from_near = lax.ppermute(to_near, axes, across)
    from_far = lax.ppermute(to_far, axes, back)
    (rest,) = call(
        rest_kernel,
        [(wide, width)],
        [todo, test_points, panels, currents, outer, mate, part, to_near],
        1,
        unread=1,
        tiles=8,
    )
    padded = jnp.where(
        lax.axis_index("narrow") == 0,
        jnp.pad(from_near, ((0, 0), (0, BLK))),
        jnp.pad(from_near, ((0, 0), (BLK, 0))),
    )
    return rest + from_far + padded


def solution(mesh):
    return jax.shard_map(
        body,
        mesh=mesh,
        in_specs=(
            P(None, ("cluster", "narrow")),
            P(None, ("cluster", "narrow")),
            P(None, ("cluster", "narrow")),
            P(("cluster", "narrow"), None),
        ),
        out_specs=P(None, ("cluster", "narrow")),
        check_vma=False,
    )
```

```python
import functools
import itertools
import math

import jax
import jax.numpy as jnp
from jax import lax
from jax.experimental import pallas as pl
from jax.experimental.pallas import tpu as pltpu
from jax.sharding import PartitionSpec as P

F32 = jnp.float32
BF16 = jnp.bfloat16
BLK = 128
QP = 14
REACH = 3
SPAN = 7
TPB = 4
GROWS = 98
NRHS = 128
SOFTEN = 0.04

Z_MAX = 14.0
DEGREE = 4
COS_HALF = (2.828426289053651, -0.35355064760758376, 0.007364148070439611, -6.107114702262049e-05, 2.4846120790492805e-07)
SIN_HALF = (1.4142135239177973, -0.05892543897495882, 0.0007364984722676873, -4.370137027858996e-06, 1.4053654408325383e-08)

TERMS = []
for _total in range(DEGREE + 1):
    for _j in range(_total + 1):
        _l = _total - _j
        for _a in itertools.product(range(_l + 1), repeat=3):
            if sum(_a) == _l:
                TERMS.append((_j, _a))
NTERM = 72
assert len(TERMS) <= NTERM
ONE = TERMS.index((0, (0, 0, 0)))
LIN = [TERMS.index((0, tuple(int(c == k) for c in range(3)))) for k in range(3)]
SQR = TERMS.index((1, (0, 0, 0)))
KDIM = 256
NOUT = 7
JC = 16
NCH = BLK // JC
MROWS = JC * QP


def powers_of(vec):
    one = None
    table = {(0, 0, 0): one}
    for total in range(1, DEGREE + 1):
        for a in itertools.product(range(total + 1), repeat=3):
            if sum(a) != total:
                continue
            axis = next(c for c in range(3) if a[c] > 0)
            prev = tuple(a[c] - (c == axis) for c in range(3))
            table[a] = vec[axis] if table[prev] is None else table[prev] * vec[axis]
    return table


def split2(value):
    high = value.astype(BF16).astype(F32)
    return high, value - high


def source_features(stage, fts, sf, centre, y):
    mono = powers_of(y)
    square = y[0] * y[0] + y[1] * y[1] + y[2] * y[2]
    sq = [None, square, square * square]
    sq.append(sq[2] * square)
    sq.append(sq[2] * sq[2])
    ones = jnp.ones_like(square)

    def put(row, value):
        fts[row * 16 : row * 16 + QP, :] = value

    for k, (j, a) in enumerate(TERMS):
        const = (-2.0) ** sum(a) / (math.prod(math.factorial(v) for v in a) * math.factorial(j))
        value = mono[a]
        if sq[j] is not None:
            value = sq[j] if value is None else value * sq[j]
        if value is None:
            value = ones
        put(k, value * const if const != 1.0 else value)
    base = NTERM
    s = [stage[(3 + c) * QP : (4 + c) * QP, :] for c in range(3)]
    d = stage[6 * QP : 7 * QP, :]
    for c in range(3):
        put(base + c, s[c])
    put(base + 3, d)
    for c in range(3):
        c1, c2 = (c + 1) % 3, (c + 2) % 3
        put(base + 4 + c, y[c1] * s[c2] - y[c2] * s[c1])
    extra = base + 8
    for half in range(2):
        for c in range(3):
            put(extra + 4 * half + c, y[c] * -2.0)
        put(extra + 4 * half + 3, square)
    rows = lax.broadcasted_iota(jnp.int32, (8, BLK), 0)
    for q in range(QP):
        main = fts[pl.ds(q, NTERM, stride=16), :]
        bil = fts[pl.ds(base * 16 + q, 8, stride=16), :]
        ext = fts[pl.ds(extra * 16 + q, 8, stride=16), :]
        mh, ml = split2(main)
        bh, bl = split2(bil)
        eh, rest = split2(ext)
        em, el = split2(rest)
        zrow = jnp.where(rows < 4, em, eh)
        zrow2 = jnp.where(rows < 4, el, jnp.where(rows == 4, 1.0, 0.0))
        full = jnp.concatenate([mh, mh, ml, bh, bh, bl, zrow, zrow2], 0)
        turned = full.astype(BF16).T
        for ch in range(NCH):
            sf[ch * MROWS + q * JC : ch * MROWS + (q + 1) * JC, :] = turned[ch * JC : (ch + 1) * JC, :]


def horner(coefs, m, w):
    der = [coefs[k] * math.factorial(k) / math.factorial(k - m) for k in range(m, len(coefs))]
    value = None
    for c in reversed(der):
        value = c if value is None else value * w + c
    return value


OFF_C, OFF_S, OFF_Z = 0, NTERM, 2 * NTERM
OFF_B = 3 * NTERM
OFF_E = OFF_B + 32
TROWS = OFF_E + 16


def test_features(xt, ftt, centre):
    x = [xt[c] - centre[c] for c in range(3)]
    t = [xt[3 + c] for c in range(3)]
    e = xt[6]
    w = x[0] * x[0] + x[1] * x[1] + x[2] * x[2] + SOFTEN
    mono = powers_of(x)

    def put(row, value):
        ftt[row * 8 : row * 8 + 8, :] = value

    for off, coefs in ((OFF_C, COS_HALF), (OFF_S, SIN_HALF)):
        der = [horner(coefs, m, w) for m in range(DEGREE + 1)]
        for k, (j, a) in enumerate(TERMS):
            level = der[j + sum(a)]
            value = level if mono[a] is None else mono[a] * level
            put(off + k, jnp.broadcast_to(value, w.shape))
    put(OFF_Z + ONE, w)
    put(OFF_Z + SQR, jnp.ones_like(w))
    for c in range(3):
        put(OFF_Z + LIN[c], x[c])
    charge = e * -0.25
    for c in range(3):
        put(OFF_B + c, t[c])
        put(OFF_B + 8 + c, t[c] * -2.0)
        put(OFF_B + 16 + c, t[c] * 1.5)
        c1, c2 = (c + 1) % 3, (c + 2) % 3
        put(OFF_B + 24 + c, (t[c1] * x[c2] - t[c2] * x[c1]) * -0.25)
        put(OFF_B + 28 + c, t[c] * 0.25)
    put(OFF_B + 3, charge)
    put(OFF_B + 11, charge)
    for half in range(2):
        for c in range(3):
            put(OFF_E + 4 * half + c, x[c])
        put(OFF_E + 4 * half + 3, jnp.ones_like(w))
    for c in range(4):
        put(OFF_E + 8 + c, x[c] if c < 3 else jnp.ones_like(w))
    put(OFF_E + 12, w)


def test_matrix(ftt, tf, b):
    rows = lax.broadcasted_iota(jnp.int32, (8, BLK), 0)
    zero8 = jnp.zeros((8, BLK), F32)
    for a in range(2):
        ba = 2 * b + a

        def take(off, n):
            return ftt[pl.ds(off * 8 + ba, n, stride=8), :]

        for out, off in ((0, OFF_Z), (1, OFF_C), (2, OFF_S)):
            high, low = split2(take(off, NTERM))
            lanes = slice(out * 256 + a * BLK, out * 256 + (a + 1) * BLK)
            tf[0:224, lanes] = jnp.concatenate([high, low, high, zero8], 0).astype(BF16)
        eh, rest = split2(take(OFF_E, 8))
        em, el = split2(rest)
        fh, rest2 = split2(take(OFF_E + 8, 8))
        fm, fl = split2(rest2)
        first = jnp.where(rows < 4, em, el)
        second = jnp.where(rows < 4, fh, jnp.where(rows == 4, fl, 0.0))
        tf[240:256, a * BLK : (a + 1) * BLK] = jnp.concatenate([first, second], 0).astype(BF16)
        for m in range(4):
            high, low = split2(take(OFF_B + 8 * m, 8))
            out = 3 + m
            lanes = slice(out * 256 + a * BLK, out * 256 + (a + 1) * BLK)
            tf[208:240, lanes] = jnp.concatenate([zero8, high, low, high], 0).astype(BF16)


EXP_RATE = -3.0 / math.log(2.0)


def pair_terms(z, cos_h, sin_h, k1, k2, k6, kk):
    inv = lax.rsqrt(z)
    dist = z * inv
    s0 = sin_h * dist
    c = 4.0 - s0 * s0
    s = s0 * cos_h
    c2 = c * c - 8.0
    s2 = c * s
    decay = jnp.exp2(dist * EXP_RATE)
    p = decay * c
    q = decay * s
    half = inv * 0.5
    c2r = c2 * half
    s2r = s2 * half
    pr = p * inv
    qr = q * inv
    weight = kk * (inv * inv)
    l1r = k1 * c2r
    l1i = k1 * s2r
    l2r = k2 * pr - k6 * qr
    l2i = k2 * qr + k6 * pr
    kr = weight * (((c2r + pr) + (s2 + 3.0 * p)) + q)
    ki = weight * (((s2r + qr) + (3.0 * q - c2)) - p)
    return l1r, l1i, l2r, l2i, kr, ki


AHEAD = 6


def fast_tile(ftt, tf, sf, bufs, ops, b, flag):
    test_matrix(ftt, tf, b)
    spare = pl.multiple_of(MROWS - 8 + 8 * flag, 8)

    def piece(chunk, buf, o):
        rows = pl.ds(pl.multiple_of(chunk * MROWS, 16), MROWS)
        lanes = slice(o * 256, (o + 1) * 256)
        buf[0:MROWS, lanes] = jnp.dot(sf[rows, :], tf[:, lanes], preferred_element_type=F32)

    def phase(chunk, buf, next_chunk, next_buf):
        work = [(g, q, a) for g in range(JC // 8) for q in range(QP) for a in range(2)]
        per = -(-len(work) // NOUT)
        acc, history = None, []
        for o in range(NOUT):
            piece(next_chunk, next_buf, o)
            for g, q, a in work[o * per : (o + 1) * per]:
                if q == 0 and a == 0:
                    acc = None
                row = q * JC + g * 8
                if len(history) >= AHEAD:
                    buf[pl.ds(spare, 8), 0:BLK] = history[-AHEAD]
                vals = [buf[row : row + 8, k * 256 + a * BLK : k * 256 + (a + 1) * BLK] for k in range(NOUT)]
                terms = pair_terms(*vals)
                acc = list(terms) if acc is None else [u + v for u, v in zip(acc, terms)]
                history.append(acc[5])
                if q == QP - 1 and a == 1:
                    start = pl.multiple_of(chunk * JC + g * 8, 8)
                    for m in range(6):
                        ops[m, pl.ds(start, 8), :] = acc[m]

    for o in range(NOUT):
        piece(0, bufs[0], o)

    def step(n, carry):
        phase(2 * n, bufs[0], 2 * n + 1, bufs[1])
        phase(2 * n + 1, bufs[1], lax.rem(2 * n + 2, NCH), bufs[0])
        return carry

    lax.fori_loop(0, NCH // 2, step, 0)


def direct_tile(stage, raw, xt, ops, b):
    for c in range(7):
        raw[c * 16 : c * 16 + QP, :] = stage[c * QP : (c + 1) * QP, :]
    raw[7 * 16 : 8 * 16, :] = jnp.zeros((16, BLK), F32)
    for m in range(6):
        ops[m] = jnp.zeros((BLK, BLK), F32)

    def point(q, carry):
        rows8 = raw[pl.ds(q, 8, stride=16), :]
        turned = jnp.concatenate([rows8, jnp.zeros((BLK - 8, BLK), F32)], 0).T
        src = [turned[:, c : c + 1] for c in range(7)]

        def centroid(a, carry2):
            tst = [xt[c, pl.ds(2 * b + a, 1), :] for c in range(7)]
            dl = [tst[c] - src[c] for c in range(3)]
            dist = jnp.sqrt(dl[0] * dl[0] + dl[1] * dl[1] + dl[2] * dl[2] + SOFTEN)
            dotted = tst[3] * src[3] + tst[4] * src[4] + tst[5] * src[5]
            charge = tst[6] * src[6]
            crossed = (
                dl[0] * (src[4] * tst[5] - src[5] * tst[4])
                + dl[1] * (src[5] * tst[3] - src[3] * tst[5])
                + dl[2] * (src[3] * tst[4] - src[4] * tst[3])
            )
            scaled = crossed / (dist * dist)
            kr = ki = None
            for m, (wr, wi) in enumerate(((2.0, 0.0), (1.0, 3.0))):
                decay = jnp.exp(-wi * dist) / dist
                gr = decay * jnp.cos(wr * dist)
                gi = decay * jnp.sin(wr * dist)
                cr = (wr * wr - wi * wi) * dotted - charge
                ci = 2.0 * wr * wi * dotted
                ops[2 * m] += cr * gr - ci * gi
                ops[2 * m + 1] += cr * gi + ci * gr
                fr = -wi * dist - 1.0
                fi = wr * dist
                ops[4] += scaled * (fr * gr - fi * gi)
                ops[5] += scaled * (fr * gi + fi * gr)
            return carry2

        return lax.fori_loop(0, 2, centroid, carry)

    lax.fori_loop(0, QP, point, 0)


def apply_operators(ops, xs, wh, wl, acc, b):
    def put(ref, value, places):
        neg = -value
        for row, col, sign in places:
            ref[row * BLK : (row + 1) * BLK, col * BLK : (col + 1) * BLK] = value if sign > 0 else neg

    def both(value, places):
        high = value.astype(BF16)
        low = (value - high.astype(F32)).astype(BF16)
        put(wh, high, places)
        put(wl, low, places)

    l1r, l1i, l2r, l2i = (ops[m] for m in range(4))
    both(l1r + l2r, ((0, 0, 1), (1, 1, 1)))
    both(l1i + l2i, ((0, 1, 1), (1, 0, -1)))
    both(l1r + 0.5 * l2r, ((2, 2, 1), (3, 3, 1)))
    both(l1i + 0.5 * l2i, ((2, 3, 1), (3, 2, -1)))
    both(ops[4], ((0, 2, 1), (1, 3, 1), (2, 0, -1), (3, 1, -1)))
    both(ops[5], ((0, 3, 1), (1, 2, -1), (2, 1, -1), (3, 0, 1)))
    first = jnp.dot(xs[...], wh[...], preferred_element_type=F32)
    second = jnp.dot(xs[0:BLK, :], wl[...], preferred_element_type=F32)
    acc[b] += first[0:BLK] + first[BLK:] + second


CROW = 104
XROW = CROW + 4 * NRHS
OUTER_ROWS = XROW + 64 + 8
FAR_ROWS = XROW + 32 + 8
MATE_ROWS = XROW + 8
FULL = TPB * SPAN


def is_even():
    return lax.axis_index("narrow") == 0


def mirrored(even, block):
    return jnp.where(even, block, TPB - 1 - block)


def load_of(mask):
    total = mask[0, 0]
    for b in range(TPB):
        for c in range(SPAN):
            if b or c:
                total = total + mask[b, c]
    return total


def number(ref, row):
    return jnp.max(ref[row : row + 8, 0:BLK]).astype(jnp.int32)


def shares(load_near, load_far):
    goal = lax.div(FULL + load_near + load_far + 1, 3)
    near = jnp.clip(goal - load_near, 3, 7)
    far = jnp.clip(lax.div(FULL - near + load_far + 1, 2) - load_far, 0, 8)
    return near, far


def is_near(u, v, share):
    option = jnp.where(u == -1, v, jnp.where(u == 0, 2 + v, FULL))
    return (u < -1) | ((v < 2) & (option < share - 3))


def is_far(u, v, share):
    return (jnp.where(u == 3, v, jnp.where(u == 2, TPB + v, FULL))) < share


PACK_COPIES = 5


def pack_kernel(mask, panels_at, test_at, currents, mate, outer, far, load, panels, test, sems):
    even = is_even()
    places = (
        (outer, 1, jnp.where(even, 0, 3 * BLK)),
        (far, 2, jnp.where(even, 2 * BLK, 0)),
        (mate, 3, jnp.where(even, BLK, 0)),
    )
    lanes = [pl.ds(pl.multiple_of(begin, BLK), count * BLK) for _, count, begin in places]
    copies = [pltpu.make_async_copy(panels_at, panels, sems.at[0]), pltpu.make_async_copy(test_at, test, sems.at[1])]
    for k in range(3):
        copies.append(pltpu.make_async_copy(currents.at[:, lanes[k]], places[k][0].at[CROW:XROW, :], sems.at[2 + k]))
    for each in copies:
        each.start()
    value = load_of(mask).astype(F32)
    outer[XROW + 64 : XROW + 72, :] = jnp.full((8, BLK), value, F32)
    far[XROW + 32 : XROW + 40, :] = jnp.full((8, 2 * BLK), value, F32)
    mate[XROW : XROW + 8, :] = jnp.full((8, 3 * BLK), value, F32)
    load[...] = jnp.full((8, BLK), value, F32)
    copies[0].wait()
    copies[1].wait()
    for k in range(3):
        places[k][0][0:GROWS, :] = panels[:, lanes[k]]
    for b in range(TPB):
        points = test[:, b * BLK : (b + 1) * BLK]
        outer[XROW + 16 * b : XROW + 16 * b + 14, :] = points
        row = XROW + 16 * (b // 2)
        far[row : row + 14, (b % 2) * BLK : (b % 2 + 1) * BLK] = points
    for each in copies[2:]:
        each.wait()


def engine(scratch, steps, wanted, load_source, accset):
    stage, xt, fts, ftt, tf, sf, buf0, buf1, ops, xs, wh, wl, acc, raw, flags = scratch

    def source(n, carry):
        any_wanted = wanted(n, 0)
        for b in range(1, TPB):
            any_wanted = any_wanted | wanted(n, b)

        @pl.when(any_wanted)
        def _():
            load_source(n)
            points = xt.at[accset(n)]
            place = [stage[c * QP : (c + 1) * QP, :] for c in range(3)]
            low = [jnp.min(jnp.min(v, 0, keepdims=True), 1, keepdims=True) for v in place]
            high = [jnp.max(jnp.max(v, 0, keepdims=True), 1, keepdims=True) for v in place]
            centre = [(u + v) * 0.5 for u, v in zip(low, high)]
            bound = jnp.full((8, BLK), SOFTEN, F32)
            for c in range(3):
                far = jnp.maximum(jnp.abs(points[c] - low[c]), jnp.abs(points[c] - high[c]))
                bound = bound + far * far
            for b in range(TPB):
                flags[b] = (jnp.max(bound[2 * b : 2 * b + 2]) <= Z_MAX).astype(jnp.int32)
            source_features(stage, fts, sf, centre, [place[c] - centre[c] for c in range(3)])
            test_features(points, ftt, centre)

            def tile(b, carry2):
                @pl.when(wanted(n, b))
                def _():
                    @pl.when(flags[b] > 0)
                    def _():
                        fast_tile(ftt, tf, sf, (buf0, buf1), ops, b, flags[b])

                    @pl.when(flags[b] == 0)
                    def _():
                        direct_tile(stage, raw, points, ops, b)

                    apply_operators(ops, xs, wh, wl, acc, TPB * accset(n) + b)

                return carry2

            lax.fori_loop(0, TPB, tile, 0)

        return carry

    tf[...] = jnp.zeros_like(tf)
    ftt[...] = jnp.zeros_like(ftt)
    fts[...] = jnp.zeros_like(fts)
    lax.fori_loop(0, steps, source, 0)


def fill(scratch, pan, cur, row, slot):
    stage, xs = scratch[0], scratch[9]
    lanes = pl.ds(pl.multiple_of(slot * BLK, BLK), BLK)
    stage[...] = pan[0:GROWS, lanes]
    for g in range(4):
        value = cur[row + g * NRHS : row + (g + 1) * NRHS, lanes]
        high = value.astype(BF16)
        xs[0:BLK, g * BLK : (g + 1) * BLK] = high
        xs[BLK : 2 * BLK, g * BLK : (g + 1) * BLK] = (value - high.astype(F32)).astype(BF16)


def fill_tests(xt, which, blocks):
    for c in range(7):
        for b in range(TPB):
            xt[which, c, 2 * b : 2 * b + 2, :] = blocks(b, 2 * c)


def own_tests(test):
    return lambda b, row: test[row : row + 2, b * BLK : (b + 1) * BLK]


def clear(acc, count):
    for b in range(count):
        acc[b] = jnp.zeros((BLK, 4 * BLK), F32)


def write_out(out, acc, blocks):
    for col, b in enumerate(blocks):
        for g in range(4):
            out[g * NRHS : (g + 1) * NRHS, col * BLK : (col + 1) * BLK] = acc[b, :, g * BLK : (g + 1) * BLK]


FIRST = 5


def first_kernel(mask, test, panels, currents, out, done, *scratch):
    scratch = scratch[:-1]
    even = is_even()
    full = load_of(mask) == FULL
    fill_tests(scratch[1], 0, own_tests(test))
    clear(scratch[12], TPB)

    def plan(i, used):
        n, b = lax.div(i, TPB), lax.rem(i, TPB)
        u, v = mirrored(even, n), mirrored(even, b)
        dense = (u == 1) | ((u == 0) & (v == 3))
        wanted = (full & dense) | (jnp.logical_not(full) & (mask[b, n - b + REACH] > 0))
        now = wanted & (used < FIRST)
        done[n, b] = now.astype(jnp.int32)
        return used + now.astype(jnp.int32)

    lax.fori_loop(0, TPB * TPB, plan, jnp.int32(0))
    engine(scratch, TPB, lambda n, b: done[n, b] > 0, lambda n: fill(scratch, panels, currents, 0, n), lambda n: 0)
    write_out(out, scratch[12], range(TPB))


QUOTA = 7
HELP_STEPS = 6
OWN_STEPS = 8


def own_place(even, n):
    return jnp.where(n < 4, n, jnp.where(n == 4, jnp.where(even, -1, 4), jnp.where(even, n - 1, n - 8)))


def load_own(scratch, panels, currents, outer, mate, n):
    @pl.when(n < 4)
    def _():
        fill(scratch, panels, currents, 0, n)

    @pl.when(n == 4)
    def _():
        fill(scratch, outer, outer, CROW, 0)

    @pl.when(n > 4)
    def _():
        fill(scratch, mate, mate, CROW, n - 5)


def second_kernel(
    mask, done, test, panels, currents, outer, far, mate, load_far, part, out_near, out_far, out_own, todo, *scratch
):
    plan, scratch = scratch[-1], scratch[:-1]
    even = is_even()
    odd = jnp.logical_not(even)
    own_load, mate_load = load_of(mask), number(mate, XROW)
    near_load, far_load = number(outer, XROW + 64), number(far, XROW + 32)
    share_near, _ = shares(own_load, mate_load)
    _, share_far = shares(mate_load, own_load)
    give_near, give_far = shares(near_load, number(load_far, 0))
    full = own_load == FULL
    xt, acc = scratch[1], scratch[12]
    fill_tests(xt, 0, lambda b, row: outer[XROW + 16 * b + row : XROW + 16 * b + row + 2, :])
    fill_tests(
        xt,
        1,
        lambda b, row: far[
            XROW + 16 * (b // 2) + row : XROW + 16 * (b // 2) + row + 2, (b % 2) * BLK : (b % 2 + 1) * BLK
        ],
    )
    fill_tests(xt, 2, own_tests(test))
    clear(acc, 2 * TPB)
    for b in range(TPB):
        for g in range(4):
            acc[2 * TPB + b, :, g * BLK : (g + 1) * BLK] = part[g * NRHS : (g + 1) * NRHS, b * BLK : (b + 1) * BLK]

    def plan_help(i, used):
        n, b = lax.div(i, TPB), lax.rem(i, TPB)
        v_near, v_far = mirrored(odd, b), mirrored(even, b)
        u_near, u_far = jnp.where(n == 3, 0, -1 - n), 7 - n
        of_near = (n < 4) & (v_near - u_near <= REACH) & is_near(u_near, v_near, share_near)
        of_far = (n >= 4) & is_far(u_far, v_far, share_far)
        wanted = ((near_load == FULL) & of_near) | ((far_load == FULL) & of_far)
        plan[i] = wanted.astype(jnp.int32)
        return used + wanted.astype(jnp.int32)

    def plan_own(i, used):
        n, b = lax.div(i, TPB), lax.rem(i, TPB)
        rel = own_place(even, n)
        column = rel - b + REACH
        inside = (column >= 0) & (column < SPAN)
        sparse = inside & (mask[b, jnp.clip(column, 0, SPAN - 1)] > 0)
        u, v = mirrored(even, rel), mirrored(even, b)
        dense = inside & jnp.logical_not(is_near(u, v, give_near) | is_far(u, v, give_far))
        earlier = (n < TPB) & (done[jnp.minimum(n, TPB - 1), b] > 0)
        wanted = ((full & dense) | (jnp.logical_not(full) & sparse)) & jnp.logical_not(earlier)
        now = wanted & (used < QUOTA)
        plan[HELP_STEPS * TPB + i] = now.astype(jnp.int32)
        todo[n, b] = (wanted & jnp.logical_not(now)).astype(jnp.int32)
        return used + now.astype(jnp.int32)

    used = lax.fori_loop(0, HELP_STEPS * TPB, plan_help, jnp.int32(0))
    lax.fori_loop(0, OWN_STEPS * TPB, plan_own, used)

    def load_source(n):
        @pl.when(n < 3)
        def _():
            fill(scratch, panels, currents, 0, mirrored(even, n))

        @pl.when(n == 3)
        def _():
            fill(scratch, outer, outer, CROW, 0)

        @pl.when((n > 3) & (n < HELP_STEPS))
        def _():
            fill(scratch, far, far, CROW, jnp.where(even, 5 - n, n - 4))

        @pl.when(n >= HELP_STEPS)
        def _():
            load_own(scratch, panels, currents, outer, mate, n - HELP_STEPS)

    engine(
        scratch,
        HELP_STEPS + OWN_STEPS,
        lambda n, b: plan[n * TPB + b] > 0,
        load_source,
        lambda n: jnp.where(n < 4, 0, jnp.where(n < HELP_STEPS, 1, 2)),
    )
    shift = jnp.where(even, 2, 0)
    write_out(out_near, acc, [b + shift for b in range(2)])
    write_out(out_far, acc, range(TPB, 2 * TPB))
    write_out(out_own, acc, range(2 * TPB, 3 * TPB))


def rest_kernel(todo, test, panels, currents, outer, mate, part, after, out, *scratch):
    acc = scratch[12]
    fill_tests(scratch[1], 0, own_tests(test))
    for b in range(TPB):
        for g in range(4):
            acc[b, :, g * BLK : (g + 1) * BLK] = part[g * NRHS : (g + 1) * NRHS, b * BLK : (b + 1) * BLK]
    engine(
        scratch,
        OWN_STEPS,
        lambda n, b: todo[n, b] > 0,
        lambda n: load_own(scratch, panels, currents, outer, mate, n),
        lambda n: 0,
    )
    write_out(out, acc, range(TPB))


def scratch_for(sets):
    return [
        pltpu.VMEM((GROWS, BLK), F32),
        pltpu.VMEM((sets, 7, 8, BLK), F32),
        pltpu.VMEM(((NTERM + 16) * 16, BLK), F32),
        pltpu.VMEM((TROWS * 8, BLK), F32),
        pltpu.VMEM((KDIM, NOUT * 256), BF16),
        pltpu.VMEM((NCH * MROWS, KDIM), BF16),
        pltpu.VMEM((MROWS + 8, NOUT * 256), F32),
        pltpu.VMEM((MROWS + 8, NOUT * 256), F32),
        pltpu.VMEM((6, BLK, BLK), F32),
        pltpu.VMEM((2 * BLK, 4 * BLK), BF16),
        pltpu.VMEM((4 * BLK, 4 * BLK), BF16),
        pltpu.VMEM((4 * BLK, 4 * BLK), BF16),
        pltpu.VMEM((sets * TPB, BLK, 4 * BLK), F32),
        pltpu.VMEM((8 * 16, BLK), F32),
        pltpu.SMEM((TPB,), jnp.int32),
    ]


def call(kernel, outs, operands, sets=0, tables=1, unread=0, tiles=1, table=(), copies=0):
    vmem = pl.BlockSpec(memory_space=pltpu.VMEM)
    smem = pl.BlockSpec(memory_space=pltpu.SMEM)
    anywhere = pl.BlockSpec(memory_space=pl.ANY)
    plain = len(operands) - tables - unread
    shapes = [jax.ShapeDtypeStruct(s, F32) for s in outs]
    specs = [vmem] * len(outs)
    scratch = scratch_for(sets) if sets else []
    if copies:
        scratch += [
            pltpu.VMEM((GROWS, TPB * BLK), F32),
            pltpu.VMEM((14, TPB * BLK), F32),
            pltpu.SemaphoreType.DMA((copies,)),
        ]
    if table:
        shapes.append(jax.ShapeDtypeStruct(table, jnp.int32))
        specs.append(smem)
        scratch.append(pltpu.SMEM(((HELP_STEPS + OWN_STEPS) * TPB,), jnp.int32))
    return pl.pallas_call(
        kernel,
        out_shape=shapes,
        in_specs=[smem] * tables + [vmem] * plain + [anywhere] * unread,
        out_specs=specs,
        scratch_shapes=scratch,
        compiler_params=pltpu.CompilerParams(vmem_limit_bytes=(60 if copies else 26) * 1024 * 1024),
        cost_estimate=pl.CostEstimate(flops=tiles * 5 * 10**9, bytes_accessed=4 * 10**6, transcendentals=0),
    )(*operands)


def body(panels, test_points, currents, near_mask):
    count = lax.axis_size("cluster") * lax.axis_size("narrow")
    axes = ("cluster", "narrow")
    swap = [(i, i ^ 1) for i in range(count)]
    across = [(i, (i - 1) % count if i % 2 == 0 else (i + 1) % count) for i in range(count)]
    away = [(i, (i - 2) % count if i % 2 == 0 else (i + 2) % count) for i in range(count)]
    back = [(target, source) for source, target in away]
    width = TPB * BLK
    wide = 4 * NRHS
    mate, outer, far, load = call(
        pack_kernel,
        [(MATE_ROWS, 3 * BLK), (OUTER_ROWS, BLK), (FAR_ROWS, 2 * BLK), (8, BLK)],
        [near_mask, panels, test_points, currents],
        unread=3,
        copies=PACK_COPIES,
    )
    load_far = lax.ppermute(load, axes, back)
    outer = lax.ppermute(outer, axes, across)
    far = lax.ppermute(far, axes, away)
    mate = lax.ppermute(mate, axes, swap)
    part, done = call(
        first_kernel, [(wide, width)], [near_mask, test_points, panels, currents], 1, tiles=5, table=(TPB, TPB)
    )
    to_near, to_far, part, todo = call(
        second_kernel,
        [(wide, 2 * BLK), (wide, width), (wide, width)],
        [near_mask, done, test_points, panels, currents, outer, far, mate, load_far, part],
        3,
        tables=2,
        tiles=7,
        table=(OWN_STEPS, TPB),
    )
    from_near = lax.ppermute(to_near, axes, across)
    from_far = lax.ppermute(to_far, axes, back)
    (rest,) = call(
        rest_kernel,
        [(wide, width)],
        [todo, test_points, panels, currents, outer, mate, part, to_near],
        1,
        unread=1,
        tiles=8,
    )
    padded = jnp.where(
        lax.axis_index("narrow") == 0,
        jnp.pad(from_near, ((0, 0), (0, 2 * BLK))),
        jnp.pad(from_near, ((0, 0), (2 * BLK, 0))),
    )
    return rest + from_far + padded


def solution(mesh):
    return jax.shard_map(
        body,
        mesh=mesh,
        in_specs=(
            P(None, ("cluster", "narrow")),
            P(None, ("cluster", "narrow")),
            P(None, ("cluster", "narrow")),
            P(("cluster", "narrow"), None),
        ),
        out_specs=P(None, ("cluster", "narrow")),
        check_vma=False,
    )
```

```python
import functools
import itertools
import math

import jax
import jax.numpy as jnp
from jax import lax
from jax.experimental import pallas as pl
from jax.experimental.pallas import tpu as pltpu
from jax.sharding import PartitionSpec as P

F32 = jnp.float32
BF16 = jnp.bfloat16
BLK = 128
QP = 14
REACH = 3
SPAN = 7
TPB = 4
GROWS = 98
NRHS = 128
SOFTEN = 0.04

Z_MAX = 14.0
DEGREE = 4
COS_HALF = (2.828426289053651, -0.35355064760758376, 0.007364148070439611, -6.107114702262049e-05, 2.4846120790492805e-07)
SIN_HALF = (1.4142135239177973, -0.05892543897495882, 0.0007364984722676873, -4.370137027858996e-06, 1.4053654408325383e-08)

TERMS = []
for _total in range(DEGREE + 1):
    for _j in range(_total + 1):
        _l = _total - _j
        for _a in itertools.product(range(_l + 1), repeat=3):
            if sum(_a) == _l:
                TERMS.append((_j, _a))
NTERM = 72
assert len(TERMS) <= NTERM
ONE = TERMS.index((0, (0, 0, 0)))
LIN = [TERMS.index((0, tuple(int(c == k) for c in range(3)))) for k in range(3)]
SQR = TERMS.index((1, (0, 0, 0)))
KDIM = 256
NOUT = 7
JC = 16
NCH = BLK // JC
MROWS = JC * QP


def powers_of(vec):
    one = None
    table = {(0, 0, 0): one}
    for total in range(1, DEGREE + 1):
        for a in itertools.product(range(total + 1), repeat=3):
            if sum(a) != total:
                continue
            axis = next(c for c in range(3) if a[c] > 0)
            prev = tuple(a[c] - (c == axis) for c in range(3))
            table[a] = vec[axis] if table[prev] is None else table[prev] * vec[axis]
    return table


def split2(value):
    high = value.astype(BF16).astype(F32)
    return high, value - high


def source_features(stage, fts, sf, centre, y):
    mono = powers_of(y)
    square = y[0] * y[0] + y[1] * y[1] + y[2] * y[2]
    sq = [None, square, square * square]
    sq.append(sq[2] * square)
    sq.append(sq[2] * sq[2])
    ones = jnp.ones_like(square)

    def put(row, value):
        fts[row * 16 : row * 16 + QP, :] = value

    for k, (j, a) in enumerate(TERMS):
        const = (-2.0) ** sum(a) / (math.prod(math.factorial(v) for v in a) * math.factorial(j))
        value = mono[a]
        if sq[j] is not None:
            value = sq[j] if value is None else value * sq[j]
        if value is None:
            value = ones
        put(k, value * const if const != 1.0 else value)
    base = NTERM
    s = [stage[(3 + c) * QP : (4 + c) * QP, :] for c in range(3)]
    d = stage[6 * QP : 7 * QP, :]
    for c in range(3):
        put(base + c, s[c])
    put(base + 3, d)
    for c in range(3):
        c1, c2 = (c + 1) % 3, (c + 2) % 3
        put(base + 4 + c, y[c1] * s[c2] - y[c2] * s[c1])
    extra = base + 8
    for half in range(2):
        for c in range(3):
            put(extra + 4 * half + c, y[c] * -2.0)
        put(extra + 4 * half + 3, square)
    rows = lax.broadcasted_iota(jnp.int32, (8, BLK), 0)
    for q in range(QP):
        main = fts[pl.ds(q, NTERM, stride=16), :]
        bil = fts[pl.ds(base * 16 + q, 8, stride=16), :]
        ext = fts[pl.ds(extra * 16 + q, 8, stride=16), :]
        mh, ml = split2(main)
        bh, bl = split2(bil)
        eh, rest = split2(ext)
        em, el = split2(rest)
        zrow = jnp.where(rows < 4, em, eh)
        zrow2 = jnp.where(rows < 4, el, jnp.where(rows == 4, 1.0, 0.0))
        full = jnp.concatenate([mh, mh, ml, bh, bh, bl, zrow, zrow2], 0)
        turned = full.astype(BF16).T
        for ch in range(NCH):
            sf[ch * MROWS + q * JC : ch * MROWS + (q + 1) * JC, :] = turned[ch * JC : (ch + 1) * JC, :]


def horner(coefs, m, w):
    der = [coefs[k] * math.factorial(k) / math.factorial(k - m) for k in range(m, len(coefs))]
    value = None
    for c in reversed(der):
        value = c if value is None else value * w + c
    return value


OFF_C, OFF_S, OFF_Z = 0, NTERM, 2 * NTERM
OFF_B = 3 * NTERM
OFF_E = OFF_B + 32
TROWS = OFF_E + 16


def test_features(xt, ftt, centre):
    x = [xt[c] - centre[c] for c in range(3)]
    t = [xt[3 + c] for c in range(3)]
    e = xt[6]
    w = x[0] * x[0] + x[1] * x[1] + x[2] * x[2] + SOFTEN
    mono = powers_of(x)

    def put(row, value):
        ftt[row * 8 : row * 8 + 8, :] = value

    for off, coefs in ((OFF_C, COS_HALF), (OFF_S, SIN_HALF)):
        der = [horner(coefs, m, w) for m in range(DEGREE + 1)]
        for k, (j, a) in enumerate(TERMS):
            level = der[j + sum(a)]
            value = level if mono[a] is None else mono[a] * level
            put(off + k, jnp.broadcast_to(value, w.shape))
    put(OFF_Z + ONE, w)
    put(OFF_Z + SQR, jnp.ones_like(w))
    for c in range(3):
        put(OFF_Z + LIN[c], x[c])
    charge = e * -0.25
    for c in range(3):
        put(OFF_B + c, t[c])
        put(OFF_B + 8 + c, t[c] * -2.0)
        put(OFF_B + 16 + c, t[c] * 1.5)
        c1, c2 = (c + 1) % 3, (c + 2) % 3
        put(OFF_B + 24 + c, (t[c1] * x[c2] - t[c2] * x[c1]) * -0.25)
        put(OFF_B + 28 + c, t[c] * 0.25)
    put(OFF_B + 3, charge)
    put(OFF_B + 11, charge)
    for half in range(2):
        for c in range(3):
            put(OFF_E + 4 * half + c, x[c])
        put(OFF_E + 4 * half + 3, jnp.ones_like(w))
    for c in range(4):
        put(OFF_E + 8 + c, x[c] if c < 3 else jnp.ones_like(w))
    put(OFF_E + 12, w)


def test_matrix(ftt, tf, b):
    rows = lax.broadcasted_iota(jnp.int32, (8, BLK), 0)
    zero8 = jnp.zeros((8, BLK), F32)
    for a in range(2):
        ba = 2 * b + a

        def take(off, n):
            return ftt[pl.ds(off * 8 + ba, n, stride=8), :]

        for out, off in ((0, OFF_Z), (1, OFF_C), (2, OFF_S)):
            high, low = split2(take(off, NTERM))
            lanes = slice(out * 256 + a * BLK, out * 256 + (a + 1) * BLK)
            tf[0:224, lanes] = jnp.concatenate([high, low, high, zero8], 0).astype(BF16)
        eh, rest = split2(take(OFF_E, 8))
        em, el = split2(rest)
        fh, rest2 = split2(take(OFF_E + 8, 8))
        fm, fl = split2(rest2)
        first = jnp.where(rows < 4, em, el)
        second = jnp.where(rows < 4, fh, jnp.where(rows == 4, fl, 0.0))
        tf[240:256, a * BLK : (a + 1) * BLK] = jnp.concatenate([first, second], 0).astype(BF16)
        for m in range(4):
            high, low = split2(take(OFF_B + 8 * m, 8))
            out = 3 + m
            lanes = slice(out * 256 + a * BLK, out * 256 + (a + 1) * BLK)
            tf[208:240, lanes] = jnp.concatenate([zero8, high, low, high], 0).astype(BF16)


EXP_RATE = -3.0 / math.log(2.0)


def pair_terms(z, cos_h, sin_h, k1, k2, k6, kk):
    inv = lax.rsqrt(z)
    dist = z * inv
    s0 = sin_h * dist
    c = 4.0 - s0 * s0
    s = s0 * cos_h
    c2 = c * c - 8.0
    s2 = c * s
    decay = jnp.exp2(dist * EXP_RATE)
    p = decay * c
    q = decay * s
    half = inv * 0.5
    c2r = c2 * half
    s2r = s2 * half
    pr = p * inv
    qr = q * inv
    weight = kk * (inv * inv)
    l1r = k1 * c2r
    l1i = k1 * s2r
    l2r = k2 * pr - k6 * qr
    l2i = k2 * qr + k6 * pr
    kr = weight * (((c2r + pr) + (s2 + 3.0 * p)) + q)
    ki = weight * (((s2r + qr) + (3.0 * q - c2)) - p)
    return l1r, l1i, l2r, l2i, kr, ki


AHEAD = 6


def fast_tile(ftt, tf, sf, bufs, ops, b, flag):
    test_matrix(ftt, tf, b)
    spare = pl.multiple_of(MROWS - 8 + 8 * flag, 8)

    def piece(chunk, buf, o):
        rows = pl.ds(pl.multiple_of(chunk * MROWS, 16), MROWS)
        lanes = slice(o * 256, (o + 1) * 256)
        buf[0:MROWS, lanes] = jnp.dot(sf[rows, :], tf[:, lanes], preferred_element_type=F32)

    def phase(chunk, buf, next_chunk, next_buf):
        work = [(g, q, a) for g in range(JC // 8) for q in range(QP) for a in range(2)]
        per = -(-len(work) // NOUT)
        acc, history = None, []
        for o in range(NOUT):
            piece(next_chunk, next_buf, o)
            for g, q, a in work[o * per : (o + 1) * per]:
                if q == 0 and a == 0:
                    acc = None
                row = q * JC + g * 8
                if len(history) >= AHEAD:
                    buf[pl.ds(spare, 8), 0:BLK] = history[-AHEAD]
                vals = [buf[row : row + 8, k * 256 + a * BLK : k * 256 + (a + 1) * BLK] for k in range(NOUT)]
                terms = pair_terms(*vals)
                acc = list(terms) if acc is None else [u + v for u, v in zip(acc, terms)]
                history.append(acc[5])
                if q == QP - 1 and a == 1:
                    start = pl.multiple_of(chunk * JC + g * 8, 8)
                    for m in range(6):
                        ops[m, pl.ds(start, 8), :] = acc[m]

    for o in range(NOUT):
        piece(0, bufs[0], o)

    def step(n, carry):
        phase(2 * n, bufs[0], 2 * n + 1, bufs[1])
        phase(2 * n + 1, bufs[1], lax.rem(2 * n + 2, NCH), bufs[0])
        return carry

    lax.fori_loop(0, NCH // 2, step, 0)


def direct_tile(stage, raw, xt, ops, b):
    for c in range(7):
        raw[c * 16 : c * 16 + QP, :] = stage[c * QP : (c + 1) * QP, :]
    raw[7 * 16 : 8 * 16, :] = jnp.zeros((16, BLK), F32)
    for m in range(6):
        ops[m] = jnp.zeros((BLK, BLK), F32)

    def point(q, carry):
        rows8 = raw[pl.ds(q, 8, stride=16), :]
        turned = jnp.concatenate([rows8, jnp.zeros((BLK - 8, BLK), F32)], 0).T
        src = [turned[:, c : c + 1] for c in range(7)]

        def centroid(a, carry2):
            tst = [xt[c, pl.ds(2 * b + a, 1), :] for c in range(7)]
            dl = [tst[c] - src[c] for c in range(3)]
            dist = jnp.sqrt(dl[0] * dl[0] + dl[1] * dl[1] + dl[2] * dl[2] + SOFTEN)
            dotted = tst[3] * src[3] + tst[4] * src[4] + tst[5] * src[5]
            charge = tst[6] * src[6]
            crossed = (
                dl[0] * (src[4] * tst[5] - src[5] * tst[4])
                + dl[1] * (src[5] * tst[3] - src[3] * tst[5])
                + dl[2] * (src[3] * tst[4] - src[4] * tst[3])
            )
            scaled = crossed / (dist * dist)
            kr = ki = None
            for m, (wr, wi) in enumerate(((2.0, 0.0), (1.0, 3.0))):
                decay = jnp.exp(-wi * dist) / dist
                gr = decay * jnp.cos(wr * dist)
                gi = decay * jnp.sin(wr * dist)
                cr = (wr * wr - wi * wi) * dotted - charge
                ci = 2.0 * wr * wi * dotted
                ops[2 * m] += cr * gr - ci * gi
                ops[2 * m + 1] += cr * gi + ci * gr
                fr = -wi * dist - 1.0
                fi = wr * dist
                ops[4] += scaled * (fr * gr - fi * gi)
                ops[5] += scaled * (fr * gi + fi * gr)
            return carry2

        return lax.fori_loop(0, 2, centroid, carry)

    lax.fori_loop(0, QP, point, 0)


def apply_operators(ops, xs, wh, wl, acc, b):
    def put(ref, value, places):
        neg = -value
        for row, col, sign in places:
            ref[row * BLK : (row + 1) * BLK, col * BLK : (col + 1) * BLK] = value if sign > 0 else neg

    def both(value, places):
        high = value.astype(BF16)
        low = (value - high.astype(F32)).astype(BF16)
        put(wh, high, places)
        put(wl, low, places)

    l1r, l1i, l2r, l2i = (ops[m] for m in range(4))
    both(l1r + l2r, ((0, 0, 1), (1, 1, 1)))
    both(l1i + l2i, ((0, 1, 1), (1, 0, -1)))
    both(l1r + 0.5 * l2r, ((2, 2, 1), (3, 3, 1)))
    both(l1i + 0.5 * l2i, ((2, 3, 1), (3, 2, -1)))
    both(ops[4], ((0, 2, 1), (1, 3, 1), (2, 0, -1), (3, 1, -1)))
    both(ops[5], ((0, 3, 1), (1, 2, -1), (2, 1, -1), (3, 0, 1)))
    first = jnp.dot(xs[...], wh[...], preferred_element_type=F32)
    second = jnp.dot(xs[0:BLK, :], wl[...], preferred_element_type=F32)
    acc[b] += first[0:BLK] + first[BLK:] + second


CROW = 104
XROW = CROW + 4 * NRHS
OUTER_ROWS = XROW + 64 + 8
FAR_ROWS = XROW + 32 + 8
MATE_ROWS = XROW
FULL = TPB * SPAN


def is_even():
    return lax.axis_index("narrow") == 0


def mirrored(even, block):
    return jnp.where(even, block, TPB - 1 - block)


def load_of(mask):
    total = mask[0, 0]
    for b in range(TPB):
        for c in range(SPAN):
            if b or c:
                total = total + mask[b, c]
    return total


def number(ref, row):
    return jnp.max(ref[row : row + 8, 0:BLK]).astype(jnp.int32)


def share(load):
    return jnp.clip(lax.div(FULL - 2 * SIDE + load + 1, 2) - load, 3, 7)


SIDE = 4


def is_near(u, v, given):
    option = jnp.where(u == -1, v, jnp.where(u == 0, 2 + v, FULL))
    return (u < -1) | ((v < 2) & (option < given - 3))


def is_side(u):
    return (u == 2) | (u == 3)


PACK_COPIES = 5


def pack_kernel(mask, panels_at, test_at, currents, mate, outer, far, panels, test, sems):
    even = is_even()
    places = (
        (outer, 1, jnp.where(even, 0, 3 * BLK)),
        (far, 2, jnp.where(even, 2 * BLK, 0)),
        (mate, 3, jnp.where(even, BLK, 0)),
    )
    lanes = [pl.ds(pl.multiple_of(begin, BLK), count * BLK) for _, count, begin in places]
    copies = [pltpu.make_async_copy(panels_at, panels, sems.at[0]), pltpu.make_async_copy(test_at, test, sems.at[1])]
    for k in range(3):
        copies.append(pltpu.make_async_copy(currents.at[:, lanes[k]], places[k][0].at[CROW:XROW, :], sems.at[2 + k]))
    for each in copies:
        each.start()
    value = load_of(mask).astype(F32)
    outer[XROW + 64 : XROW + 72, :] = jnp.full((8, BLK), value, F32)
    far[XROW + 32 : XROW + 40, :] = jnp.full((8, 2 * BLK), value, F32)
    copies[0].wait()
    copies[1].wait()
    for k in range(3):
        places[k][0][0:GROWS, :] = panels[:, lanes[k]]
    for b in range(TPB):
        points = test[:, b * BLK : (b + 1) * BLK]
        outer[XROW + 16 * b : XROW + 16 * b + 14, :] = points
        row = XROW + 16 * (b // 2)
        far[row : row + 14, (b % 2) * BLK : (b % 2 + 1) * BLK] = points
    for each in copies[2:]:
        each.wait()


def engine(scratch, steps, wanted, load_source, accset):
    stage, xt, fts, ftt, tf, sf, buf0, buf1, ops, xs, wh, wl, acc, raw, flags = scratch

    def source(n, carry):
        any_wanted = wanted(n, 0)
        for b in range(1, TPB):
            any_wanted = any_wanted | wanted(n, b)

        @pl.when(any_wanted)
        def _():
            load_source(n)
            points = xt.at[accset(n)]
            place = [stage[c * QP : (c + 1) * QP, :] for c in range(3)]
            low = [jnp.min(jnp.min(v, 0, keepdims=True), 1, keepdims=True) for v in place]
            high = [jnp.max(jnp.max(v, 0, keepdims=True), 1, keepdims=True) for v in place]
            centre = [(u + v) * 0.5 for u, v in zip(low, high)]
            bound = jnp.full((8, BLK), SOFTEN, F32)
            for c in range(3):
                far = jnp.maximum(jnp.abs(points[c] - low[c]), jnp.abs(points[c] - high[c]))
                bound = bound + far * far
            for b in range(TPB):
                flags[b] = (jnp.max(bound[2 * b : 2 * b + 2]) <= Z_MAX).astype(jnp.int32)
            source_features(stage, fts, sf, centre, [place[c] - centre[c] for c in range(3)])
            test_features(points, ftt, centre)

            def tile(b, carry2):
                @pl.when(wanted(n, b))
                def _():
                    @pl.when(flags[b] > 0)
                    def _():
                        fast_tile(ftt, tf, sf, (buf0, buf1), ops, b, flags[b])

                    @pl.when(flags[b] == 0)
                    def _():
                        direct_tile(stage, raw, points, ops, b)

                    apply_operators(ops, xs, wh, wl, acc, TPB * accset(n) + b)

                return carry2

            lax.fori_loop(0, TPB, tile, 0)

        return carry

    tf[...] = jnp.zeros_like(tf)
    ftt[...] = jnp.zeros_like(ftt)
    fts[...] = jnp.zeros_like(fts)
    lax.fori_loop(0, steps, source, 0)


def fill(scratch, pan, cur, row, slot):
    stage, xs = scratch[0], scratch[9]
    lanes = pl.ds(pl.multiple_of(slot * BLK, BLK), BLK)
    stage[...] = pan[0:GROWS, lanes]
    for g in range(4):
        value = cur[row + g * NRHS : row + (g + 1) * NRHS, lanes]
        high = value.astype(BF16)
        xs[0:BLK, g * BLK : (g + 1) * BLK] = high
        xs[BLK : 2 * BLK, g * BLK : (g + 1) * BLK] = (value - high.astype(F32)).astype(BF16)


def fill_tests(xt, which, blocks):
    for c in range(7):
        for b in range(TPB):
            xt[which, c, 2 * b : 2 * b + 2, :] = blocks(b, 2 * c)


def own_tests(test):
    return lambda b, row: test[row : row + 2, b * BLK : (b + 1) * BLK]


def clear(acc, count):
    for b in range(count):
        acc[b] = jnp.zeros((BLK, 4 * BLK), F32)


def write_out(out, acc, blocks):
    for col, b in enumerate(blocks):
        for g in range(4):
            out[g * NRHS : (g + 1) * NRHS, col * BLK : (col + 1) * BLK] = acc[b, :, g * BLK : (g + 1) * BLK]


FIRST = 5


def first_kernel(mask, test, panels, currents, out, done, *scratch):
    scratch = scratch[:-1]
    even = is_even()
    full = load_of(mask) == FULL
    fill_tests(scratch[1], 0, own_tests(test))
    clear(scratch[12], TPB)

    def plan(i, used):
        n, b = lax.div(i, TPB), lax.rem(i, TPB)
        u, v = mirrored(even, n), mirrored(even, b)
        dense = (u == 1) | ((u == 0) & (v == 2))
        wanted = (full & dense) | (jnp.logical_not(full) & (mask[b, n - b + REACH] > 0))
        now = wanted & (used < FIRST)
        done[n, b] = now.astype(jnp.int32)
        return used + now.astype(jnp.int32)

    lax.fori_loop(0, TPB * TPB, plan, jnp.int32(0))
    engine(scratch, TPB, lambda n, b: done[n, b] > 0, lambda n: fill(scratch, panels, currents, 0, n), lambda n: 0)
    write_out(out, scratch[12], range(TPB))


QUOTA = 7
HELP_STEPS = 8
OWN_STEPS = 8


def own_place(even, n):
    return jnp.where(n < 4, n, jnp.where(n == 4, jnp.where(even, -1, 4), jnp.where(even, n - 1, n - 8)))


def load_own(scratch, panels, currents, outer, mate, n):
    @pl.when(n < 4)
    def _():
        fill(scratch, panels, currents, 0, n)

    @pl.when(n == 4)
    def _():
        fill(scratch, outer, outer, CROW, 0)

    @pl.when(n > 4)
    def _():
        fill(scratch, mate, mate, CROW, n - 5)


def second_kernel(
    mask, done, test, panels, currents, outer, far, wing, mate, out_near, out_far, out_wing, out_own, todo, *scratch
):
    plan, scratch = scratch[-1], scratch[:-1]
    even = is_even()
    odd = jnp.logical_not(even)
    own_load, near_load = load_of(mask), number(outer, XROW + 64)
    far_full, wing_full = number(far, XROW + 32) == FULL, number(wing, XROW + 32) == FULL
    near_full, full = near_load == FULL, own_load == FULL
    take, give = share(own_load), share(near_load)
    xt, acc = scratch[1], scratch[12]
    fill_tests(xt, 0, lambda b, row: outer[XROW + 16 * b + row : XROW + 16 * b + row + 2, :])
    for which, ref in ((1, far), (2, wing)):
        fill_tests(
            xt,
            which,
            lambda b, row, ref=ref: ref[
                XROW + 16 * (b // 2) + row : XROW + 16 * (b // 2) + row + 2, (b % 2) * BLK : (b % 2 + 1) * BLK
            ],
        )
    fill_tests(xt, 3, own_tests(test))
    clear(acc, 4 * TPB)

    def plan_help(i, used):
        n, b = lax.div(i, TPB), lax.rem(i, TPB)
        v_near, v_side = mirrored(odd, b), mirrored(even, b)
        u_near = jnp.where(n == 3, 0, -1 - n)
        of_near = (n < 4) & (v_near - u_near <= REACH) & is_near(u_near, v_near, take)
        of_far = ((n == 4) | (n == 5)) & (v_side >= 2)
        of_wing = (n >= 6) & (v_side < 2)
        wanted = (near_full & of_near) | (far_full & of_far) | (wing_full & of_wing)
        plan[i] = wanted.astype(jnp.int32)
        return used + wanted.astype(jnp.int32)

    def plan_own(i, used):
        n, b = lax.div(i, TPB), lax.rem(i, TPB)
        rel = own_place(even, n)
        column = rel - b + REACH
        inside = (column >= 0) & (column < SPAN)
        sparse = inside & (mask[b, jnp.clip(column, 0, SPAN - 1)] > 0)
        u, v = mirrored(even, rel), mirrored(even, b)
        dense = inside & jnp.logical_not(is_near(u, v, give) | is_side(u))
        earlier = (n < TPB) & (done[jnp.minimum(n, TPB - 1), b] > 0)
        wanted = ((full & dense) | (jnp.logical_not(full) & sparse)) & jnp.logical_not(earlier)
        now = wanted & (used < QUOTA)
        plan[HELP_STEPS * TPB + i] = now.astype(jnp.int32)
        todo[n, b] = (wanted & jnp.logical_not(now)).astype(jnp.int32)
        return used + now.astype(jnp.int32)

    used = lax.fori_loop(0, HELP_STEPS * TPB, plan_help, jnp.int32(0))
    lax.fori_loop(0, OWN_STEPS * TPB, plan_own, used)

    def load_source(n):
        @pl.when(n < 3)
        def _():
            fill(scratch, panels, currents, 0, mirrored(even, n))

        @pl.when(n == 3)
        def _():
            fill(scratch, outer, outer, CROW, 0)

        @pl.when((n == 4) | (n == 5))
        def _():
            fill(scratch, far, far, CROW, n - 4)

        @pl.when((n == 6) | (n == 7))
        def _():
            fill(scratch, wing, wing, CROW, n - 6)

        @pl.when(n >= HELP_STEPS)
        def _():
            load_own(scratch, panels, currents, outer, mate, n - HELP_STEPS)

    engine(
        scratch,
        HELP_STEPS + OWN_STEPS,
        lambda n, b: plan[n * TPB + b] > 0,
        load_source,
        lambda n: jnp.where(n < 4, 0, jnp.where(n < 6, 1, jnp.where(n < 8, 2, 3))),
    )
    shift = jnp.where(even, 2, 0)
    write_out(out_near, acc, [b + shift for b in range(2)])
    shift_side = 2 - shift
    back = shift
    write_out(out_far, acc, [TPB + b + back for b in range(2)])
    write_out(out_wing, acc, [2 * TPB + b + shift_side for b in range(2)])
    write_out(out_own, acc, range(3 * TPB, 4 * TPB))


def rest_kernel(todo, test, panels, currents, outer, mate, after, out, *scratch):
    acc = scratch[12]
    fill_tests(scratch[1], 0, own_tests(test))
    clear(acc, TPB)
    engine(
        scratch,
        OWN_STEPS,
        lambda n, b: todo[n, b] > 0,
        lambda n: load_own(scratch, panels, currents, outer, mate, n),
        lambda n: 0,
    )
    write_out(out, acc, range(TPB))


def scratch_for(sets):
    return [
        pltpu.VMEM((GROWS, BLK), F32),
        pltpu.VMEM((sets, 7, 8, BLK), F32),
        pltpu.VMEM(((NTERM + 16) * 16, BLK), F32),
        pltpu.VMEM((TROWS * 8, BLK), F32),
        pltpu.VMEM((KDIM, NOUT * 256), BF16),
        pltpu.VMEM((NCH * MROWS, KDIM), BF16),
        pltpu.VMEM((MROWS + 8, NOUT * 256), F32),
        pltpu.VMEM((MROWS + 8, NOUT * 256), F32),
        pltpu.VMEM((6, BLK, BLK), F32),
        pltpu.VMEM((2 * BLK, 4 * BLK), BF16),
        pltpu.VMEM((4 * BLK, 4 * BLK), BF16),
        pltpu.VMEM((4 * BLK, 4 * BLK), BF16),
        pltpu.VMEM((sets * TPB, BLK, 4 * BLK), F32),
        pltpu.VMEM((8 * 16, BLK), F32),
        pltpu.SMEM((TPB,), jnp.int32),
    ]


def call(kernel, outs, operands, sets=0, tables=1, unread=0, tiles=1, table=(), copies=0):
    vmem = pl.BlockSpec(memory_space=pltpu.VMEM)
    smem = pl.BlockSpec(memory_space=pltpu.SMEM)
    anywhere = pl.BlockSpec(memory_space=pl.ANY)
    plain = len(operands) - tables - unread
    shapes = [jax.ShapeDtypeStruct(s, F32) for s in outs]
    specs = [vmem] * len(outs)
    scratch = scratch_for(sets) if sets else []
    if copies:
        scratch += [
            pltpu.VMEM((GROWS, TPB * BLK), F32),
            pltpu.VMEM((14, TPB * BLK), F32),
            pltpu.SemaphoreType.DMA((copies,)),
        ]
    if table:
        shapes.append(jax.ShapeDtypeStruct(table, jnp.int32))
        specs.append(smem)
        scratch.append(pltpu.SMEM(((HELP_STEPS + OWN_STEPS) * TPB,), jnp.int32))
    return pl.pallas_call(
        kernel,
        out_shape=shapes,
        in_specs=[smem] * tables + [vmem] * plain + [anywhere] * unread,
        out_specs=specs,
        scratch_shapes=scratch,
        compiler_params=pltpu.CompilerParams(vmem_limit_bytes=(60 if copies else 20) * 1024 * 1024),
        cost_estimate=pl.CostEstimate(flops=tiles * 5 * 10**9, bytes_accessed=4 * 10**6, transcendentals=0),
    )(*operands)


def body(panels, test_points, currents, near_mask):
    count = lax.axis_size("cluster") * lax.axis_size("narrow")
    axes = ("cluster", "narrow")
    swap = [(i, i ^ 1) for i in range(count)]
    across = [(i, (i - 1) % count if i % 2 == 0 else (i + 1) % count) for i in range(count)]
    away = [(i, (i - 2) % count if i % 2 == 0 else (i + 2) % count) for i in range(count)]
    across_wing = [(i, (i - 4) % count if i % 2 == 0 else (i + 4) % count) for i in range(count)]
    width = TPB * BLK
    wide = 4 * NRHS
    half = (wide, 2 * BLK)

    def reverse(pairs):
        return [(target, source) for source, target in pairs]

    mate, outer, far = call(
        pack_kernel,
        [(MATE_ROWS, 3 * BLK), (OUTER_ROWS, BLK), (FAR_ROWS, 2 * BLK)],
        [near_mask, panels, test_points, currents],
        unread=3,
        copies=PACK_COPIES,
    )
    outer = lax.ppermute(outer, axes, across)
    wing = lax.ppermute(far, axes, across_wing)
    far = lax.ppermute(far, axes, away)
    mate = lax.ppermute(mate, axes, swap)
    part, done = call(
        first_kernel, [(wide, width)], [near_mask, test_points, panels, currents], 1, tiles=5, table=(TPB, TPB)
    )
    to_near, to_far, to_wing, more, todo = call(
        second_kernel,
        [half, half, half, (wide, width)],
        [near_mask, done, test_points, panels, currents, outer, far, wing, mate],
        4,
        tables=2,
        tiles=7,
        table=(OWN_STEPS, TPB),
    )
    from_near = lax.ppermute(to_near, axes, across)
    from_far = lax.ppermute(to_far, axes, reverse(away))
    from_wing = lax.ppermute(to_wing, axes, reverse(across_wing))
    (rest,) = call(
        rest_kernel,
        [(wide, width)],
        [todo, test_points, panels, currents, outer, mate, to_near],
        1,
        unread=1,
        tiles=8,
    )
    even = lax.axis_index("narrow") == 0
    inner = from_near + from_wing
    helped = jnp.concatenate([jnp.where(even, inner, from_far), jnp.where(even, from_far, inner)], 1)
    return part + more + rest + helped


def solution(mesh):
    return jax.shard_map(
        body,
        mesh=mesh,
        in_specs=(
            P(None, ("cluster", "narrow")),
            P(None, ("cluster", "narrow")),
            P(None, ("cluster", "narrow")),
            P(("cluster", "narrow"), None),
        ),
        out_specs=P(None, ("cluster", "narrow")),
        check_vma=False,
    )
```

```python
import functools
import itertools
import math

import jax
import jax.numpy as jnp
from jax import lax
from jax.experimental import pallas as pl
from jax.experimental.pallas import tpu as pltpu
from jax.sharding import PartitionSpec as P

F32 = jnp.float32
BF16 = jnp.bfloat16
BLK = 128
QP = 14
REACH = 3
SPAN = 7
TPB = 4
GROWS = 98
NRHS = 128
SOFTEN = 0.04

Z_MAX = 14.0
DEGREE = 4
COS_HALF = (2.828426289053651, -0.35355064760758376, 0.007364148070439611, -6.107114702262049e-05, 2.4846120790492805e-07)
SIN_HALF = (1.4142135239177973, -0.05892543897495882, 0.0007364984722676873, -4.370137027858996e-06, 1.4053654408325383e-08)

TERMS = []
for _total in range(DEGREE + 1):
    for _j in range(_total + 1):
        _l = _total - _j
        for _a in itertools.product(range(_l + 1), repeat=3):
            if sum(_a) == _l:
                TERMS.append((_j, _a))
NTERM = 72
assert len(TERMS) <= NTERM
ONE = TERMS.index((0, (0, 0, 0)))
LIN = [TERMS.index((0, tuple(int(c == k) for c in range(3)))) for k in range(3)]
SQR = TERMS.index((1, (0, 0, 0)))
KDIM = 256
NOUT = 7
JC = 16
NCH = BLK // JC
MROWS = JC * QP


def powers_of(vec):
    one = None
    table = {(0, 0, 0): one}
    for total in range(1, DEGREE + 1):
        for a in itertools.product(range(total + 1), repeat=3):
            if sum(a) != total:
                continue
            axis = next(c for c in range(3) if a[c] > 0)
            prev = tuple(a[c] - (c == axis) for c in range(3))
            table[a] = vec[axis] if table[prev] is None else table[prev] * vec[axis]
    return table


def split2(value):
    high = value.astype(BF16).astype(F32)
    return high, value - high


def source_features(stage, fts, sf, centre, y):
    mono = powers_of(y)
    square = y[0] * y[0] + y[1] * y[1] + y[2] * y[2]
    sq = [None, square, square * square]
    sq.append(sq[2] * square)
    sq.append(sq[2] * sq[2])
    ones = jnp.ones_like(square)

    def put(row, value):
        fts[row * 16 : row * 16 + QP, :] = value

    for k, (j, a) in enumerate(TERMS):
        const = (-2.0) ** sum(a) / (math.prod(math.factorial(v) for v in a) * math.factorial(j))
        value = mono[a]
        if sq[j] is not None:
            value = sq[j] if value is None else value * sq[j]
        if value is None:
            value = ones
        put(k, value * const if const != 1.0 else value)
    base = NTERM
    s = [stage[(3 + c) * QP : (4 + c) * QP, :] for c in range(3)]
    d = stage[6 * QP : 7 * QP, :]
    for c in range(3):
        put(base + c, s[c])
    put(base + 3, d)
    for c in range(3):
        c1, c2 = (c + 1) % 3, (c + 2) % 3
        put(base + 4 + c, y[c1] * s[c2] - y[c2] * s[c1])
    extra = base + 8
    for half in range(2):
        for c in range(3):
            put(extra + 4 * half + c, y[c] * -2.0)
        put(extra + 4 * half + 3, square)
    rows = lax.broadcasted_iota(jnp.int32, (8, BLK), 0)
    for q in range(QP):
        main = fts[pl.ds(q, NTERM, stride=16), :]
        bil = fts[pl.ds(base * 16 + q, 8, stride=16), :]
        ext = fts[pl.ds(extra * 16 + q, 8, stride=16), :]
        mh, ml = split2(main)
        bh, bl = split2(bil)
        eh, rest = split2(ext)
        em, el = split2(rest)
        zrow = jnp.where(rows < 4, em, eh)
        zrow2 = jnp.where(rows < 4, el, jnp.where(rows == 4, 1.0, 0.0))
        full = jnp.concatenate([mh, mh, ml, bh, bh, bl, zrow, zrow2], 0)
        turned = full.astype(BF16).T
        for ch in range(NCH):
            sf[ch * MROWS + q * JC : ch * MROWS + (q + 1) * JC, :] = turned[ch * JC : (ch + 1) * JC, :]


def horner(coefs, m, w):
    der = [coefs[k] * math.factorial(k) / math.factorial(k - m) for k in range(m, len(coefs))]
    value = None
    for c in reversed(der):
        value = c if value is None else value * w + c
    return value


OFF_C, OFF_S, OFF_Z = 0, NTERM, 2 * NTERM
OFF_B = 3 * NTERM
OFF_E = OFF_B + 32
TROWS = OFF_E + 16


def test_features(xt, ftt, centre):
    x = [xt[c] - centre[c] for c in range(3)]
    t = [xt[3 + c] for c in range(3)]
    e = xt[6]
    w = x[0] * x[0] + x[1] * x[1] + x[2] * x[2] + SOFTEN
    mono = powers_of(x)

    def put(row, value):
        ftt[row * 8 : row * 8 + 8, :] = value

    for off, coefs in ((OFF_C, COS_HALF), (OFF_S, SIN_HALF)):
        der = [horner(coefs, m, w) for m in range(DEGREE + 1)]
        for k, (j, a) in enumerate(TERMS):
            level = der[j + sum(a)]
            value = level if mono[a] is None else mono[a] * level
            put(off + k, jnp.broadcast_to(value, w.shape))
    put(OFF_Z + ONE, w)
    put(OFF_Z + SQR, jnp.ones_like(w))
    for c in range(3):
        put(OFF_Z + LIN[c], x[c])
    charge = e * -0.25
    for c in range(3):
        put(OFF_B + c, t[c])
        put(OFF_B + 8 + c, t[c] * -2.0)
        put(OFF_B + 16 + c, t[c] * 1.5)
        c1, c2 = (c + 1) % 3, (c + 2) % 3
        put(OFF_B + 24 + c, (t[c1] * x[c2] - t[c2] * x[c1]) * -0.25)
        put(OFF_B + 28 + c, t[c] * 0.25)
    put(OFF_B + 3, charge)
    put(OFF_B + 11, charge)
    for half in range(2):
        for c in range(3):
            put(OFF_E + 4 * half + c, x[c])
        put(OFF_E + 4 * half + 3, jnp.ones_like(w))
    for c in range(4):
        put(OFF_E + 8 + c, x[c] if c < 3 else jnp.ones_like(w))
    put(OFF_E + 12, w)


def test_matrix(ftt, tf, b):
    rows = lax.broadcasted_iota(jnp.int32, (8, BLK), 0)
    zero8 = jnp.zeros((8, BLK), F32)
    for a in range(2):
        ba = 2 * b + a

        def take(off, n):
            return ftt[pl.ds(off * 8 + ba, n, stride=8), :]

        for out, off in ((0, OFF_Z), (1, OFF_C), (2, OFF_S)):
            high, low = split2(take(off, NTERM))
            lanes = slice(out * 256 + a * BLK, out * 256 + (a + 1) * BLK)
            tf[0:224, lanes] = jnp.concatenate([high, low, high, zero8], 0).astype(BF16)
        eh, rest = split2(take(OFF_E, 8))
        em, el = split2(rest)
        fh, rest2 = split2(take(OFF_E + 8, 8))
        fm, fl = split2(rest2)
        first = jnp.where(rows < 4, em, el)
        second = jnp.where(rows < 4, fh, jnp.where(rows == 4, fl, 0.0))
        tf[240:256, a * BLK : (a + 1) * BLK] = jnp.concatenate([first, second], 0).astype(BF16)
        for m in range(4):
            high, low = split2(take(OFF_B + 8 * m, 8))
            out = 3 + m
            lanes = slice(out * 256 + a * BLK, out * 256 + (a + 1) * BLK)
            tf[208:240, lanes] = jnp.concatenate([zero8, high, low, high], 0).astype(BF16)


EXP_RATE = -3.0 / math.log(2.0)


def pair_terms(z, cos_h, sin_h, k1, k2, k6, kk):
    inv = lax.rsqrt(z)
    dist = z * inv
    s0 = sin_h * dist
    c = 4.0 - s0 * s0
    s = s0 * cos_h
    c2 = c * c - 8.0
    s2 = c * s
    decay = jnp.exp2(dist * EXP_RATE)
    p = decay * c
    q = decay * s
    half = inv * 0.5
    c2r = c2 * half
    s2r = s2 * half
    pr = p * inv
    qr = q * inv
    weight = kk * (inv * inv)
    l1r = k1 * c2r
    l1i = k1 * s2r
    l2r = k2 * pr - k6 * qr
    l2i = k2 * qr + k6 * pr
    kr = weight * (((c2r + pr) + (s2 + 3.0 * p)) + q)
    ki = weight * (((s2r + qr) + (3.0 * q - c2)) - p)
    return l1r, l1i, l2r, l2i, kr, ki


AHEAD = 6


def fast_tile(ftt, tf, sf, bufs, ops, b, flag):
    test_matrix(ftt, tf, b)
    spare = pl.multiple_of(MROWS - 8 + 8 * flag, 8)

    def piece(chunk, buf, o):
        rows = pl.ds(pl.multiple_of(chunk * MROWS, 16), MROWS)
        lanes = slice(o * 256, (o + 1) * 256)
        buf[0:MROWS, lanes] = jnp.dot(sf[rows, :], tf[:, lanes], preferred_element_type=F32)

    def phase(chunk, buf, next_chunk, next_buf):
        work = [(g, q, a) for g in range(JC // 8) for q in range(QP) for a in range(2)]
        per = -(-len(work) // NOUT)
        acc, history = None, []
        for o in range(NOUT):
            if next_buf is not None:
                piece(next_chunk, next_buf, o)
            for g, q, a in work[o * per : (o + 1) * per]:
                if q == 0 and a == 0:
                    acc = None
                row = q * JC + g * 8
                if len(history) >= AHEAD:
                    buf[pl.ds(spare, 8), 0:BLK] = history[-AHEAD]
                vals = [buf[row : row + 8, k * 256 + a * BLK : k * 256 + (a + 1) * BLK] for k in range(NOUT)]
                terms = pair_terms(*vals)
                acc = list(terms) if acc is None else [u + v for u, v in zip(acc, terms)]
                history.append(acc[5])
                if q == QP - 1 and a == 1:
                    start = pl.multiple_of(chunk * JC + g * 8, 8)
                    for m in range(6):
                        ops[m, pl.ds(start, 8), :] = acc[m]

    for o in range(NOUT):
        piece(0, bufs[0], o)

    def step(n, carry):
        phase(2 * n, bufs[0], 2 * n + 1, bufs[1])
        phase(2 * n + 1, bufs[1], 2 * n + 2, bufs[0])
        return carry

    lax.fori_loop(0, NCH // 2 - 1, step, 0)
    phase(NCH - 2, bufs[0], NCH - 1, bufs[1])
    phase(NCH - 1, bufs[1], None, None)


def direct_tile(stage, raw, xt, ops, b):
    for c in range(7):
        raw[c * 16 : c * 16 + QP, :] = stage[c * QP : (c + 1) * QP, :]
    raw[7 * 16 : 8 * 16, :] = jnp.zeros((16, BLK), F32)
    for m in range(6):
        ops[m] = jnp.zeros((BLK, BLK), F32)

    def point(q, carry):
        rows8 = raw[pl.ds(q, 8, stride=16), :]
        turned = jnp.concatenate([rows8, jnp.zeros((BLK - 8, BLK), F32)], 0).T
        src = [turned[:, c : c + 1] for c in range(7)]

        def centroid(a, carry2):
            tst = [xt[c, pl.ds(2 * b + a, 1), :] for c in range(7)]
            dl = [tst[c] - src[c] for c in range(3)]
            dist = jnp.sqrt(dl[0] * dl[0] + dl[1] * dl[1] + dl[2] * dl[2] + SOFTEN)
            dotted = tst[3] * src[3] + tst[4] * src[4] + tst[5] * src[5]
            charge = tst[6] * src[6]
            crossed = (
                dl[0] * (src[4] * tst[5] - src[5] * tst[4])
                + dl[1] * (src[5] * tst[3] - src[3] * tst[5])
                + dl[2] * (src[3] * tst[4] - src[4] * tst[3])
            )
            scaled = crossed / (dist * dist)
            kr = ki = None
            for m, (wr, wi) in enumerate(((2.0, 0.0), (1.0, 3.0))):
                decay = jnp.exp(-wi * dist) / dist
                gr = decay * jnp.cos(wr * dist)
                gi = decay * jnp.sin(wr * dist)
                cr = (wr * wr - wi * wi) * dotted - charge
                ci = 2.0 * wr * wi * dotted
                ops[2 * m] += cr * gr - ci * gi
                ops[2 * m + 1] += cr * gi + ci * gr
                fr = -wi * dist - 1.0
                fi = wr * dist
                ops[4] += scaled * (fr * gr - fi * gi)
                ops[5] += scaled * (fr * gi + fi * gr)
            return carry2

        return lax.fori_loop(0, 2, centroid, carry)

    lax.fori_loop(0, QP, point, 0)


def apply_operators(ops, xs, wh, wl, acc, b):
    def put(ref, value, places):
        neg = -value
        for row, col, sign in places:
            ref[row * BLK : (row + 1) * BLK, col * BLK : (col + 1) * BLK] = value if sign > 0 else neg

    def both(value, places):
        high = value.astype(BF16)
        low = (value - high.astype(F32)).astype(BF16)
        put(wh, high, places)
        put(wl, low, places)

    l1r, l1i, l2r, l2i = (ops[m] for m in range(4))
    both(l1r + l2r, ((0, 0, 1), (1, 1, 1)))
    both(l1i + l2i, ((0, 1, 1), (1, 0, -1)))
    both(l1r + 0.5 * l2r, ((2, 2, 1), (3, 3, 1)))
    both(l1i + 0.5 * l2i, ((2, 3, 1), (3, 2, -1)))
    both(ops[4], ((0, 2, 1), (1, 3, 1), (2, 0, -1), (3, 1, -1)))
    both(ops[5], ((0, 3, 1), (1, 2, -1), (2, 1, -1), (3, 0, 1)))
    first = jnp.dot(xs[...], wh[...], preferred_element_type=F32)
    second = jnp.dot(xs[0:BLK, :], wl[...], preferred_element_type=F32)
    acc[b] += first[0:BLK] + first[BLK:] + second


CROW = 104
XROW = CROW + 4 * NRHS
OUTER_ROWS = XROW + 64 + 8
FAR_ROWS = XROW + 32 + 8
MATE_ROWS = XROW + 8
FULL = TPB * SPAN


def is_even():
    return lax.axis_index("narrow") == 0


def mirrored(even, block):
    return jnp.where(even, block, TPB - 1 - block)


def load_of(mask):
    total = mask[0, 0]
    for b in range(TPB):
        for c in range(SPAN):
            if b or c:
                total = total + mask[b, c]
    return total


def number(ref, row):
    return jnp.max(ref[row : row + 8, 0:BLK]).astype(jnp.int32)


def shares(load_near, load_far):
    goal = lax.div(FULL + load_near + load_far + 1, 3)
    near = jnp.clip(goal - load_near, 3, 7)
    far = jnp.clip(lax.div(FULL - near + load_far + 1, 2) - load_far, 0, 6)
    near = jnp.clip(lax.div(FULL - far + load_near + 1, 2) - load_near, 3, 7)
    return near, far


def is_near(u, v, share):
    option = jnp.where(u == -1, v, jnp.where(u == 0, 2 + v, FULL))
    return (u < -1) | ((v < 2) & (option < share - 3))


def is_far(u, v, share):
    return (v >= 2) & (jnp.where((u >= 1) & (u <= 3), 2 * (3 - u) + v - 2, FULL) < share)


PACK_COPIES = 5


def pack_kernel(mask, panels_at, test_at, currents, mate, outer, far, load, panels, test, sems):
    even = is_even()
    places = (
        (outer, 1, jnp.where(even, 0, 3 * BLK)),
        (far, 3, jnp.where(even, BLK, 0)),
        (mate, 3, jnp.where(even, BLK, 0)),
    )
    lanes = [pl.ds(pl.multiple_of(begin, BLK), count * BLK) for _, count, begin in places]
    copies = [pltpu.make_async_copy(panels_at, panels, sems.at[0]), pltpu.make_async_copy(test_at, test, sems.at[1])]
    for k in range(3):
        copies.append(pltpu.make_async_copy(currents.at[:, lanes[k]], places[k][0].at[CROW:XROW, :], sems.at[2 + k]))
    for each in copies:
        each.start()
    value = load_of(mask).astype(F32)
    outer[XROW + 64 : XROW + 72, :] = jnp.full((8, BLK), value, F32)
    far[XROW + 32 : XROW + 40, :] = jnp.full((8, 3 * BLK), value, F32)
    mate[XROW : XROW + 8, :] = jnp.full((8, 3 * BLK), value, F32)
    load[...] = jnp.full((8, BLK), value, F32)
    copies[0].wait()
    copies[1].wait()
    for k in range(3):
        places[k][0][0:GROWS, :] = panels[:, lanes[k]]
    for b in range(TPB):
        points = test[:, b * BLK : (b + 1) * BLK]
        outer[XROW + 16 * b : XROW + 16 * b + 14, :] = points
        row = XROW + 16 * (b // 3)
        far[row : row + 14, (b % 3) * BLK : (b % 3 + 1) * BLK] = points
    for each in copies[2:]:
        each.wait()


def engine(scratch, steps, wanted, load_source, accset):
    stage, xt, fts, ftt, tf, sf, buf0, buf1, ops, xs, wh, wl, acc, raw, flags = scratch

    def source(n, carry):
        any_wanted = wanted(n, 0)
        for b in range(1, TPB):
            any_wanted = any_wanted | wanted(n, b)

        @pl.when(any_wanted)
        def _():
            load_source(n)
            points = xt.at[accset(n)]
            place = [stage[c * QP : (c + 1) * QP, :] for c in range(3)]
            low = [jnp.min(jnp.min(v, 0, keepdims=True), 1, keepdims=True) for v in place]
            high = [jnp.max(jnp.max(v, 0, keepdims=True), 1, keepdims=True) for v in place]
            centre = [(u + v) * 0.5 for u, v in zip(low, high)]
            bound = jnp.full((8, BLK), SOFTEN, F32)
            for c in range(3):
                far = jnp.maximum(jnp.abs(points[c] - low[c]), jnp.abs(points[c] - high[c]))
                bound = bound + far * far
            for b in range(TPB):
                flags[b] = (jnp.max(bound[2 * b : 2 * b + 2]) <= Z_MAX).astype(jnp.int32)
            source_features(stage, fts, sf, centre, [place[c] - centre[c] for c in range(3)])
            test_features(points, ftt, centre)

            def tile(b, carry2):
                @pl.when(wanted(n, b))
                def _():
                    @pl.when(flags[b] > 0)
                    def _():
                        fast_tile(ftt, tf, sf, (buf0, buf1), ops, b, flags[b])

                    @pl.when(flags[b] == 0)
                    def _():
                        direct_tile(stage, raw, points, ops, b)

                    apply_operators(ops, xs, wh, wl, acc, TPB * accset(n) + b)

                return carry2

            lax.fori_loop(0, TPB, tile, 0)

        return carry

    tf[...] = jnp.zeros_like(tf)
    ftt[...] = jnp.zeros_like(ftt)
    fts[...] = jnp.zeros_like(fts)
    lax.fori_loop(0, steps, source, 0)


def fill(scratch, pan, cur, row, slot):
    stage, xs = scratch[0], scratch[9]
    lanes = pl.ds(pl.multiple_of(slot * BLK, BLK), BLK)
    stage[...] = pan[0:GROWS, lanes]
    for g in range(4):
        value = cur[row + g * NRHS : row + (g + 1) * NRHS, lanes]
        high = value.astype(BF16)
        xs[0:BLK, g * BLK : (g + 1) * BLK] = high
        xs[BLK : 2 * BLK, g * BLK : (g + 1) * BLK] = (value - high.astype(F32)).astype(BF16)


def fill_tests(xt, which, blocks):
    for c in range(7):
        for b in range(TPB):
            xt[which, c, 2 * b : 2 * b + 2, :] = blocks(b, 2 * c)


def own_tests(test):
    return lambda b, row: test[row : row + 2, b * BLK : (b + 1) * BLK]


def clear(acc, count):
    for b in range(count):
        acc[b] = jnp.zeros((BLK, 4 * BLK), F32)


def write_out(out, acc, blocks):
    for col, b in enumerate(blocks):
        for g in range(4):
            out[g * NRHS : (g + 1) * NRHS, col * BLK : (col + 1) * BLK] = acc[b, :, g * BLK : (g + 1) * BLK]


FIRST = 5


def first_kernel(mask, test, panels, currents, out, done, *scratch):
    scratch = scratch[:-1]
    even = is_even()
    full = load_of(mask) == FULL
    fill_tests(scratch[1], 0, own_tests(test))
    clear(scratch[12], TPB)

    def plan(i, used):
        n, b = lax.div(i, TPB), lax.rem(i, TPB)
        u, v = mirrored(even, n), mirrored(even, b)
        dense = (u > 0) & (v < 2)
        wanted = (full & dense) | (jnp.logical_not(full) & (mask[b, n - b + REACH] > 0))
        now = wanted & (used < FIRST)
        done[n, b] = now.astype(jnp.int32)
        return used + now.astype(jnp.int32)

    lax.fori_loop(0, TPB * TPB, plan, jnp.int32(0))
    engine(scratch, TPB, lambda n, b: done[n, b] > 0, lambda n: fill(scratch, panels, currents, 0, n), lambda n: 0)
    write_out(out, scratch[12], range(TPB))


QUOTA = 7
HELP_STEPS = 7
OWN_STEPS = 8


def own_place(even, n):
    return jnp.where(n < 4, n, jnp.where(n == 4, jnp.where(even, -1, 4), jnp.where(even, n - 1, n - 8)))


def load_own(scratch, panels, currents, outer, mate, n):
    @pl.when(n < 4)
    def _():
        fill(scratch, panels, currents, 0, n)

    @pl.when(n == 4)
    def _():
        fill(scratch, outer, outer, CROW, 0)

    @pl.when(n > 4)
    def _():
        fill(scratch, mate, mate, CROW, n - 5)


def second_kernel(
    mask, done, test, panels, currents, outer, far, mate, load_far, out_near, out_far, out_own, todo, *scratch
):
    plan, scratch = scratch[-1], scratch[:-1]
    even = is_even()
    odd = jnp.logical_not(even)
    own_load, mate_load = load_of(mask), number(mate, XROW)
    near_load, far_load = number(outer, XROW + 64), number(far, XROW + 32)
    share_near, _ = shares(own_load, mate_load)
    _, share_far = shares(mate_load, own_load)
    give_near, give_far = shares(near_load, number(load_far, 0))
    full = own_load == FULL
    xt, acc = scratch[1], scratch[12]
    fill_tests(xt, 0, lambda b, row: outer[XROW + 16 * b + row : XROW + 16 * b + row + 2, :])
    fill_tests(
        xt,
        1,
        lambda b, row: far[
            XROW + 16 * (b // 3) + row : XROW + 16 * (b // 3) + row + 2, (b % 3) * BLK : (b % 3 + 1) * BLK
        ],
    )
    fill_tests(xt, 2, own_tests(test))
    clear(acc, 3 * TPB)

    def plan_help(i, used):
        n, b = lax.div(i, TPB), lax.rem(i, TPB)
        v_near, v_far = mirrored(odd, b), mirrored(even, b)
        u_near, u_far = jnp.where(n == 3, 0, -1 - n), jnp.where(even, n - 3, 7 - n)
        of_near = (n < 4) & (v_near - u_near <= REACH) & is_near(u_near, v_near, share_near)
        of_far = (n >= 4) & is_far(u_far, v_far, share_far)
        wanted = ((near_load == FULL) & of_near) | ((far_load == FULL) & of_far)
        plan[i] = wanted.astype(jnp.int32)
        return used + wanted.astype(jnp.int32)

    def plan_own(i, used):
        n, b = lax.div(i, TPB), lax.rem(i, TPB)
        rel = own_place(even, n)
        column = rel - b + REACH
        inside = (column >= 0) & (column < SPAN)
        sparse = inside & (mask[b, jnp.clip(column, 0, SPAN - 1)] > 0)
        u, v = mirrored(even, rel), mirrored(even, b)
        dense = inside & jnp.logical_not(is_near(u, v, give_near) | is_far(u, v, give_far))
        earlier = (n < TPB) & (done[jnp.minimum(n, TPB - 1), b] > 0)
        wanted = ((full & dense) | (jnp.logical_not(full) & sparse)) & jnp.logical_not(earlier)
        now = wanted & (used < QUOTA)
        plan[HELP_STEPS * TPB + i] = now.astype(jnp.int32)
        todo[n, b] = (wanted & jnp.logical_not(now)).astype(jnp.int32)
        return used + now.astype(jnp.int32)

    used = lax.fori_loop(0, HELP_STEPS * TPB, plan_help, jnp.int32(0))
    lax.fori_loop(0, OWN_STEPS * TPB, plan_own, used)

    def load_source(n):
        @pl.when(n < 3)
        def _():
            fill(scratch, panels, currents, 0, mirrored(even, n))

        @pl.when(n == 3)
        def _():
            fill(scratch, outer, outer, CROW, 0)

        @pl.when((n > 3) & (n < HELP_STEPS))
        def _():
            fill(scratch, far, far, CROW, n - 4)

        @pl.when(n >= HELP_STEPS)
        def _():
            load_own(scratch, panels, currents, outer, mate, n - HELP_STEPS)

    engine(
        scratch,
        HELP_STEPS + OWN_STEPS,
        lambda n, b: plan[n * TPB + b] > 0,
        load_source,
        lambda n: jnp.where(n < 4, 0, jnp.where(n < HELP_STEPS, 1, 2)),
    )
    shift = jnp.where(even, 2, 0)
    write_out(out_near, acc, [b + shift for b in range(2)])
    write_out(out_far, acc, [TPB + b + shift for b in range(2)])
    write_out(out_own, acc, range(2 * TPB, 3 * TPB))


def rest_kernel(todo, test, panels, currents, outer, mate, after, out, *scratch):
    acc = scratch[12]
    fill_tests(scratch[1], 0, own_tests(test))
    clear(acc, TPB)
    engine(
        scratch,
        OWN_STEPS,
        lambda n, b: todo[n, b] > 0,
        lambda n: load_own(scratch, panels, currents, outer, mate, n),
        lambda n: 0,
    )
    write_out(out, acc, range(TPB))


def scratch_for(sets):
    return [
        pltpu.VMEM((GROWS, BLK), F32),
        pltpu.VMEM((sets, 7, 8, BLK), F32),
        pltpu.VMEM(((NTERM + 16) * 16, BLK), F32),
        pltpu.VMEM((TROWS * 8, BLK), F32),
        pltpu.VMEM((KDIM, NOUT * 256), BF16),
        pltpu.VMEM((NCH * MROWS, KDIM), BF16),
        pltpu.VMEM((MROWS + 8, NOUT * 256), F32),
        pltpu.VMEM((MROWS + 8, NOUT * 256), F32),
        pltpu.VMEM((6, BLK, BLK), F32),
        pltpu.VMEM((2 * BLK, 4 * BLK), BF16),
        pltpu.VMEM((4 * BLK, 4 * BLK), BF16),
        pltpu.VMEM((4 * BLK, 4 * BLK), BF16),
        pltpu.VMEM((sets * TPB, BLK, 4 * BLK), F32),
        pltpu.VMEM((8 * 16, BLK), F32),
        pltpu.SMEM((TPB,), jnp.int32),
    ]


def call(kernel, outs, operands, sets=0, tables=1, unread=0, tiles=1, table=(), copies=0):
    vmem = pl.BlockSpec(memory_space=pltpu.VMEM)
    smem = pl.BlockSpec(memory_space=pltpu.SMEM)
    anywhere = pl.BlockSpec(memory_space=pl.ANY)
    plain = len(operands) - tables - unread
    shapes = [jax.ShapeDtypeStruct(s, F32) for s in outs]
    specs = [vmem] * len(outs)
    scratch = scratch_for(sets) if sets else []
    if copies:
        scratch += [
            pltpu.VMEM((GROWS, TPB * BLK), F32),
            pltpu.VMEM((14, TPB * BLK), F32),
            pltpu.SemaphoreType.DMA((copies,)),
        ]
    if table:
        shapes.append(jax.ShapeDtypeStruct(table, jnp.int32))
        specs.append(smem)
        scratch.append(pltpu.SMEM(((HELP_STEPS + OWN_STEPS) * TPB,), jnp.int32))
    return pl.pallas_call(
        kernel,
        out_shape=shapes,
        in_specs=[smem] * tables + [vmem] * plain + [anywhere] * unread,
        out_specs=specs,
        scratch_shapes=scratch,
        compiler_params=pltpu.CompilerParams(vmem_limit_bytes=(60 if copies else 20) * 1024 * 1024),
        cost_estimate=pl.CostEstimate(flops=tiles * 5 * 10**9, bytes_accessed=4 * 10**6, transcendentals=0),
    )(*operands)


def body(panels, test_points, currents, near_mask):
    count = lax.axis_size("cluster") * lax.axis_size("narrow")
    axes = ("cluster", "narrow")
    swap = [(i, i ^ 1) for i in range(count)]
    across = [(i, (i - 1) % count if i % 2 == 0 else (i + 1) % count) for i in range(count)]
    away = [(i, (i - 2) % count if i % 2 == 0 else (i + 2) % count) for i in range(count)]
    back = [(target, source) for source, target in away]
    width = TPB * BLK
    wide = 4 * NRHS
    mate, outer, far, load = call(
        pack_kernel,
        [(MATE_ROWS, 3 * BLK), (OUTER_ROWS, BLK), (FAR_ROWS, 3 * BLK), (8, BLK)],
        [near_mask, panels, test_points, currents],
        unread=3,
        copies=PACK_COPIES,
    )
    load_far = lax.ppermute(load, axes, back)
    outer = lax.ppermute(outer, axes, across)
    far = lax.ppermute(far, axes, away)
    mate = lax.ppermute(mate, axes, swap)
    part, done = call(
        first_kernel, [(wide, width)], [near_mask, test_points, panels, currents], 1, tiles=5, table=(TPB, TPB)
    )
    to_near, to_far, more, todo = call(
        second_kernel,
        [(wide, 2 * BLK), (wide, 2 * BLK), (wide, width)],
        [near_mask, done, test_points, panels, currents, outer, far, mate, load_far],
        3,
        tables=2,
        tiles=7,
        table=(OWN_STEPS, TPB),
    )
    from_near = lax.ppermute(to_near, axes, across)
    from_far = lax.ppermute(to_far, axes, back)
    (rest,) = call(
        rest_kernel,
        [(wide, width)],
        [todo, test_points, panels, currents, outer, mate, to_near],
        1,
        unread=1,
        tiles=8,
    )
    even = lax.axis_index("narrow") == 0
    helped = jnp.concatenate([jnp.where(even, from_near, from_far), jnp.where(even, from_far, from_near)], 1)
    return part + more + rest + helped


def solution(mesh):
    return jax.shard_map(
        body,
        mesh=mesh,
        in_specs=(
            P(None, ("cluster", "narrow")),
            P(None, ("cluster", "narrow")),
            P(None, ("cluster", "narrow")),
            P(("cluster", "narrow"), None),
        ),
        out_specs=P(None, ("cluster", "narrow")),
        check_vma=False,
    )
```

```python
import functools
import itertools
import math

import jax
import jax.numpy as jnp
from jax import lax
from jax.experimental import pallas as pl
from jax.experimental.pallas import tpu as pltpu
from jax.sharding import PartitionSpec as P

F32 = jnp.float32
BF16 = jnp.bfloat16
BLK = 128
QP = 14
REACH = 3
SPAN = 7
TPB = 4
GROWS = 98
NRHS = 128
SOFTEN = 0.04

Z_MAX = 14.0
DEGREE = 4
COS_HALF = (2.828426289053651, -0.35355064760758376, 0.007364148070439611, -6.107114702262049e-05, 2.4846120790492805e-07)
SIN_HALF = (1.4142135239177973, -0.05892543897495882, 0.0007364984722676873, -4.370137027858996e-06, 1.4053654408325383e-08)

TERMS = []
for _total in range(DEGREE + 1):
    for _j in range(_total + 1):
        _l = _total - _j
        for _a in itertools.product(range(_l + 1), repeat=3):
            if sum(_a) == _l:
                TERMS.append((_j, _a))
NTERM = 72
assert len(TERMS) <= NTERM
ONE = TERMS.index((0, (0, 0, 0)))
LIN = [TERMS.index((0, tuple(int(c == k) for c in range(3)))) for k in range(3)]
SQR = TERMS.index((1, (0, 0, 0)))
KDIM = 256
NOUT = 7
JC = 16
NCH = BLK // JC
MROWS = JC * QP


def powers_of(vec):
    one = None
    table = {(0, 0, 0): one}
    for total in range(1, DEGREE + 1):
        for a in itertools.product(range(total + 1), repeat=3):
            if sum(a) != total:
                continue
            axis = next(c for c in range(3) if a[c] > 0)
            prev = tuple(a[c] - (c == axis) for c in range(3))
            table[a] = vec[axis] if table[prev] is None else table[prev] * vec[axis]
    return table


def split2(value):
    high = value.astype(BF16).astype(F32)
    return high, value - high


def source_features(stage, fts, sf, centre, y):
    mono = powers_of(y)
    square = y[0] * y[0] + y[1] * y[1] + y[2] * y[2]
    sq = [None, square, square * square]
    sq.append(sq[2] * square)
    sq.append(sq[2] * sq[2])
    ones = jnp.ones_like(square)

    def put(row, value):
        fts[row * 16 : row * 16 + QP, :] = value

    for k, (j, a) in enumerate(TERMS):
        const = (-2.0) ** sum(a) / (math.prod(math.factorial(v) for v in a) * math.factorial(j))
        value = mono[a]
        if sq[j] is not None:
            value = sq[j] if value is None else value * sq[j]
        if value is None:
            value = ones
        put(k, value * const if const != 1.0 else value)
    base = NTERM
    s = [stage[(3 + c) * QP : (4 + c) * QP, :] for c in range(3)]
    d = stage[6 * QP : 7 * QP, :]
    for c in range(3):
        put(base + c, s[c])
    put(base + 3, d)
    for c in range(3):
        c1, c2 = (c + 1) % 3, (c + 2) % 3
        put(base + 4 + c, y[c1] * s[c2] - y[c2] * s[c1])
    extra = base + 8
    for half in range(2):
        for c in range(3):
            put(extra + 4 * half + c, y[c] * -2.0)
        put(extra + 4 * half + 3, square)
    rows = lax.broadcasted_iota(jnp.int32, (8, BLK), 0)
    for q in range(QP):
        main = fts[pl.ds(q, NTERM, stride=16), :]
        bil = fts[pl.ds(base * 16 + q, 8, stride=16), :]
        ext = fts[pl.ds(extra * 16 + q, 8, stride=16), :]
        mh, ml = split2(main)
        bh, bl = split2(bil)
        eh, rest = split2(ext)
        em, el = split2(rest)
        zrow = jnp.where(rows < 4, em, eh)
        zrow2 = jnp.where(rows < 4, el, jnp.where(rows == 4, 1.0, 0.0))
        full = jnp.concatenate([mh, mh, ml, bh, bh, bl, zrow, zrow2], 0)
        turned = full.astype(BF16).T
        for ch in range(NCH):
            sf[ch * MROWS + q * JC : ch * MROWS + (q + 1) * JC, :] = turned[ch * JC : (ch + 1) * JC, :]


def horner(coefs, m, w):
    der = [coefs[k] * math.factorial(k) / math.factorial(k - m) for k in range(m, len(coefs))]
    value = None
    for c in reversed(der):
        value = c if value is None else value * w + c
    return value


OFF_C, OFF_S, OFF_Z = 0, NTERM, 2 * NTERM
OFF_B = 3 * NTERM
OFF_E = OFF_B + 32
TROWS = OFF_E + 16


def test_features(xt, ftt, centre):
    x = [xt[c] - centre[c] for c in range(3)]
    t = [xt[3 + c] for c in range(3)]
    e = xt[6]
    w = x[0] * x[0] + x[1] * x[1] + x[2] * x[2] + SOFTEN
    mono = powers_of(x)

    def put(row, value):
        ftt[row * 8 : row * 8 + 8, :] = value

    for off, coefs in ((OFF_C, COS_HALF), (OFF_S, SIN_HALF)):
        der = [horner(coefs, m, w) for m in range(DEGREE + 1)]
        for k, (j, a) in enumerate(TERMS):
            level = der[j + sum(a)]
            value = level if mono[a] is None else mono[a] * level
            put(off + k, jnp.broadcast_to(value, w.shape))
    put(OFF_Z + ONE, w)
    put(OFF_Z + SQR, jnp.ones_like(w))
    for c in range(3):
        put(OFF_Z + LIN[c], x[c])
    charge = e * -0.25
    for c in range(3):
        put(OFF_B + c, t[c])
        put(OFF_B + 8 + c, t[c] * -2.0)
        put(OFF_B + 16 + c, t[c] * 1.5)
        c1, c2 = (c + 1) % 3, (c + 2) % 3
        put(OFF_B + 24 + c, (t[c1] * x[c2] - t[c2] * x[c1]) * -0.25)
        put(OFF_B + 28 + c, t[c] * 0.25)
    put(OFF_B + 3, charge)
    put(OFF_B + 11, charge)
    for half in range(2):
        for c in range(3):
            put(OFF_E + 4 * half + c, x[c])
        put(OFF_E + 4 * half + 3, jnp.ones_like(w))
    for c in range(4):
        put(OFF_E + 8 + c, x[c] if c < 3 else jnp.ones_like(w))
    put(OFF_E + 12, w)


def test_matrix(ftt, tf, b):
    rows = lax.broadcasted_iota(jnp.int32, (8, BLK), 0)
    zero8 = jnp.zeros((8, BLK), F32)
    for a in range(2):
        ba = 2 * b + a

        def take(off, n):
            return ftt[pl.ds(off * 8 + ba, n, stride=8), :]

        for out, off in ((0, OFF_Z), (1, OFF_C), (2, OFF_S)):
            high, low = split2(take(off, NTERM))
            lanes = slice(out * 256 + a * BLK, out * 256 + (a + 1) * BLK)
            tf[0:224, lanes] = jnp.concatenate([high, low, high, zero8], 0).astype(BF16)
        eh, rest = split2(take(OFF_E, 8))
        em, el = split2(rest)
        fh, rest2 = split2(take(OFF_E + 8, 8))
        fm, fl = split2(rest2)
        first = jnp.where(rows < 4, em, el)
        second = jnp.where(rows < 4, fh, jnp.where(rows == 4, fl, 0.0))
        tf[240:256, a * BLK : (a + 1) * BLK] = jnp.concatenate([first, second], 0).astype(BF16)
        for m in range(4):
            high, low = split2(take(OFF_B + 8 * m, 8))
            out = 3 + m
            lanes = slice(out * 256 + a * BLK, out * 256 + (a + 1) * BLK)
            tf[208:240, lanes] = jnp.concatenate([zero8, high, low, high], 0).astype(BF16)


EXP_RATE = -3.0 / math.log(2.0)


def pair_terms(z, cos_h, sin_h, k1, k2, k6, kk):
    inv = lax.rsqrt(z)
    dist = z * inv
    s0 = sin_h * dist
    c = 4.0 - s0 * s0
    s = s0 * cos_h
    c2 = c * c - 8.0
    s2 = c * s
    decay = jnp.exp2(dist * EXP_RATE)
    p = decay * c
    q = decay * s
    half = inv * 0.5
    c2r = c2 * half
    s2r = s2 * half
    pr = p * inv
    qr = q * inv
    weight = kk * (inv * inv)
    l1r = k1 * c2r
    l1i = k1 * s2r
    l2r = k2 * pr - k6 * qr
    l2i = k2 * qr + k6 * pr
    inv3 = inv + 3.0
    kr = weight * ((c2r + s2) + (p * inv3 + q))
    ki = weight * ((s2r - c2) + (q * inv3 - p))
    return l1r, l1i, l2r, l2i, kr, ki


AHEAD = 6


def fast_tile(ftt, tf, sf, bufs, ops, b, flag):
    test_matrix(ftt, tf, b)
    spare = pl.multiple_of(MROWS - 8 + 8 * flag, 8)

    def piece(chunk, buf, o):
        rows = pl.ds(pl.multiple_of(chunk * MROWS, 16), MROWS)
        lanes = slice(o * 256, (o + 1) * 256)
        buf[0:MROWS, lanes] = jnp.dot(sf[rows, :], tf[:, lanes], preferred_element_type=F32)

    def phase(chunk, buf, next_chunk, next_buf):
        work = [(g, q, a) for g in range(JC // 8) for q in range(QP) for a in range(2)]
        per = -(-len(work) // NOUT)
        acc, history = None, []
        for o in range(NOUT):
            if next_buf is not None:
                piece(next_chunk, next_buf, o)
            for g, q, a in work[o * per : (o + 1) * per]:
                if q == 0 and a == 0:
                    acc = None
                row = q * JC + g * 8
                if len(history) >= AHEAD and len(history) % 2 == 0:
                    buf[pl.ds(spare, 8), 0:BLK] = history[-AHEAD]
                vals = [buf[row : row + 8, k * 256 + a * BLK : k * 256 + (a + 1) * BLK] for k in range(NOUT)]
                terms = pair_terms(*vals)
                acc = list(terms) if acc is None else [u + v for u, v in zip(acc, terms)]
                history.append(acc[5])
                if q == QP - 1 and a == 1:
                    start = pl.multiple_of(chunk * JC + g * 8, 8)
                    for m in range(6):
                        ops[m, pl.ds(start, 8), :] = acc[m]

    for o in range(NOUT):
        piece(0, bufs[0], o)

    def step(n, carry):
        phase(2 * n, bufs[0], 2 * n + 1, bufs[1])
        phase(2 * n + 1, bufs[1], 2 * n + 2, bufs[0])
        return carry

    lax.fori_loop(0, NCH // 2 - 1, step, 0)
    phase(NCH - 2, bufs[0], NCH - 1, bufs[1])
    phase(NCH - 1, bufs[1], None, None)


def direct_tile(stage, raw, xt, ops, b):
    for c in range(7):
        raw[c * 16 : c * 16 + QP, :] = stage[c * QP : (c + 1) * QP, :]
    raw[7 * 16 : 8 * 16, :] = jnp.zeros((16, BLK), F32)
    for m in range(6):
        ops[m] = jnp.zeros((BLK, BLK), F32)

    def point(q, carry):
        rows8 = raw[pl.ds(q, 8, stride=16), :]
        turned = jnp.concatenate([rows8, jnp.zeros((BLK - 8, BLK), F32)], 0).T
        src = [turned[:, c : c + 1] for c in range(7)]

        def centroid(a, carry2):
            tst = [xt[c, pl.ds(2 * b + a, 1), :] for c in range(7)]
            dl = [tst[c] - src[c] for c in range(3)]
            dist = jnp.sqrt(dl[0] * dl[0] + dl[1] * dl[1] + dl[2] * dl[2] + SOFTEN)
            dotted = tst[3] * src[3] + tst[4] * src[4] + tst[5] * src[5]
            charge = tst[6] * src[6]
            crossed = (
                dl[0] * (src[4] * tst[5] - src[5] * tst[4])
                + dl[1] * (src[5] * tst[3] - src[3] * tst[5])
                + dl[2] * (src[3] * tst[4] - src[4] * tst[3])
            )
            scaled = crossed / (dist * dist)
            kr = ki = None
            for m, (wr, wi) in enumerate(((2.0, 0.0), (1.0, 3.0))):
                decay = jnp.exp(-wi * dist) / dist
                gr = decay * jnp.cos(wr * dist)
                gi = decay * jnp.sin(wr * dist)
                cr = (wr * wr - wi * wi) * dotted - charge
                ci = 2.0 * wr * wi * dotted
                ops[2 * m] += cr * gr - ci * gi
                ops[2 * m + 1] += cr * gi + ci * gr
                fr = -wi * dist - 1.0
                fi = wr * dist
                ops[4] += scaled * (fr * gr - fi * gi)
                ops[5] += scaled * (fr * gi + fi * gr)
            return carry2

        return lax.fori_loop(0, 2, centroid, carry)

    lax.fori_loop(0, QP, point, 0)


def apply_operators(ops, xs, wh, wl, acc, b):
    def put(ref, value, places):
        neg = -value
        for row, col, sign in places:
            ref[row * BLK : (row + 1) * BLK, col * BLK : (col + 1) * BLK] = value if sign > 0 else neg

    def both(value, places):
        high = value.astype(BF16)
        low = (value - high.astype(F32)).astype(BF16)
        put(wh, high, places)
        put(wl, low, places)

    l1r, l1i, l2r, l2i = (ops[m] for m in range(4))
    both(l1r + l2r, ((0, 0, 1), (1, 1, 1)))
    both(l1i + l2i, ((0, 1, 1), (1, 0, -1)))
    both(l1r + 0.5 * l2r, ((2, 2, 1), (3, 3, 1)))
    both(l1i + 0.5 * l2i, ((2, 3, 1), (3, 2, -1)))
    both(ops[4], ((0, 2, 1), (1, 3, 1), (2, 0, -1), (3, 1, -1)))
    both(ops[5], ((0, 3, 1), (1, 2, -1), (2, 1, -1), (3, 0, 1)))
    first = jnp.dot(xs[...], wh[...], preferred_element_type=F32)
    second = jnp.dot(xs[0:BLK, :], wl[...], preferred_element_type=F32)
    acc[b] += first[0:BLK] + first[BLK:] + second


CROW = 104
XROW = CROW + 4 * NRHS
OUTER_ROWS = XROW + 64 + 8
FAR_ROWS = XROW + 32 + 8
MATE_ROWS = XROW + 8
FULL = TPB * SPAN


def is_even():
    return lax.axis_index("narrow") == 0


def mirrored(even, block):
    return jnp.where(even, block, TPB - 1 - block)


def load_of(mask):
    total = mask[0, 0]
    for b in range(TPB):
        for c in range(SPAN):
            if b or c:
                total = total + mask[b, c]
    return total


def number(ref, row):
    return jnp.max(ref[row : row + 8, 0:BLK]).astype(jnp.int32)


def shares(load_near, load_far):
    goal = lax.div(FULL + load_near + load_far + 1, 3)
    near = jnp.clip(goal - load_near, 3, 7)
    far = jnp.clip(lax.div(FULL - near + load_far + 1, 2) - load_far, 0, 6)
    near = jnp.clip(lax.div(FULL - far + load_near + 1, 2) - load_near, 3, 7)
    return near, far


def is_near(u, v, share):
    option = jnp.where(u == -1, v, jnp.where(u == 0, 2 + v, FULL))
    return (u < -1) | ((v < 2) & (option < share - 3))


def is_far(u, v, share):
    return (v >= 2) & (jnp.where((u >= 1) & (u <= 3), 2 * (3 - u) + v - 2, FULL) < share)


PACK_COPIES = 11


def pack_kernel(
    mask, panels_at, test_at, currents, mate, outer, far, load, panels, test, geo, outer_end, far_end, mate_end, sems
):
    even = is_even()
    places = (
        (outer, 1, jnp.where(even, 0, 3 * BLK)),
        (far, 3, jnp.where(even, BLK, 0)),
        (mate, 3, jnp.where(even, BLK, 0)),
    )
    lanes = [pl.ds(pl.multiple_of(begin, BLK), count * BLK) for _, count, begin in places]
    copies = []

    def copy(source, target):
        copies.append(pltpu.make_async_copy(source, target, sems.at[len(copies)]))
        copies[-1].start()

    copy(panels_at, panels)
    copy(test_at, test)
    for k in range(3):
        copy(currents.at[:, lanes[k]], places[k][0].at[CROW:XROW, :])
    value = load_of(mask).astype(F32)
    load[...] = jnp.full((8, BLK), value, F32)
    mate_end[...] = jnp.full((8, 3 * BLK), value, F32)
    copy(mate_end, mate.at[XROW:MATE_ROWS, :])
    outer_end[0:64, :] = jnp.zeros((64, BLK), F32)
    outer_end[64:72, :] = jnp.full((8, BLK), value, F32)
    far_end[0:32, :] = jnp.zeros((32, 3 * BLK), F32)
    far_end[32:40, :] = jnp.full((8, 3 * BLK), value, F32)
    geo[GROWS - 2 : CROW, :] = jnp.zeros((CROW - GROWS + 2, TPB * BLK), F32)
    copies[0].wait()
    geo[0:GROWS, :] = panels[...]
    for k in range(3):
        copy(geo.at[:, lanes[k]], places[k][0].at[0:CROW, :])
    copies[1].wait()
    for b in range(TPB):
        points = test[:, b * BLK : (b + 1) * BLK]
        outer_end[16 * b : 16 * b + 14, :] = points
        row = 16 * (b // 3)
        far_end[row : row + 14, (b % 3) * BLK : (b % 3 + 1) * BLK] = points
    copy(outer_end, outer.at[XROW:OUTER_ROWS, :])
    copy(far_end, far.at[XROW:FAR_ROWS, :])
    for each in copies[2:]:
        each.wait()


def engine(scratch, steps, wanted, load_source, accset):
    stage, xt, fts, ftt, tf, sf, buf0, buf1, ops, xs, wh, wl, acc, raw, flags = scratch

    def source(n, carry):
        any_wanted = wanted(n, 0)
        for b in range(1, TPB):
            any_wanted = any_wanted | wanted(n, b)

        @pl.when(any_wanted)
        def _():
            load_source(n)
            points = xt.at[accset(n)]
            place = [stage[c * QP : (c + 1) * QP, :] for c in range(3)]
            low = [jnp.min(jnp.min(v, 0, keepdims=True), 1, keepdims=True) for v in place]
            high = [jnp.max(jnp.max(v, 0, keepdims=True), 1, keepdims=True) for v in place]
            centre = [(u + v) * 0.5 for u, v in zip(low, high)]
            bound = jnp.full((8, BLK), SOFTEN, F32)
            for c in range(3):
                far = jnp.maximum(jnp.abs(points[c] - low[c]), jnp.abs(points[c] - high[c]))
                bound = bound + far * far
            for b in range(TPB):
                flags[b] = (jnp.max(bound[2 * b : 2 * b + 2]) <= Z_MAX).astype(jnp.int32)
            source_features(stage, fts, sf, centre, [place[c] - centre[c] for c in range(3)])
            test_features(points, ftt, centre)

            def tile(b, carry2):
                @pl.when(wanted(n, b))
                def _():
                    @pl.when(flags[b] > 0)
                    def _():
                        fast_tile(ftt, tf, sf, (buf0, buf1), ops, b, flags[b])

                    @pl.when(flags[b] == 0)
                    def _():
                        direct_tile(stage, raw, points, ops, b)

                    apply_operators(ops, xs, wh, wl, acc, TPB * accset(n) + b)

                return carry2

            lax.fori_loop(0, TPB, tile, 0)

        return carry

    tf[...] = jnp.zeros_like(tf)
    ftt[...] = jnp.zeros_like(ftt)
    fts[...] = jnp.zeros_like(fts)
    lax.fori_loop(0, steps, source, 0)


def fill(scratch, pan, cur, row, slot):
    stage, xs = scratch[0], scratch[9]
    lanes = pl.ds(pl.multiple_of(slot * BLK, BLK), BLK)
    stage[...] = pan[0:GROWS, lanes]
    for g in range(4):
        value = cur[row + g * NRHS : row + (g + 1) * NRHS, lanes]
        high = value.astype(BF16)
        xs[0:BLK, g * BLK : (g + 1) * BLK] = high
        xs[BLK : 2 * BLK, g * BLK : (g + 1) * BLK] = (value - high.astype(F32)).astype(BF16)


def fill_tests(xt, which, blocks):
    for c in range(7):
        for b in range(TPB):
            xt[which, c, 2 * b : 2 * b + 2, :] = blocks(b, 2 * c)


def own_tests(test):
    return lambda b, row: test[row : row + 2, b * BLK : (b + 1) * BLK]


def clear(acc, count):
    for b in range(count):
        acc[b] = jnp.zeros((BLK, 4 * BLK), F32)


def write_out(out, acc, blocks):
    for col, b in enumerate(blocks):
        for g in range(4):
            out[g * NRHS : (g + 1) * NRHS, col * BLK : (col + 1) * BLK] = acc[b, :, g * BLK : (g + 1) * BLK]


FIRST = 5


def first_kernel(mask, test, panels, currents, out, done, *scratch):
    scratch = scratch[:-1]
    even = is_even()
    full = load_of(mask) == FULL
    fill_tests(scratch[1], 0, own_tests(test))
    clear(scratch[12], TPB)

    def plan(i, used):
        n, b = lax.div(i, TPB), lax.rem(i, TPB)
        u, v = mirrored(even, n), mirrored(even, b)
        dense = (u > 0) & (v < 2)
        wanted = (full & dense) | (jnp.logical_not(full) & (mask[b, n - b + REACH] > 0))
        now = wanted & (used < FIRST)
        done[n, b] = now.astype(jnp.int32)
        return used + now.astype(jnp.int32)

    lax.fori_loop(0, TPB * TPB, plan, jnp.int32(0))
    engine(scratch, TPB, lambda n, b: done[n, b] > 0, lambda n: fill(scratch, panels, currents, 0, n), lambda n: 0)
    write_out(out, scratch[12], range(TPB))


QUOTA = 7
HELP_STEPS = 7
OWN_STEPS = 8


def own_place(even, n):
    return jnp.where(n < 4, n, jnp.where(n == 4, jnp.where(even, -1, 4), jnp.where(even, n - 1, n - 8)))


def load_own(scratch, panels, currents, outer, mate, n):
    @pl.when(n < 4)
    def _():
        fill(scratch, panels, currents, 0, n)

    @pl.when(n == 4)
    def _():
        fill(scratch, outer, outer, CROW, 0)

    @pl.when(n > 4)
    def _():
        fill(scratch, mate, mate, CROW, n - 5)


def second_kernel(
    mask, done, test, panels, currents, outer, far, mate, load_far, out_near, out_far, out_own, todo, *scratch
):
    plan, scratch = scratch[-1], scratch[:-1]
    even = is_even()
    odd = jnp.logical_not(even)
    own_load, mate_load = load_of(mask), number(mate, XROW)
    near_load, far_load = number(outer, XROW + 64), number(far, XROW + 32)
    share_near, _ = shares(own_load, mate_load)
    _, share_far = shares(mate_load, own_load)
    give_near, give_far = shares(near_load, number(load_far, 0))
    full = own_load == FULL
    xt, acc = scratch[1], scratch[12]
    fill_tests(xt, 0, lambda b, row: outer[XROW + 16 * b + row : XROW + 16 * b + row + 2, :])
    fill_tests(
        xt,
        1,
        lambda b, row: far[
            XROW + 16 * (b // 3) + row : XROW + 16 * (b // 3) + row + 2, (b % 3) * BLK : (b % 3 + 1) * BLK
        ],
    )
    fill_tests(xt, 2, own_tests(test))
    clear(acc, 3 * TPB)

    def plan_help(i, used):
        n, b = lax.div(i, TPB), lax.rem(i, TPB)
        v_near, v_far = mirrored(odd, b), mirrored(even, b)
        u_near, u_far = jnp.where(n == 3, 0, -1 - n), jnp.where(even, n - 3, 7 - n)
        of_near = (n < 4) & (v_near - u_near <= REACH) & is_near(u_near, v_near, share_near)
        of_far = (n >= 4) & is_far(u_far, v_far, share_far)
        wanted = ((near_load == FULL) & of_near) | ((far_load == FULL) & of_far)
        plan[i] = wanted.astype(jnp.int32)
        return used + wanted.astype(jnp.int32)

    def plan_own(i, used):
        n, b = lax.div(i, TPB), lax.rem(i, TPB)
        rel = own_place(even, n)
        column = rel - b + REACH
        inside = (column >= 0) & (column < SPAN)
        sparse = inside & (mask[b, jnp.clip(column, 0, SPAN - 1)] > 0)
        u, v = mirrored(even, rel), mirrored(even, b)
        dense = inside & jnp.logical_not(is_near(u, v, give_near) | is_far(u, v, give_far))
        earlier = (n < TPB) & (done[jnp.minimum(n, TPB - 1), b] > 0)
        wanted = ((full & dense) | (jnp.logical_not(full) & sparse)) & jnp.logical_not(earlier)
        now = wanted & (used < QUOTA)
        plan[HELP_STEPS * TPB + i] = now.astype(jnp.int32)
        todo[n, b] = (wanted & jnp.logical_not(now)).astype(jnp.int32)
        return used + now.astype(jnp.int32)

    used = lax.fori_loop(0, HELP_STEPS * TPB, plan_help, jnp.int32(0))
    lax.fori_loop(0, OWN_STEPS * TPB, plan_own, used)

    def load_source(n):
        @pl.when(n < 3)
        def _():
            fill(scratch, panels, currents, 0, mirrored(even, n))

        @pl.when(n == 3)
        def _():
            fill(scratch, outer, outer, CROW, 0)

        @pl.when((n > 3) & (n < HELP_STEPS))
        def _():
            fill(scratch, far, far, CROW, n - 4)

        @pl.when(n >= HELP_STEPS)
        def _():
            load_own(scratch, panels, currents, outer, mate, n - HELP_STEPS)

    engine(
        scratch,
        HELP_STEPS + OWN_STEPS,
        lambda n, b: plan[n * TPB + b] > 0,
        load_source,
        lambda n: jnp.where(n < 4, 0, jnp.where(n < HELP_STEPS, 1, 2)),
    )
    shift = jnp.where(even, 2, 0)
    write_out(out_near, acc, [b + shift for b in range(2)])
    write_out(out_far, acc, [TPB + b + shift for b in range(2)])
    write_out(out_own, acc, range(2 * TPB, 3 * TPB))


def rest_kernel(todo, test, panels, currents, outer, mate, after, out, *scratch):
    acc = scratch[12]
    fill_tests(scratch[1], 0, own_tests(test))
    clear(acc, TPB)
    engine(
        scratch,
        OWN_STEPS,
        lambda n, b: todo[n, b] > 0,
        lambda n: load_own(scratch, panels, currents, outer, mate, n),
        lambda n: 0,
    )
    write_out(out, acc, range(TPB))


def scratch_for(sets):
    return [
        pltpu.VMEM((GROWS, BLK), F32),
        pltpu.VMEM((sets, 7, 8, BLK), F32),
        pltpu.VMEM(((NTERM + 16) * 16, BLK), F32),
        pltpu.VMEM((TROWS * 8, BLK), F32),
        pltpu.VMEM((KDIM, NOUT * 256), BF16),
        pltpu.VMEM((NCH * MROWS, KDIM), BF16),
        pltpu.VMEM((MROWS + 8, NOUT * 256), F32),
        pltpu.VMEM((MROWS + 8, NOUT * 256), F32),
        pltpu.VMEM((6, BLK, BLK), F32),
        pltpu.VMEM((2 * BLK, 4 * BLK), BF16),
        pltpu.VMEM((4 * BLK, 4 * BLK), BF16),
        pltpu.VMEM((4 * BLK, 4 * BLK), BF16),
        pltpu.VMEM((sets * TPB, BLK, 4 * BLK), F32),
        pltpu.VMEM((8 * 16, BLK), F32),
        pltpu.SMEM((TPB,), jnp.int32),
    ]


def call(kernel, outs, operands, sets=0, tables=1, unread=0, tiles=1, table=(), copies=0):
    vmem = pl.BlockSpec(memory_space=pltpu.VMEM)
    smem = pl.BlockSpec(memory_space=pltpu.SMEM)
    anywhere = pl.BlockSpec(memory_space=pl.ANY)
    plain = len(operands) - tables - unread
    shapes = [jax.ShapeDtypeStruct(s, F32) for s in outs]
    specs = [vmem] * len(outs)
    scratch = scratch_for(sets) if sets else []
    if copies:
        specs = [anywhere] * 3 + [vmem]
        scratch += [
            pltpu.VMEM((GROWS, TPB * BLK), F32),
            pltpu.VMEM((14, TPB * BLK), F32),
            pltpu.VMEM((CROW, TPB * BLK), F32),
            pltpu.VMEM((72, BLK), F32),
            pltpu.VMEM((40, 3 * BLK), F32),
            pltpu.VMEM((8, 3 * BLK), F32),
            pltpu.SemaphoreType.DMA((copies,)),
        ]
    if table:
        shapes.append(jax.ShapeDtypeStruct(table, jnp.int32))
        specs.append(smem)
        scratch.append(pltpu.SMEM(((HELP_STEPS + OWN_STEPS) * TPB,), jnp.int32))
    return pl.pallas_call(
        kernel,
        out_shape=shapes,
        in_specs=[smem] * tables + [vmem] * plain + [anywhere] * unread,
        out_specs=specs,
        scratch_shapes=scratch,
        compiler_params=pltpu.CompilerParams(vmem_limit_bytes=(60 if copies else 20) * 1024 * 1024),
        cost_estimate=pl.CostEstimate(flops=tiles * 5 * 10**9, bytes_accessed=4 * 10**6, transcendentals=0),
    )(*operands)


def body(panels, test_points, currents, near_mask):
    count = lax.axis_size("cluster") * lax.axis_size("narrow")
    axes = ("cluster", "narrow")
    swap = [(i, i ^ 1) for i in range(count)]
    across = [(i, (i - 1) % count if i % 2 == 0 else (i + 1) % count) for i in range(count)]
    away = [(i, (i - 2) % count if i % 2 == 0 else (i + 2) % count) for i in range(count)]
    back = [(target, source) for source, target in away]
    width = TPB * BLK
    wide = 4 * NRHS
    mate, outer, far, load = call(
        pack_kernel,
        [(MATE_ROWS, 3 * BLK), (OUTER_ROWS, BLK), (FAR_ROWS, 3 * BLK), (8, BLK)],
        [near_mask, panels, test_points, currents],
        unread=3,
        copies=PACK_COPIES,
    )
    load_far = lax.ppermute(load, axes, back)
    outer = lax.ppermute(outer, axes, across)
    far = lax.ppermute(far, axes, away)
    mate = lax.ppermute(mate, axes, swap)
    part, done = call(
        first_kernel, [(wide, width)], [near_mask, test_points, panels, currents], 1, tiles=5, table=(TPB, TPB)
    )
    to_near, to_far, more, todo = call(
        second_kernel,
        [(wide, 2 * BLK), (wide, 2 * BLK), (wide, width)],
        [near_mask, done, test_points, panels, currents, outer, far, mate, load_far],
        3,
        tables=2,
        tiles=7,
        table=(OWN_STEPS, TPB),
    )
    from_near = lax.ppermute(to_near, axes, across)
    from_far = lax.ppermute(to_far, axes, back)
    (rest,) = call(
        rest_kernel,
        [(wide, width)],
        [todo, test_points, panels, currents, outer, mate, to_near],
        1,
        unread=1,
        tiles=8,
    )
    even = lax.axis_index("narrow") == 0
    helped = jnp.concatenate([jnp.where(even, from_near, from_far), jnp.where(even, from_far, from_near)], 1)
    return part + more + rest + helped


def solution(mesh):
    return jax.shard_map(
        body,
        mesh=mesh,
        in_specs=(
            P(None, ("cluster", "narrow")),
            P(None, ("cluster", "narrow")),
            P(None, ("cluster", "narrow")),
            P(("cluster", "narrow"), None),
        ),
        out_specs=P(None, ("cluster", "narrow")),
        check_vma=False,
    )
```

```python
import functools
import itertools
import math

import jax
import jax.numpy as jnp
from jax import lax
from jax.experimental import pallas as pl
from jax.experimental.pallas import tpu as pltpu
from jax.sharding import PartitionSpec as P

F32 = jnp.float32
BF16 = jnp.bfloat16
BLK = 128
QP = 14
REACH = 3
SPAN = 7
TPB = 4
GROWS = 98
NRHS = 128
SOFTEN = 0.04

Z_MAX = 14.0
DEGREE = 4
COS_HALF = (2.828426289053651, -0.35355064760758376, 0.007364148070439611, -6.107114702262049e-05, 2.4846120790492805e-07)
SIN_HALF = (1.4142135239177973, -0.05892543897495882, 0.0007364984722676873, -4.370137027858996e-06, 1.4053654408325383e-08)

TERMS = []
for _total in range(DEGREE + 1):
    for _j in range(_total + 1):
        _l = _total - _j
        for _a in itertools.product(range(_l + 1), repeat=3):
            if sum(_a) == _l:
                TERMS.append((_j, _a))
NTERM = 72
assert len(TERMS) <= NTERM
ONE = TERMS.index((0, (0, 0, 0)))
LIN = [TERMS.index((0, tuple(int(c == k) for c in range(3)))) for k in range(3)]
SQR = TERMS.index((1, (0, 0, 0)))
KDIM = 256
NOUT = 7
JC = 16
NCH = BLK // JC
MROWS = JC * QP


def powers_of(vec):
    one = None
    table = {(0, 0, 0): one}
    for total in range(1, DEGREE + 1):
        for a in itertools.product(range(total + 1), repeat=3):
            if sum(a) != total:
                continue
            axis = next(c for c in range(3) if a[c] > 0)
            prev = tuple(a[c] - (c == axis) for c in range(3))
            table[a] = vec[axis] if table[prev] is None else table[prev] * vec[axis]
    return table


def split2(value):
    high = value.astype(BF16).astype(F32)
    return high, value - high


def source_features(stage, fts, sf, centre, y):
    mono = powers_of(y)
    square = y[0] * y[0] + y[1] * y[1] + y[2] * y[2]
    sq = [None, square, square * square]
    sq.append(sq[2] * square)
    sq.append(sq[2] * sq[2])
    ones = jnp.ones_like(square)

    def put(row, value):
        fts[row * 16 : row * 16 + QP, :] = value

    for k, (j, a) in enumerate(TERMS):
        const = (-2.0) ** sum(a) / (math.prod(math.factorial(v) for v in a) * math.factorial(j))
        value = mono[a]
        if sq[j] is not None:
            value = sq[j] if value is None else value * sq[j]
        if value is None:
            value = ones
        put(k, value * const if const != 1.0 else value)
    base = NTERM
    s = [stage[(3 + c) * QP : (4 + c) * QP, :] for c in range(3)]
    d = stage[6 * QP : 7 * QP, :]
    for c in range(3):
        put(base + c, s[c])
    put(base + 3, d)
    for c in range(3):
        c1, c2 = (c + 1) % 3, (c + 2) % 3
        put(base + 4 + c, y[c1] * s[c2] - y[c2] * s[c1])
    extra = base + 8
    for half in range(2):
        for c in range(3):
            put(extra + 4 * half + c, y[c] * -2.0)
        put(extra + 4 * half + 3, square)
    rows = lax.broadcasted_iota(jnp.int32, (8, BLK), 0)
    for q in range(QP):
        main = fts[pl.ds(q, NTERM, stride=16), :]
        bil = fts[pl.ds(base * 16 + q, 8, stride=16), :]
        ext = fts[pl.ds(extra * 16 + q, 8, stride=16), :]
        mh, ml = split2(main)
        bh, bl = split2(bil)
        eh, rest = split2(ext)
        em, el = split2(rest)
        zrow = jnp.where(rows < 4, em, eh)
        zrow2 = jnp.where(rows < 4, el, jnp.where(rows == 4, 1.0, 0.0))
        full = jnp.concatenate([mh, mh, ml, bh, bh, bl, zrow, zrow2], 0)
        turned = full.astype(BF16).T
        for ch in range(NCH):
            sf[ch * MROWS + q * JC : ch * MROWS + (q + 1) * JC, :] = turned[ch * JC : (ch + 1) * JC, :]


def horner(coefs, m, w):
    der = [coefs[k] * math.factorial(k) / math.factorial(k - m) for k in range(m, len(coefs))]
    value = None
    for c in reversed(der):
        value = c if value is None else value * w + c
    return value


OFF_C, OFF_S, OFF_Z = 0, NTERM, 2 * NTERM
OFF_B = 3 * NTERM
OFF_E = OFF_B + 32
TROWS = OFF_E + 16


def test_features(xt, ftt, centre):
    x = [xt[c] - centre[c] for c in range(3)]
    t = [xt[3 + c] for c in range(3)]
    e = xt[6]
    w = x[0] * x[0] + x[1] * x[1] + x[2] * x[2] + SOFTEN
    mono = powers_of(x)

    def put(row, value):
        ftt[row * 8 : row * 8 + 8, :] = value

    for off, coefs in ((OFF_C, COS_HALF), (OFF_S, SIN_HALF)):
        der = [horner(coefs, m, w) for m in range(DEGREE + 1)]
        for k, (j, a) in enumerate(TERMS):
            level = der[j + sum(a)]
            value = level if mono[a] is None else mono[a] * level
            put(off + k, jnp.broadcast_to(value, w.shape))
    put(OFF_Z + ONE, w)
    put(OFF_Z + SQR, jnp.ones_like(w))
    for c in range(3):
        put(OFF_Z + LIN[c], x[c])
    charge = e * -0.25
    for c in range(3):
        put(OFF_B + c, t[c])
        put(OFF_B + 8 + c, t[c] * -2.0)
        put(OFF_B + 16 + c, t[c] * 1.5)
        c1, c2 = (c + 1) % 3, (c + 2) % 3
        put(OFF_B + 24 + c, (t[c1] * x[c2] - t[c2] * x[c1]) * -0.25)
        put(OFF_B + 28 + c, t[c] * 0.25)
    put(OFF_B + 3, charge)
    put(OFF_B + 11, charge)
    for half in range(2):
        for c in range(3):
            put(OFF_E + 4 * half + c, x[c])
        put(OFF_E + 4 * half + 3, jnp.ones_like(w))
    for c in range(4):
        put(OFF_E + 8 + c, x[c] if c < 3 else jnp.ones_like(w))
    put(OFF_E + 12, w)


def test_matrix(ftt, tf, b):
    rows = lax.broadcasted_iota(jnp.int32, (8, BLK), 0)
    zero8 = jnp.zeros((8, BLK), F32)
    for a in range(2):
        ba = 2 * b + a

        def take(off, n):
            return ftt[pl.ds(off * 8 + ba, n, stride=8), :]

        for out, off in ((0, OFF_Z), (1, OFF_C), (2, OFF_S)):
            high, low = split2(take(off, NTERM))
            lanes = slice(out * 256 + a * BLK, out * 256 + (a + 1) * BLK)
            tf[0:224, lanes] = jnp.concatenate([high, low, high, zero8], 0).astype(BF16)
        eh, rest = split2(take(OFF_E, 8))
        em, el = split2(rest)
        fh, rest2 = split2(take(OFF_E + 8, 8))
        fm, fl = split2(rest2)
        first = jnp.where(rows < 4, em, el)
        second = jnp.where(rows < 4, fh, jnp.where(rows == 4, fl, 0.0))
        tf[240:256, a * BLK : (a + 1) * BLK] = jnp.concatenate([first, second], 0).astype(BF16)
        for m in range(4):
            high, low = split2(take(OFF_B + 8 * m, 8))
            out = 3 + m
            lanes = slice(out * 256 + a * BLK, out * 256 + (a + 1) * BLK)
            tf[208:240, lanes] = jnp.concatenate([zero8, high, low, high], 0).astype(BF16)


EXP_RATE = -3.0 / math.log(2.0)


def pair_terms(z, cos_h, sin_h, k1, k2, k6, kk):
    inv = lax.rsqrt(z)
    dist = z * inv
    s0 = sin_h * dist
    c = 4.0 - s0 * s0
    s = s0 * cos_h
    c2 = c * c - 8.0
    s2 = c * s
    decay = jnp.exp2(dist * EXP_RATE)
    p = decay * c
    q = decay * s
    half = inv * 0.5
    c2r = c2 * half
    s2r = s2 * half
    pr = p * inv
    qr = q * inv
    weight = kk * (inv * inv)
    l1r = k1 * c2r
    l1i = k1 * s2r
    l2r = k2 * pr - k6 * qr
    l2i = k2 * qr + k6 * pr
    inv3 = inv + 3.0
    kr = weight * ((c2r + s2) + (p * inv3 + q))
    ki = weight * ((s2r - c2) + (q * inv3 - p))
    return l1r, l1i, l2r, l2i, kr, ki


AHEAD = 6


def fast_tile(ftt, tf, sf, bufs, ops, b, flag):
    test_matrix(ftt, tf, b)
    spare = pl.multiple_of(MROWS - 8 + 8 * flag, 8)

    def piece(chunk, buf, o):
        rows = pl.ds(pl.multiple_of(chunk * MROWS, 16), MROWS)
        lanes = slice(o * 256, (o + 1) * 256)
        buf[0:MROWS, lanes] = jnp.dot(sf[rows, :], tf[:, lanes], preferred_element_type=F32)

    def phase(chunk, buf, next_chunk, next_buf):
        work = [(g, q, a) for g in range(JC // 8) for q in range(QP) for a in range(2)]
        per = -(-len(work) // NOUT)
        acc, history = None, []
        for o in range(NOUT):
            if next_buf is not None:
                piece(next_chunk, next_buf, o)
            for g, q, a in work[o * per : (o + 1) * per]:
                if q == 0 and a == 0:
                    acc = None
                row = q * JC + g * 8
                if len(history) >= AHEAD and len(history) % 2 == 0:
                    buf[pl.ds(spare, 8), 0:BLK] = history[-AHEAD]
                vals = [buf[row : row + 8, k * 256 + a * BLK : k * 256 + (a + 1) * BLK] for k in range(NOUT)]
                terms = pair_terms(*vals)
                acc = list(terms) if acc is None else [u + v for u, v in zip(acc, terms)]
                history.append(acc[5])
                if q == QP - 1 and a == 1:
                    start = pl.multiple_of(chunk * JC + g * 8, 8)
                    for m in range(6):
                        ops[m, pl.ds(start, 8), :] = acc[m]

    for o in range(NOUT):
        piece(0, bufs[0], o)

    def step(n, carry):
        phase(2 * n, bufs[0], 2 * n + 1, bufs[1])
        phase(2 * n + 1, bufs[1], 2 * n + 2, bufs[0])
        return carry

    lax.fori_loop(0, NCH // 2 - 1, step, 0)
    phase(NCH - 2, bufs[0], NCH - 1, bufs[1])
    phase(NCH - 1, bufs[1], None, None)


def direct_tile(stage, raw, xt, ops, b):
    for c in range(7):
        raw[c * 16 : c * 16 + QP, :] = stage[c * QP : (c + 1) * QP, :]
    raw[7 * 16 : 8 * 16, :] = jnp.zeros((16, BLK), F32)
    for m in range(6):
        ops[m] = jnp.zeros((BLK, BLK), F32)

    def point(q, carry):
        rows8 = raw[pl.ds(q, 8, stride=16), :]
        turned = jnp.concatenate([rows8, jnp.zeros((BLK - 8, BLK), F32)], 0).T
        src = [turned[:, c : c + 1] for c in range(7)]

        def centroid(a, carry2):
            tst = [xt[c, pl.ds(2 * b + a, 1), :] for c in range(7)]
            dl = [tst[c] - src[c] for c in range(3)]
            dist = jnp.sqrt(dl[0] * dl[0] + dl[1] * dl[1] + dl[2] * dl[2] + SOFTEN)
            dotted = tst[3] * src[3] + tst[4] * src[4] + tst[5] * src[5]
            charge = tst[6] * src[6]
            crossed = (
                dl[0] * (src[4] * tst[5] - src[5] * tst[4])
                + dl[1] * (src[5] * tst[3] - src[3] * tst[5])
                + dl[2] * (src[3] * tst[4] - src[4] * tst[3])
            )
            scaled = crossed / (dist * dist)
            kr = ki = None
            for m, (wr, wi) in enumerate(((2.0, 0.0), (1.0, 3.0))):
                decay = jnp.exp(-wi * dist) / dist
                gr = decay * jnp.cos(wr * dist)
                gi = decay * jnp.sin(wr * dist)
                cr = (wr * wr - wi * wi) * dotted - charge
                ci = 2.0 * wr * wi * dotted
                ops[2 * m] += cr * gr - ci * gi
                ops[2 * m + 1] += cr * gi + ci * gr
                fr = -wi * dist - 1.0
                fi = wr * dist
                ops[4] += scaled * (fr * gr - fi * gi)
                ops[5] += scaled * (fr * gi + fi * gr)
            return carry2

        return lax.fori_loop(0, 2, centroid, carry)

    lax.fori_loop(0, QP, point, 0)


def apply_operators(ops, xs, wh, wl, acc, b):
    def put(ref, value, places):
        neg = -value
        for row, col, sign in places:
            ref[row * BLK : (row + 1) * BLK, col * BLK : (col + 1) * BLK] = value if sign > 0 else neg

    def both(value, places):
        high = value.astype(BF16)
        low = (value - high.astype(F32)).astype(BF16)
        put(wh, high, places)
        put(wl, low, places)

    l1r, l1i, l2r, l2i = (ops[m] for m in range(4))
    both(l1r + l2r, ((0, 0, 1), (1, 1, 1)))
    both(l1i + l2i, ((0, 1, 1), (1, 0, -1)))
    both(l1r + 0.5 * l2r, ((2, 2, 1), (3, 3, 1)))
    both(l1i + 0.5 * l2i, ((2, 3, 1), (3, 2, -1)))
    both(ops[4], ((0, 2, 1), (1, 3, 1), (2, 0, -1), (3, 1, -1)))
    both(ops[5], ((0, 3, 1), (1, 2, -1), (2, 1, -1), (3, 0, 1)))
    first = jnp.dot(xs[...], wh[...], preferred_element_type=F32)
    second = jnp.dot(xs[0:BLK, :], wl[...], preferred_element_type=F32)
    acc[b] += first[0:BLK] + first[BLK:] + second


CROW = 104
XROW = CROW + 4 * NRHS
OUTER_ROWS = XROW + 64 + 8
FAR_ROWS = XROW + 32 + 8
MATE_ROWS = XROW + 8
FULL = TPB * SPAN


def is_even():
    return lax.axis_index("narrow") == 0


def mirrored(even, block):
    return jnp.where(even, block, TPB - 1 - block)


def load_of(mask):
    total = mask[0, 0]
    for b in range(TPB):
        for c in range(SPAN):
            if b or c:
                total = total + mask[b, c]
    return total


def number(ref, row):
    return jnp.max(ref[row : row + 8, 0:BLK]).astype(jnp.int32)


def shares(load_near, load_far):
    goal = lax.div(FULL + load_near + load_far + 1, 3)
    near = jnp.clip(goal - load_near, 3, 7)
    far = jnp.clip(lax.div(FULL - near + load_far + 1, 2) - load_far, 0, 6)
    near = jnp.clip(lax.div(FULL - far + load_near + 1, 2) - load_near, 3, 7)
    return near, far


def is_near(u, v, share):
    option = jnp.where(u == -1, v, jnp.where(u == 0, 2 + v, FULL))
    return (u < -1) | ((v < 2) & (option < share - 3))


def is_far(u, v, share):
    return (v >= 2) & (jnp.where((u >= 1) & (u <= 3), 2 * (3 - u) + v - 2, FULL) < share)


PACK_COPIES = 5


def pack_kernel(mask, panels_at, test_at, currents, mate, outer, far, load, panels, test, sems):
    even = is_even()
    places = (
        (outer, 1, jnp.where(even, 0, 3 * BLK)),
        (far, 3, jnp.where(even, BLK, 0)),
        (mate, 3, jnp.where(even, BLK, 0)),
    )
    lanes = [pl.ds(pl.multiple_of(begin, BLK), count * BLK) for _, count, begin in places]
    copies = [pltpu.make_async_copy(panels_at, panels, sems.at[0]), pltpu.make_async_copy(test_at, test, sems.at[1])]
    for k in range(3):
        copies.append(pltpu.make_async_copy(currents.at[:, lanes[k]], places[k][0].at[CROW:XROW, :], sems.at[2 + k]))
    for each in copies:
        each.start()
    value = load_of(mask).astype(F32)
    outer[XROW + 64 : XROW + 72, :] = jnp.full((8, BLK), value, F32)
    far[XROW + 32 : XROW + 40, :] = jnp.full((8, 3 * BLK), value, F32)
    mate[XROW : XROW + 8, :] = jnp.full((8, 3 * BLK), value, F32)
    load[...] = jnp.full((8, BLK), value, F32)
    copies[0].wait()
    copies[1].wait()
    for k in range(3):
        places[k][0][0:GROWS, :] = panels[:, lanes[k]]
    for b in range(TPB):
        points = test[:, b * BLK : (b + 1) * BLK]
        outer[XROW + 16 * b : XROW + 16 * b + 14, :] = points
        row = XROW + 16 * (b // 3)
        far[row : row + 14, (b % 3) * BLK : (b % 3 + 1) * BLK] = points
    for each in copies[2:]:
        each.wait()


def engine(scratch, steps, wanted, load_source, accset):
    stage, xt, fts, ftt, tf, sf, buf0, buf1, ops, xs, wh, wl, acc, raw, flags = scratch

    def source(n, carry):
        any_wanted = wanted(n, 0)
        for b in range(1, TPB):
            any_wanted = any_wanted | wanted(n, b)

        @pl.when(any_wanted)
        def _():
            load_source(n)
            points = xt.at[accset(n)]
            place = [stage[c * QP : (c + 1) * QP, :] for c in range(3)]
            low = [jnp.min(jnp.min(v, 0, keepdims=True), 1, keepdims=True) for v in place]
            high = [jnp.max(jnp.max(v, 0, keepdims=True), 1, keepdims=True) for v in place]
            centre = [(u + v) * 0.5 for u, v in zip(low, high)]
            bound = jnp.full((8, BLK), SOFTEN, F32)
            for c in range(3):
                far = jnp.maximum(jnp.abs(points[c] - low[c]), jnp.abs(points[c] - high[c]))
                bound = bound + far * far
            for b in range(TPB):
                flags[b] = (jnp.max(bound[2 * b : 2 * b + 2]) <= Z_MAX).astype(jnp.int32)
            source_features(stage, fts, sf, centre, [place[c] - centre[c] for c in range(3)])
            test_features(points, ftt, centre)

            def tile(b, carry2):
                @pl.when(wanted(n, b))
                def _():
                    @pl.when(flags[b] > 0)
                    def _():
                        fast_tile(ftt, tf, sf, (buf0, buf1), ops, b, flags[b])

                    @pl.when(flags[b] == 0)
                    def _():
                        direct_tile(stage, raw, points, ops, b)

                    apply_operators(ops, xs, wh, wl, acc, TPB * accset(n) + b)

                return carry2

            lax.fori_loop(0, TPB, tile, 0)

        return carry

    tf[...] = jnp.zeros_like(tf)
    spare = NTERM - len(TERMS)
    ftt[OFF_Z * 8 :, :] = jnp.zeros(((TROWS - OFF_Z) * 8, BLK), F32)
    for off in (OFF_C, OFF_S):
        ftt[(off + NTERM - spare) * 8 : (off + NTERM) * 8, :] = jnp.zeros((spare * 8, BLK), F32)
    fts[(NTERM - spare) * 16 : NTERM * 16, :] = jnp.zeros((spare * 16, BLK), F32)
    fts[(NTERM + 7) * 16 : (NTERM + 8) * 16, :] = jnp.zeros((16, BLK), F32)
    lax.fori_loop(0, steps, source, 0)


def fill(scratch, pan, cur, row, slot):
    stage, xs = scratch[0], scratch[9]
    lanes = pl.ds(pl.multiple_of(slot * BLK, BLK), BLK)
    stage[...] = pan[0:GROWS, lanes]
    for g in range(4):
        value = cur[row + g * NRHS : row + (g + 1) * NRHS, lanes]
        high = value.astype(BF16)
        xs[0:BLK, g * BLK : (g + 1) * BLK] = high
        xs[BLK : 2 * BLK, g * BLK : (g + 1) * BLK] = (value - high.astype(F32)).astype(BF16)


def fill_tests(xt, which, blocks):
    for c in range(7):
        for b in range(TPB):
            xt[which, c, 2 * b : 2 * b + 2, :] = blocks(b, 2 * c)


def own_tests(test):
    return lambda b, row: test[row : row + 2, b * BLK : (b + 1) * BLK]


def clear(acc, count):
    for b in range(count):
        acc[b] = jnp.zeros((BLK, 4 * BLK), F32)


def write_out(out, acc, blocks):
    for col, b in enumerate(blocks):
        for g in range(4):
            out[g * NRHS : (g + 1) * NRHS, col * BLK : (col + 1) * BLK] = acc[b, :, g * BLK : (g + 1) * BLK]


FIRST = 5


def first_kernel(mask, test, panels, currents, out, done, *scratch):
    scratch = scratch[:-1]
    even = is_even()
    full = load_of(mask) == FULL
    fill_tests(scratch[1], 0, own_tests(test))
    clear(scratch[12], TPB)

    def plan(i, used):
        n, b = lax.div(i, TPB), lax.rem(i, TPB)
        u, v = mirrored(even, n), mirrored(even, b)
        dense = (u > 0) & (v < 2)
        wanted = (full & dense) | (jnp.logical_not(full) & (mask[b, n - b + REACH] > 0))
        now = wanted & (used < FIRST)
        done[n, b] = now.astype(jnp.int32)
        return used + now.astype(jnp.int32)

    lax.fori_loop(0, TPB * TPB, plan, jnp.int32(0))
    engine(scratch, TPB, lambda n, b: done[n, b] > 0, lambda n: fill(scratch, panels, currents, 0, n), lambda n: 0)
    write_out(out, scratch[12], range(TPB))


QUOTA = 7
HELP_STEPS = 7
OWN_STEPS = 8


def own_place(even, n):
    return jnp.where(n < 4, n, jnp.where(n == 4, jnp.where(even, -1, 4), jnp.where(even, n - 1, n - 8)))


def load_own(scratch, panels, currents, outer, mate, n):
    @pl.when(n < 4)
    def _():
        fill(scratch, panels, currents, 0, n)

    @pl.when(n == 4)
    def _():
        fill(scratch, outer, outer, CROW, 0)

    @pl.when(n > 4)
    def _():
        fill(scratch, mate, mate, CROW, n - 5)


def second_kernel(
    mask, done, test, panels, currents, outer, far, mate, load_far, out_near, out_far, out_own, todo, *scratch
):
    plan, scratch = scratch[-1], scratch[:-1]
    even = is_even()
    odd = jnp.logical_not(even)
    own_load, mate_load = load_of(mask), number(mate, XROW)
    near_load, far_load = number(outer, XROW + 64), number(far, XROW + 32)
    share_near, _ = shares(own_load, mate_load)
    _, share_far = shares(mate_load, own_load)
    give_near, give_far = shares(near_load, number(load_far, 0))
    full = own_load == FULL
    xt, acc = scratch[1], scratch[12]
    fill_tests(xt, 0, lambda b, row: outer[XROW + 16 * b + row : XROW + 16 * b + row + 2, :])
    fill_tests(
        xt,
        1,
        lambda b, row: far[
            XROW + 16 * (b // 3) + row : XROW + 16 * (b // 3) + row + 2, (b % 3) * BLK : (b % 3 + 1) * BLK
        ],
    )
    fill_tests(xt, 2, own_tests(test))
    clear(acc, 3 * TPB)

    def plan_help(i, used):
        n, b = lax.div(i, TPB), lax.rem(i, TPB)
        v_near, v_far = mirrored(odd, b), mirrored(even, b)
        u_near, u_far = jnp.where(n == 3, 0, -1 - n), jnp.where(even, n - 3, 7 - n)
        of_near = (n < 4) & (v_near - u_near <= REACH) & is_near(u_near, v_near, share_near)
        of_far = (n >= 4) & is_far(u_far, v_far, share_far)
        wanted = ((near_load == FULL) & of_near) | ((far_load == FULL) & of_far)
        plan[i] = wanted.astype(jnp.int32)
        return used + wanted.astype(jnp.int32)

    def plan_own(i, used):
        n, b = lax.div(i, TPB), lax.rem(i, TPB)
        rel = own_place(even, n)
        column = rel - b + REACH
        inside = (column >= 0) & (column < SPAN)
        sparse = inside & (mask[b, jnp.clip(column, 0, SPAN - 1)] > 0)
        u, v = mirrored(even, rel), mirrored(even, b)
        dense = inside & jnp.logical_not(is_near(u, v, give_near) | is_far(u, v, give_far))
        earlier = (n < TPB) & (done[jnp.minimum(n, TPB - 1), b] > 0)
        wanted = ((full & dense) | (jnp.logical_not(full) & sparse)) & jnp.logical_not(earlier)
        now = wanted & (used < QUOTA)
        plan[HELP_STEPS * TPB + i] = now.astype(jnp.int32)
        todo[n, b] = (wanted & jnp.logical_not(now)).astype(jnp.int32)
        return used + now.astype(jnp.int32)

    used = lax.fori_loop(0, HELP_STEPS * TPB, plan_help, jnp.int32(0))
    lax.fori_loop(0, OWN_STEPS * TPB, plan_own, used)

    def load_source(n):
        @pl.when(n < 3)
        def _():
            fill(scratch, panels, currents, 0, mirrored(even, n))

        @pl.when(n == 3)
        def _():
            fill(scratch, outer, outer, CROW, 0)

        @pl.when((n > 3) & (n < HELP_STEPS))
        def _():
            fill(scratch, far, far, CROW, n - 4)

        @pl.when(n >= HELP_STEPS)
        def _():
            load_own(scratch, panels, currents, outer, mate, n - HELP_STEPS)

    engine(
        scratch,
        HELP_STEPS + OWN_STEPS,
        lambda n, b: plan[n * TPB + b] > 0,
        load_source,
        lambda n: jnp.where(n < 4, 0, jnp.where(n < HELP_STEPS, 1, 2)),
    )
    shift = jnp.where(even, 2, 0)
    write_out(out_near, acc, [b + shift for b in range(2)])
    write_out(out_far, acc, [TPB + b + shift for b in range(2)])
    write_out(out_own, acc, range(2 * TPB, 3 * TPB))


def rest_kernel(todo, test, panels, currents, outer, mate, after, out, *scratch):
    acc = scratch[12]
    fill_tests(scratch[1], 0, own_tests(test))
    clear(acc, TPB)
    engine(
        scratch,
        OWN_STEPS,
        lambda n, b: todo[n, b] > 0,
        lambda n: load_own(scratch, panels, currents, outer, mate, n),
        lambda n: 0,
    )
    write_out(out, acc, range(TPB))


def scratch_for(sets):
    return [
        pltpu.VMEM((GROWS, BLK), F32),
        pltpu.VMEM((sets, 7, 8, BLK), F32),
        pltpu.VMEM(((NTERM + 16) * 16, BLK), F32),
        pltpu.VMEM((TROWS * 8, BLK), F32),
        pltpu.VMEM((KDIM, NOUT * 256), BF16),
        pltpu.VMEM((NCH * MROWS, KDIM), BF16),
        pltpu.VMEM((MROWS + 8, NOUT * 256), F32),
        pltpu.VMEM((MROWS + 8, NOUT * 256), F32),
        pltpu.VMEM((6, BLK, BLK), F32),
        pltpu.VMEM((2 * BLK, 4 * BLK), BF16),
        pltpu.VMEM((4 * BLK, 4 * BLK), BF16),
        pltpu.VMEM((4 * BLK, 4 * BLK), BF16),
        pltpu.VMEM((sets * TPB, BLK, 4 * BLK), F32),
        pltpu.VMEM((8 * 16, BLK), F32),
        pltpu.SMEM((TPB,), jnp.int32),
    ]


def call(kernel, outs, operands, sets=0, tables=1, unread=0, tiles=1, table=(), copies=0):
    vmem = pl.BlockSpec(memory_space=pltpu.VMEM)
    smem = pl.BlockSpec(memory_space=pltpu.SMEM)
    anywhere = pl.BlockSpec(memory_space=pl.ANY)
    plain = len(operands) - tables - unread
    shapes = [jax.ShapeDtypeStruct(s, F32) for s in outs]
    specs = [vmem] * len(outs)
    scratch = scratch_for(sets) if sets else []
    if copies:
        scratch += [
            pltpu.VMEM((GROWS, TPB * BLK), F32),
            pltpu.VMEM((14, TPB * BLK), F32),
            pltpu.SemaphoreType.DMA((copies,)),
        ]
    if table:
        shapes.append(jax.ShapeDtypeStruct(table, jnp.int32))
        specs.append(smem)
        scratch.append(pltpu.SMEM(((HELP_STEPS + OWN_STEPS) * TPB,), jnp.int32))
    return pl.pallas_call(
        kernel,
        out_shape=shapes,
        in_specs=[smem] * tables + [vmem] * plain + [anywhere] * unread,
        out_specs=specs,
        scratch_shapes=scratch,
        compiler_params=pltpu.CompilerParams(vmem_limit_bytes=(60 if copies else 20) * 1024 * 1024),
        cost_estimate=pl.CostEstimate(flops=tiles * 5 * 10**9, bytes_accessed=4 * 10**6, transcendentals=0),
    )(*operands)


def body(panels, test_points, currents, near_mask):
    count = lax.axis_size("cluster") * lax.axis_size("narrow")
    axes = ("cluster", "narrow")
    swap = [(i, i ^ 1) for i in range(count)]
    across = [(i, (i - 1) % count if i % 2 == 0 else (i + 1) % count) for i in range(count)]
    away = [(i, (i - 2) % count if i % 2 == 0 else (i + 2) % count) for i in range(count)]
    back = [(target, source) for source, target in away]
    width = TPB * BLK
    wide = 4 * NRHS
    mate, outer, far, load = call(
        pack_kernel,
        [(MATE_ROWS, 3 * BLK), (OUTER_ROWS, BLK), (FAR_ROWS, 3 * BLK), (8, BLK)],
        [near_mask, panels, test_points, currents],
        unread=3,
        copies=PACK_COPIES,
    )
    load_far = lax.ppermute(load, axes, back)
    outer = lax.ppermute(outer, axes, across)
    far = lax.ppermute(far, axes, away)
    mate = lax.ppermute(mate, axes, swap)
    part, done = call(
        first_kernel, [(wide, width)], [near_mask, test_points, panels, currents], 1, tiles=5, table=(TPB, TPB)
    )
    to_near, to_far, more, todo = call(
        second_kernel,
        [(wide, 2 * BLK), (wide, 2 * BLK), (wide, width)],
        [near_mask, done, test_points, panels, currents, outer, far, mate, load_far],
        3,
        tables=2,
        tiles=7,
        table=(OWN_STEPS, TPB),
    )
    from_near = lax.ppermute(to_near, axes, across)
    from_far = lax.ppermute(to_far, axes, back)
    (rest,) = call(
        rest_kernel,
        [(wide, width)],
        [todo, test_points, panels, currents, outer, mate, to_near],
        1,
        unread=1,
        tiles=8,
    )
    even = lax.axis_index("narrow") == 0
    helped = jnp.concatenate([jnp.where(even, from_near, from_far), jnp.where(even, from_far, from_near)], 1)
    return part + more + rest + helped


def solution(mesh):
    return jax.shard_map(
        body,
        mesh=mesh,
        in_specs=(
            P(None, ("cluster", "narrow")),
            P(None, ("cluster", "narrow")),
            P(None, ("cluster", "narrow")),
            P(("cluster", "narrow"), None),
        ),
        out_specs=P(None, ("cluster", "narrow")),
        check_vma=False,
    )
```
